32 devices in a mesh: groups: 2 (over y), seq: 16 (over z, x, core).
Axes of the slice: x: 2, y: 2, z: 4, core: 2. Of those that a mesh axis runs over, the one named last changes fastest.
Arguments:
- queries: bfloat16 [4096, 4096], P(('groups', 'seq')), parts along dimension 0, may hold values from -6 to 6
- keys: bfloat16 [4096, 4096], P(('groups', 'seq')), parts along dimension 0, may hold values from -6 to 6
- values: bfloat16 [4096, 4096], P(('groups', 'seq')), parts along dimension 0, may hold values from -6 to 6
- kept: int32 [64, 4, 8], P('groups'), parts along dimension 0, may hold values from 0 to 15, as said below
- counts: int32 [64, 4], P('groups'), parts along dimension 0, may hold values from 4 to 8
Outputs:
- attended: bfloat16 [4096, 4096], P(('groups', 'seq')), parts along dimension 0
The draws below stay inside these ranges and needn't reach their ends.
There are 2 independent parts, one for each index of `groups`. The reference program is written for one: setup_inputs(seed, part) draws one part's arguments, and reference() takes and returns one part's arrays. A program takes and returns all parts, laid end to end along the dimension named above; each array names one. Nothing has to cross between parts.
Inputs may be any that keep to these rules, and one draw needn't show every extreme that they name: `kept`: for head h and query tile t, slots 0 to 3 hold the key tiles 4 * t to 4 * t + 3 in order; the entries of one list are distinct; slots at or past counts[h, t] are padding.
All inputs are finite; a program needn't handle non-finite values.
Results may differ from the reference program's by a relative error of at most 0.0046.
Values may be sent and summed in bfloat16 or wider, within the bound.
No kernel may reach another device: no remote copies, remote signals or barrier semaphores. Data moves between devices by JAX's collectives and lax.ppermute only.
A program may use at most 128 MiB of HBM per device.

```python
import jax
import jax.numpy as jnp
from jax import lax

HEADS = 32
HEAD_DIM = 128
QTILE = 512
KTILE = 128
GROUP = 4
SEQ = 2048
QT = 4
KT = 16
OWN = 4
KEEP_MAX = 8


def draw_queries(key, part):
    key = jax.random.fold_in(key, 1)
    drawn = jnp.clip(jax.random.normal(key, (SEQ, HEADS * HEAD_DIM), jnp.float32), -6.0, 6.0)
    return drawn.astype(jnp.bfloat16)


def draw_keys(key, part):
    key = jax.random.fold_in(key, 2)
    drawn = jnp.clip(jax.random.normal(key, (SEQ, HEADS * HEAD_DIM), jnp.float32), -6.0, 6.0)
    return drawn.astype(jnp.bfloat16)


def draw_kept(key, part):
    key = jax.random.fold_in(key, 9)
    others = KT - OWN
    ranking = jax.random.randint(key, (HEADS, QT, others), 0, 1 << 20) * others + jnp.arange(others, dtype=jnp.int32)
    shuffled = jnp.argsort(ranking, axis=-1)[:, :, :KEEP_MAX - OWN].astype(jnp.int32)
    tile_base = (jnp.arange(QT, dtype=jnp.int32) * OWN)[None, :, None]
    mapped = jnp.where(shuffled >= tile_base, shuffled + OWN, shuffled)
    own_tiles = jnp.broadcast_to(tile_base + jnp.arange(OWN, dtype=jnp.int32)[None, None, :], (HEADS, QT, OWN))
    return jnp.concatenate([own_tiles, mapped], axis=-1).astype(jnp.int32)


def draw_counts(key, part):
    key = jax.random.fold_in(key, 7)
    heaviness = 2 ** jax.random.randint(jax.random.fold_in(key, 1), (HEADS, 1), 0, 4)
    upper = (KEEP_MAX - OWN) * heaviness // 8
    additional = jax.random.randint(jax.random.fold_in(key, 2), (HEADS, QT), 0, upper + 1)
    counts = (OWN + additional).astype(jnp.int32)
    heavy_head = jax.random.randint(jax.random.fold_in(key, 3), (), 0, HEADS)
    heavy_tile = jax.random.randint(jax.random.fold_in(key, 4), (), 0, QT)
    return counts.at[heavy_head, heavy_tile].set(KEEP_MAX).astype(jnp.int32)


def steps_of(key, dims, cuts, low, high):
    factor_of, own = 1.0, jax.random.fold_in(key, 6)
    for axis_at, parts in cuts:
        heights = jnp.exp(jax.random.uniform(jax.random.fold_in(own, axis_at), (parts,), jnp.float32, low / len(cuts), high / len(cuts)))
        factor_of = factor_of * jnp.repeat(heights, dims[axis_at] // parts).reshape([-1 if axis == axis_at else 1 for axis in range(len(dims))])
    return factor_of


def normal_values(stream_key, dims, spread, bound, split=(), kind=jnp.bfloat16):
    result = spread * jax.random.normal(stream_key, dims, jnp.float32)
    if split:
        result = result * steps_of(stream_key, dims, split, -0.22, 0.18)
    return jnp.clip(result, -bound, bound).astype(kind)


def setup_inputs(seed: int = 0, part: int = 0) -> dict:
    key_of = jax.random.split(jax.random.key(seed), 6)
    part_splits = jax.random.split(jax.random.fold_in(key_of[5], part), 6)
    queries = draw_queries(jax.random.fold_in(jax.random.fold_in(key_of[5], part), 71), part)
    keys = draw_keys(jax.random.fold_in(jax.random.fold_in(key_of[5], part), 71), part)
    values = normal_values(part_splits[2], (SEQ, HEADS * HEAD_DIM), 1.0, 6.0, ((0, 16),))
    kept = draw_kept(jax.random.fold_in(jax.random.fold_in(key_of[5], part), 71), part)
    counts = draw_counts(jax.random.fold_in(jax.random.fold_in(key_of[5], part), 71), part)
    return dict(queries=queries, keys=keys, values=values, kept=kept, counts=counts)


def attend_tile(query_tile, key_tiles, value_tiles, slot_list, live_count):
    row_count = query_tile.shape[0]
    factor = 1.0 / (query_tile.shape[1] ** 0.5)
    start_state = (jnp.full((row_count,), -1e30, jnp.float32), jnp.zeros((row_count,), jnp.float32), jnp.zeros((row_count, query_tile.shape[1]), jnp.float32))

    def advance(block_num, state_now):
        running, totals, numerator = state_now
        first = (block_num * GROUP).astype(jnp.int32)
        chosen = lax.dynamic_slice_in_dim(slot_list, first, GROUP)
        key_block = key_tiles[chosen].reshape(GROUP * KTILE, query_tile.shape[1])
        value_block = value_tiles[chosen].reshape(GROUP * KTILE, query_tile.shape[1])
        scores = jnp.dot(query_tile, key_block.T, preferred_element_type=jnp.float32) * factor
        live_mask = jnp.repeat((first + jnp.arange(GROUP, dtype=jnp.int32)) < live_count, KTILE)
        scores = jnp.where(live_mask[None, :], scores, -1e30)
        new_max = jnp.maximum(running, jnp.max(scores, axis=1))
        rescale = jnp.exp(running - new_max)
        weights = jnp.exp(scores - new_max[:, None])
        totals = totals * rescale + jnp.sum(weights, axis=1)
        numerator = numerator * rescale[:, None] + jnp.dot(weights.astype(jnp.bfloat16), value_block, preferred_element_type=jnp.float32)
        return (new_max, totals, numerator)

    block_total = ((live_count + GROUP - 1) // GROUP).astype(jnp.int32)
    running, totals, numerator = lax.fori_loop(jnp.int32(0), block_total, advance, start_state)
    return (numerator / totals[:, None]).astype(jnp.bfloat16)


def reference(queries, keys, values, kept, counts):
    head_q = queries.reshape(SEQ, HEADS, HEAD_DIM).transpose(1, 0, 2)
    head_k = keys.reshape(SEQ, HEADS, HEAD_DIM).transpose(1, 0, 2)
    head_v = values.reshape(SEQ, HEADS, HEAD_DIM).transpose(1, 0, 2)

    def per_head(packed):
        one_q, one_k, one_v, slot_rows, count_row = packed
        key_tiles = one_k.reshape(KT, KTILE, HEAD_DIM)
        value_tiles = one_v.reshape(KT, KTILE, HEAD_DIM)

        def per_tile(inner):
            query_tile, slot_list, live_count = inner
            return attend_tile(query_tile, key_tiles, value_tiles, slot_list, live_count)

        return lax.map(per_tile, (one_q.reshape(QT, QTILE, HEAD_DIM), slot_rows, count_row))

    results = lax.map(per_head, (head_q, head_k, head_v, kept, counts))
    return results.reshape(HEADS, SEQ, HEAD_DIM).transpose(1, 0, 2).reshape(SEQ, HEADS * HEAD_DIM)
```

```python
import functools

import jax
import jax.numpy as jnp
from jax import lax
from jax.experimental import pallas as pl
from jax.experimental.pallas import tpu as pltpu
from jax.sharding import PartitionSpec as P

HEAD_DIM = 128
QTILE = 512
KTILE = 128
GROUP = 4
OWN = QTILE // KTILE
SIZES = ((6, 16), (7, 16), (8, 20), (11, 24))
LIMIT = 56 * 1024 * 1024
SMEM = pl.BlockSpec(memory_space=pltpu.SMEM)
VMEM = pl.BlockSpec(memory_space=pltpu.VMEM)
HBM = pl.BlockSpec(memory_space=pl.ANY)


def params():
    return pltpu.CompilerParams(vmem_limit_bytes=LIMIT)


def columns(head):
    return pl.ds(pl.multiple_of(head * HEAD_DIM, HEAD_DIM), HEAD_DIM)


def dot_t(a, b):
    return lax.dot_general(a, b, (((1,), (1,)), ((), ())), preferred_element_type=jnp.float32)


def dot(a, b):
    return jnp.dot(a, b, preferred_element_type=jnp.float32)


def pack_kernel(heads, planes, slots, room, where, kept, counts, k_ref, v_ref, *outs):
    plane, tile = where[0], where[1]
    for step, out in enumerate(outs, 1):
        target = lax.rem(plane + step, planes)

        def look(head, used, out=out, target=target):
            row = head * planes + target
            live = counts[row]
            hit = jnp.int32(0)
            for j in range(OWN, slots):
                hit = jnp.where((j < live) & (kept[row * slots + j] == tile), 1, hit)

            @pl.when((hit == 1) & (used < room))
            def _():
                out[used, 0] = k_ref[:, columns(head)]
                out[used, 1] = v_ref[:, columns(head)]

            return used + hit

        lax.fori_loop(0, heads, look, jnp.int32(0))


def plan_kernel(heads, planes, slots, room, where, kept, counts, extra, spot, order, place, far, used):
    plane, side, core = where[0], where[2], where[3]
    for b in range(2 * (planes - 1)):
        used[b] = 0

    def look(head, free):
        row = head * planes + plane
        live = counts[row]
        near, other = jnp.int32(0), jnp.int32(0)
        for j in range(OWN, slots):
            tile = kept[row * slots + j]
            is_live = j < live
            here = ((tile >> 1) & 1) == side
            step = lax.rem(plane - (tile >> 2) + planes, planes)
            box = jnp.clip((step - 1) * 2 + jnp.where((tile & 1) == core, 0, 1), 0, 2 * (planes - 1) - 1)
            taken = used[box]

            @pl.when(is_live & here)
            def _(box=box, taken=taken, near=near):
                used[box] = taken + 1
                spot[head * (slots - OWN) + near] = box * room + taken

            near = near + jnp.where(is_live & here, 1, 0)
            other = other + jnp.where(is_live & ~here, 1, 0)
        extra[head] = near
        far[head] = other
        return (free[0] + jnp.where(near == 0, 1, 0), free[1] + jnp.where(other == 0, 1, 0))

    free, far_free = lax.fori_loop(0, heads, look, (jnp.int32(0), jnp.int32(0)))

    def put(head, state):
        a, b, c, d = state
        none, far_none = extra[head] == 0, far[head] == 0
        at = jnp.where(none, a, b)
        order[at] = head
        place[head] = at
        far[head] = jnp.where(far_none, c, d)
        return (
            a + jnp.where(none, 1, 0),
            b + jnp.where(none, 0, 1),
            c + jnp.where(far_none, 1, 0),
            d + jnp.where(far_none, 0, 1),
        )

    lax.fori_loop(0, heads, put, (jnp.int32(0), free, jnp.int32(0), far_free))


def own_kernel(heads, early, order, q_ref, far_q, k_ref, v_ref, mate_k, mate_v, *outs):
    if early:
        sent, late, here, lse_far, lse_here = outs
    else:
        late, here, lse_far, lse_here = outs
    rows = q_ref.shape[0]
    factor = 1.0 / HEAD_DIM**0.5
    lane = lax.broadcasted_iota(jnp.int32, (2 * rows, HEAD_DIM), 1)

    def attend(slot, lse):
        at = columns(order[slot])
        q = jnp.concatenate([far_q[:, at], q_ref[:, at]], axis=0)
        k = jnp.concatenate([k_ref[:, at], mate_k[:, at]], axis=0)
        v = jnp.concatenate([v_ref[:, at], mate_v[:, at]], axis=0)
        s = dot_t(q, k) * factor
        m = jnp.max(s, axis=1, keepdims=True)
        w = jnp.exp(s - m)
        l = jnp.sum(w, axis=1, keepdims=True)
        o = dot(w.astype(jnp.bfloat16), v) / l
        here[slot] = o[rows:]
        return o[:rows], jnp.where(lane == slot, m + jnp.log(l), lse)

    def first(slot, lse):
        o, lse = attend(slot, lse)
        sent[slot] = o.astype(jnp.bfloat16)
        return lse

    def second(slot, lse):
        o, lse = attend(slot, lse)
        late[slot - early] = o
        return lse

    lse = jnp.zeros((2 * rows, HEAD_DIM), jnp.float32)
    if early:
        lse = lax.fori_loop(0, early, first, lse, unroll=2)
    lse = lax.fori_loop(early, heads, second, lse, unroll=2)
    lse_far[...] = lse[:rows]
    lse_here[...] = lse[rows:]


def late_kernel(late, early, first, depth, room, order, extra, spot, q_ref, o_ref, lse_ref, *rest):
    boxes, (out, lse_out, tiles, sems) = rest[:-4], rest[-4:]
    copies = [
        pltpu.make_async_copy(box, tiles.at[pl.ds(b * room, room)], sems.at[b]) for b, box in enumerate(boxes)
    ]
    for copy in copies:
        copy.start()
    rows = q_ref.shape[0]
    factor = 1.0 / HEAD_DIM**0.5
    lane = lax.broadcasted_iota(jnp.int32, (rows, HEAD_DIM), 1)
    for copy in copies:
        copy.wait()

    def attend(i, lse):
        slot = early + i
        head = order[slot]
        q = q_ref[:, columns(head)]
        start = jnp.sum(jnp.where(lane == slot, lse_ref[...], 0.0), axis=1, keepdims=True)

        def add(e, state):
            m, l, o = state
            at = spot[head * depth + e]
            s = dot_t(q, tiles[at, 0]) * factor
            new = jnp.maximum(m, jnp.max(s, axis=1, keepdims=True))
            w = jnp.exp(s - new)
            shrink = jnp.exp(m - new)
            l = l * shrink + jnp.sum(w, axis=1, keepdims=True)
            return new, l, o * shrink + dot(w.astype(jnp.bfloat16), tiles[at, 1])

        m, l, o = lax.fori_loop(0, extra[head], add, (start, jnp.ones_like(start), o_ref[first + i]))
        out[i] = (o / l).astype(out.dtype)
        return jnp.where(lane == slot, m + jnp.log(l), lse)

    lse_out[...] = lax.fori_loop(0, late, attend, jnp.zeros((rows, HEAD_DIM), jnp.float32))


def merge_kernel(heads, early, place, far, here, here_late, lse_here, lse_here_late, *rest):
    if early:
        got, lse_got, got_late, lse_got_late, out, mine, theirs, sems = rest
    else:
        got_late, lse_got_late, out, mine, theirs, sems = rest
    copies = [
        pltpu.make_async_copy(here_late, mine.at[pl.ds(early, heads - early)], sems.at[0]),
        pltpu.make_async_copy(got_late, theirs.at[pl.ds(early, heads - early)], sems.at[1]),
    ]
    if early:
        copies += [
            pltpu.make_async_copy(here.at[pl.ds(0, early)], mine.at[pl.ds(0, early)], sems.at[2]),
            pltpu.make_async_copy(got, theirs.at[pl.ds(0, early)], sems.at[3]),
        ]
    for copy in copies:
        copy.start()
    rows = out.shape[0]
    lane = lax.broadcasted_iota(jnp.int32, (rows, HEAD_DIM), 1)
    a_all, b_all = lse_here_late[...], lse_got_late[...]
    if early:
        a_all = jnp.where(lane < early, lse_here[...], a_all)
        b_all = jnp.where(lane < early, lse_got[...], b_all)
    for copy in copies:
        copy.wait()

    def merge(head, carry):
        p, r = place[head], far[head]
        a = jnp.sum(jnp.where(lane == p, a_all, 0.0), axis=1, keepdims=True)
        b = jnp.sum(jnp.where(lane == r, b_all, 0.0), axis=1, keepdims=True)
        m = jnp.maximum(a, b)
        wa, wb = jnp.exp(a - m), jnp.exp(b - m)
        total = wa * mine[p] + wb * theirs[r].astype(jnp.float32)
        out[:, columns(head)] = (total / (wa + wb)).astype(out.dtype)
        return carry

    lax.fori_loop(0, heads, merge, 0, unroll=2)


def exchange(room, late, planes, slots, queries, keys, values, kept, counts, where):
    rows, features = queries.shape
    heads = features // HEAD_DIM
    early = heads - late
    depth = slots - OWN
    f32, bf16, i32 = jnp.float32, jnp.bfloat16, jnp.int32
    shape = jax.ShapeDtypeStruct
    tile = (rows, HEAD_DIM)
    count = planes * OWN
    across = [(d, d ^ 2) for d in range(count)]
    beside = [(d, d ^ 1) for d in range(count)]

    packed = pl.pallas_call(
        functools.partial(pack_kernel, heads, planes, slots, room),
        out_shape=[shape((room, 2) + tile, bf16)] * (planes - 1),
        in_specs=[SMEM] * 3 + [VMEM] * 2,
        out_specs=[VMEM] * (planes - 1),
        compiler_params=params(),
        name="pack",
    )(where, kept, counts, keys, values)
    far_q = lax.ppermute(queries, "seq", across)
    mate_k = lax.ppermute(keys, "seq", beside)
    mate_v = lax.ppermute(values, "seq", beside)
    boxes = []
    for step in range(1, planes):
        got = lax.ppermute(packed[step - 1], "seq", [(d, (d + OWN * step) % count) for d in range(count)])
        boxes += [got, lax.ppermute(got, "seq", beside)]

    extra, spot, order, place, far = pl.pallas_call(
        functools.partial(plan_kernel, heads, planes, slots, room),
        out_shape=[shape((n,), i32) for n in (heads, heads * depth, heads, heads, heads)],
        in_specs=[SMEM] * 3,
        out_specs=[SMEM] * 5,
        scratch_shapes=[pltpu.SMEM((2 * planes,), i32)],
        compiler_params=params(),
        name="plan",
    )(where, kept, counts)

    sent_shape = [shape((early,) + tile, bf16)] if early else []
    *sent, rest, here, lse_far, lse_here = pl.pallas_call(
        functools.partial(own_kernel, heads, early),
        out_shape=sent_shape
        + [shape((late,) + tile, f32), shape((heads,) + tile, f32), shape(tile, f32), shape(tile, f32)],
        in_specs=[SMEM] + [VMEM] * 6,
        out_specs=[VMEM] * (len(sent_shape) + 4),
        compiler_params=params(),
        name="own",
    )(order, queries, far_q, keys, values, mate_k, mate_v)

    def add_extras(q, o, lse, first, kind):
        return pl.pallas_call(
            functools.partial(late_kernel, late, early, first, depth, room),
            out_shape=[shape((late,) + tile, kind), shape(tile, f32)],
            in_specs=[SMEM] * 3 + [VMEM] * 3 + [HBM] * len(boxes),
            out_specs=[VMEM] * 2,
            scratch_shapes=[
                pltpu.VMEM((len(boxes) * room, 2) + tile, bf16),
                pltpu.SemaphoreType.DMA((len(boxes),)),
            ],
            compiler_params=params(),
            name="late",
        )(order, extra, spot, q, o, lse, *boxes)

    arrived = []
    if early:
        arrived = [lax.ppermute(sent[0], "seq", across), lax.ppermute(lse_far, "seq", across)]
    far_late, lse_far_late = add_extras(far_q, rest, lse_far, 0, bf16)
    arrived += [lax.ppermute(far_late, "seq", across), lax.ppermute(lse_far_late, "seq", across)]
    here_late, lse_here_late = add_extras(queries, here, lse_here, early, f32)

    return pl.pallas_call(
        functools.partial(merge_kernel, heads, early),
        out_shape=shape((rows, features), bf16),
        in_specs=[SMEM] * 2 + [HBM] * 2 + [VMEM] * 2 + [HBM, VMEM] * (len(arrived) // 2),
        out_specs=VMEM,
        scratch_shapes=[
            pltpu.VMEM((heads,) + tile, f32),
            pltpu.VMEM((heads,) + tile, bf16),
            pltpu.SemaphoreType.DMA((4,)),
        ],
        compiler_params=params(),
        name="merge",
    )(place, far, here, here_late, lse_here, lse_here_late, *arrived)


def per_plane(queries, keys, values, kept, counts):
    heads, planes, slots = kept.shape
    device = lax.axis_index("seq").astype(jnp.int32)
    where = jnp.stack([device // OWN, device, (device // 2) % 2, device % 2])
    live = jnp.arange(OWN, slots, dtype=jnp.int32) < counts[:, :, None]
    tiles = jnp.arange(planes * OWN, dtype=jnp.int32)
    need = ((kept[:, :, OWN:, None] == tiles) & live[..., None]).astype(jnp.int32).sum(axis=2)
    most = need.sum(axis=0).max()
    sided = need.reshape(heads, planes, planes, 2, 2).sum(axis=(2, 4))
    touched = (sided > 0).astype(jnp.int32).sum(axis=0).max()
    sizes = SIZES + ((heads, heads),)
    choice = jnp.int32(0)
    for room, late in sizes[:-1]:
        choice = choice + ((most > room) | (touched > late)).astype(jnp.int32)
    return lax.switch(
        choice,
        [functools.partial(exchange, room, late, planes, slots) for room, late in sizes],
        queries,
        keys,
        values,
        kept.reshape(-1),
        counts.reshape(-1),
        where,
    )


def attend_tile(query_tile, key_tiles, value_tiles, slot_list, live_count):
    row_count = query_tile.shape[0]
    factor = 1.0 / query_tile.shape[1] ** 0.5
    start_state = (
        jnp.full((row_count,), -1e30, jnp.float32),
        jnp.zeros((row_count,), jnp.float32),
        jnp.zeros((row_count, query_tile.shape[1]), jnp.float32),
    )

    def advance(block_num, state_now):
        running, totals, numerator = state_now
        first = (block_num * GROUP).astype(jnp.int32)
        chosen = lax.dynamic_slice_in_dim(slot_list, first, GROUP)
        key_block = key_tiles[chosen].reshape(GROUP * KTILE, query_tile.shape[1])
        value_block = value_tiles[chosen].reshape(GROUP * KTILE, query_tile.shape[1])
        scores = jnp.dot(query_tile, key_block.T, preferred_element_type=jnp.float32) * factor
        live_mask = jnp.repeat(first + jnp.arange(GROUP, dtype=jnp.int32) < live_count, KTILE)
        scores = jnp.where(live_mask[None, :], scores, -1e30)
        new_max = jnp.maximum(running, jnp.max(scores, axis=1))
        rescale = jnp.exp(running - new_max)
        weights = jnp.exp(scores - new_max[:, None])
        totals = totals * rescale + jnp.sum(weights, axis=1)
        numerator = numerator * rescale[:, None] + jnp.dot(
            weights.astype(jnp.bfloat16), value_block, preferred_element_type=jnp.float32
        )
        return (new_max, totals, numerator)

    block_total = (live_count + GROUP - 1) // GROUP
    running, totals, numerator = lax.fori_loop(jnp.int32(0), block_total, advance, start_state)
    return (numerator / totals[:, None]).astype(jnp.bfloat16)


def per_device(queries, keys, values, kept, counts):
    local_rows, feature_count = queries.shape
    shards = lax.axis_size("seq")
    device = lax.axis_index("seq")
    head_count = feature_count // HEAD_DIM
    replicas = max(1, shards // head_count)
    slots_here = max(1, head_count // shards)
    total_rows = local_rows * shards
    tile_count = counts.shape[1]
    stacked = jnp.stack([queries, keys, values])
    copied = jnp.broadcast_to(
        stacked.reshape(3, local_rows, head_count, 1, HEAD_DIM),
        (3, local_rows, head_count, replicas, HEAD_DIM),
    )
    copied = copied.reshape(3, local_rows, head_count * replicas, HEAD_DIM)
    arrived = lax.all_to_all(copied, "seq", split_axis=2, concat_axis=1, tiled=True)
    head_data = arrived.transpose(2, 0, 1, 3)
    tiles_each = tile_count // replicas
    results = []
    for j in range(slots_here):
        global_slot = device * slots_here + j
        head_id = global_slot // replicas
        replica_id = global_slot % replicas
        slot_rows = lax.dynamic_index_in_dim(kept, head_id, 0, keepdims=False)
        count_row = lax.dynamic_index_in_dim(counts, head_id, 0, keepdims=False)
        all_queries = head_data[j, 0]
        key_tiles = head_data[j, 1].reshape(total_rows // KTILE, KTILE, HEAD_DIM)
        value_tiles = head_data[j, 2].reshape(total_rows // KTILE, KTILE, HEAD_DIM)
        rounds = jnp.arange(tiles_each, dtype=jnp.int32)
        tile_ids = replica_id * tiles_each + rounds

        def process(i, output):
            tile_id = tile_ids[i]
            query_tile = lax.dynamic_slice_in_dim(all_queries, tile_id * QTILE, QTILE, 0)
            finished = attend_tile(
                query_tile, key_tiles, value_tiles, slot_rows[tile_id], count_row[tile_id]
            )
            return lax.dynamic_update_slice_in_dim(output, finished, tile_id * QTILE, 0)

        results.append(
            lax.fori_loop(0, tiles_each, process, jnp.zeros((total_rows, HEAD_DIM), jnp.bfloat16))
        )
    gathered = jnp.stack(results, axis=1)
    returned = lax.all_to_all(gathered, "seq", split_axis=0, concat_axis=1, tiled=True)
    combined = (
        returned.reshape(local_rows, head_count, replicas, HEAD_DIM).astype(jnp.float32).sum(axis=2)
    )
    return combined.astype(jnp.bfloat16).reshape(local_rows, feature_count)


def solution(mesh):
    by_rows = P(("groups", "seq"), None)
    placed = (by_rows, by_rows, by_rows, P("groups", None, None), P("groups", None))

    def step(queries, keys, values, kept, counts):
        planes = counts.shape[1]
        one_tile_each = queries.shape[0] == KTILE and mesh.shape["seq"] == planes * OWN
        run = per_plane if one_tile_each and planes == 4 else per_device
        return run(queries, keys, values, kept, counts)

    return jax.shard_map(step, mesh=mesh, in_specs=placed, out_specs=by_rows, check_vma=False)
```

```python
import functools

import jax
import jax.numpy as jnp
from jax import lax
from jax.experimental import pallas as pl
from jax.experimental.pallas import tpu as pltpu
from jax.sharding import PartitionSpec as P

HEAD_DIM = 128
QTILE = 512
KTILE = 128
GROUP = 4
OWN = QTILE // KTILE
SIZES = ((5, 16), (6, 16), (7, 16), (8, 20), (11, 24))
LIMIT = 56 * 1024 * 1024
SMEM = pl.BlockSpec(memory_space=pltpu.SMEM)
VMEM = pl.BlockSpec(memory_space=pltpu.VMEM)
HBM = pl.BlockSpec(memory_space=pl.ANY)


def params():
    return pltpu.CompilerParams(vmem_limit_bytes=LIMIT)


def cost(flops):
    return pl.CostEstimate(flops=flops, bytes_accessed=8 << 20, transcendentals=0)


def pieces(early):
    return (early // 2, early - early // 2) if early else ()


def columns(head):
    if isinstance(head, int):
        return pl.ds(head * HEAD_DIM, HEAD_DIM)
    return pl.ds(pl.multiple_of(head * HEAD_DIM, HEAD_DIM), HEAD_DIM)


def dot_t(a, b):
    return lax.dot_general(a, b, (((1,), (1,)), ((), ())), preferred_element_type=jnp.float32)


def dot(a, b):
    return jnp.dot(a, b, preferred_element_type=jnp.float32)


def lists_kernel(planes, slots, where, kept, counts, sends, takes, choice):
    plane, tile = where[0], where[1]
    heads = kept.shape[1]
    shape = (planes * OWN, heads)
    ids = lax.broadcasted_iota(jnp.int32, shape, 0)
    bit = jnp.left_shift(jnp.int32(1), lax.broadcasted_iota(jnp.int32, shape, 1))
    most = jnp.zeros((planes * OWN, 1), jnp.int32)
    touched = jnp.zeros((1, 1), jnp.int32)
    taken = jnp.zeros(shape, jnp.int32)
    for t in range(planes):
        hits = jnp.zeros(shape, jnp.int32)
        for j in range(OWN, slots):
            named = (ids == kept[t * slots + j : t * slots + j + 1, :]) & (counts[t : t + 1, :] > j)
            hits = jnp.where(named, 1, hits)
        most = jnp.maximum(most, jnp.sum(hits, axis=1, keepdims=True))
        for side in range(2):
            some = jnp.max(jnp.where(((ids >> 1) & 1) == side, hits, 0), axis=0, keepdims=True)
            touched = jnp.maximum(touched, jnp.sum(some, axis=1, keepdims=True))
        bits = hits * bit
        mine = jnp.sum(jnp.where(ids == tile, bits, 0), axis=0, keepdims=True)
        sends[t : t + 1, :] = jnp.broadcast_to(jnp.sum(mine, axis=1, keepdims=True), (1, HEAD_DIM))
        taken = jnp.where(plane == t, bits, taken)
    takes[...] = jnp.broadcast_to(jnp.sum(taken, axis=1, keepdims=True), (planes * OWN, HEAD_DIM))
    top, wide = jnp.max(most), jnp.max(touched)
    index = jnp.int32(0)
    for room, late in SIZES:
        index = index + jnp.where((top > room) | (wide > late), 1, 0)
    choice[0] = index


def pack_kernel(heads, planes, room, where, sends, k_ref, v_ref, *outs):
    for step, out in enumerate(outs, 1):
        bits = sends[lax.rem(where[0] + step, planes), 0]

        def look(head, used, out=out, bits=bits):
            hit = (bits >> head) & 1

            @pl.when((hit == 1) & (used < room))
            def _():
                out[used, 0] = k_ref[:, columns(head)]
                out[used, 1] = v_ref[:, columns(head)]

            return used + hit

        lax.fori_loop(0, heads, look, jnp.int32(0))


def plan_kernel(heads, planes, room, where, takes, pair, begin, order, place, far):
    plane, side, core = where[0], where[2], where[3]
    near, other = [], []
    for step in range(1, planes):
        source = lax.rem(plane - step + planes, planes) * OWN
        for turn in range(2):
            who = jnp.where(core == turn, 0, 1)
            near.append(takes[source + 2 * side + who, 0])
            other.append(takes[source + 2 * (1 - side) + turn, 0])
    any_near = functools.reduce(jnp.bitwise_or, near)
    any_other = functools.reduce(jnp.bitwise_or, other)

    def free(bits):
        return lax.fori_loop(0, heads, lambda h, n: n + 1 - ((bits >> h) & 1), jnp.int32(0))

    def put(head, state):
        a, b, c, d, pairs, *used = state
        none, far_none = 1 - ((any_near >> head) & 1), 1 - ((any_other >> head) & 1)
        at = jnp.where(none == 1, a, b)
        order[at] = head
        place[head] = at
        far[head] = jnp.where(far_none == 1, c, d)
        begin[head] = pairs
        for box, bits in enumerate(near):
            hit = (bits >> head) & 1

            @pl.when(hit == 1)
            def _(box=box, pairs=pairs, used=used):
                pair[pairs] = head * 4096 + box * room + used[box]

            pairs = pairs + hit
            used = used[:box] + [used[box] + hit] + used[box + 1 :]
        return (a + none, b + 1 - none, c + far_none, d + 1 - far_none, pairs, *used)

    zero = jnp.int32(0)
    state = lax.fori_loop(0, heads, put, (zero, free(any_near), zero, free(any_other), zero) + (zero,) * len(near))
    begin[heads] = state[4]


def soften(q, k, v):
    s = dot_t(q, k) * (1.0 / HEAD_DIM**0.5)
    m = jnp.max(s, axis=1, keepdims=True)
    w = jnp.exp(s - m)
    l = jnp.sum(w, axis=1, keepdims=True)
    return dot(w.astype(jnp.bfloat16), v) / l, m + jnp.log(l)


def own_kernel(order, q_ref, k_ref, v_ref, mate_k, mate_v, *outs):
    *parts, lse_out = outs
    lane = lax.broadcasted_iota(jnp.int32, lse_out.shape, 1)
    lse = jnp.zeros(lse_out.shape, jnp.float32)
    start = 0
    for part in parts:

        def attend(i, lse, part=part, start=start):
            head = order[start + i]
            at = columns(head)
            k = jnp.concatenate([k_ref[:, at], mate_k[:, at]], axis=0)
            v = jnp.concatenate([v_ref[:, at], mate_v[:, at]], axis=0)
            o, new = soften(q_ref[:, at], k, v)
            part[i] = o.astype(part.dtype)
            return jnp.where(lane == head, new, lse)

        lse = lax.fori_loop(0, part.shape[0], attend, lse, unroll=4)
        start += part.shape[0]
    lse_out[...] = lse


def late_kernel(late, early, first, room, order, pair, begin, q_ref, o_ref, lse_ref, *rest):
    boxes, (out, lse_out, tiles, partial, sems) = rest[:-5], rest[-5:]
    copies = [
        pltpu.make_async_copy(box, tiles.at[pl.ds(b * room, room)], sems.at[b]) for b, box in enumerate(boxes)
    ]
    for copy in copies:
        copy.start()
    heads = order.shape[0]
    rows = q_ref.shape[0]
    lane = lax.broadcasted_iota(jnp.int32, (rows, HEAD_DIM), 1)
    total = begin[heads]
    for copy in copies:
        copy.wait()

    def both(i, parts):
        at = jnp.minimum(i, total - 1)
        code = pair[at]
        head, tile = code >> 12, code & 4095
        o, new = soften(q_ref[:, columns(head)], tiles[tile, 0], tiles[tile, 1])
        partial[at] = o
        return jnp.where(lane == at, new, parts)

    def four(i, parts):
        for j in range(4):
            parts = both(4 * i + j, parts)
        return parts

    parts = lax.fori_loop(0, (total + 3) >> 2, four, jnp.zeros((rows, HEAD_DIM), jnp.float32))

    def join(i, lse):
        head = order[early + i]
        start, end = begin[head], begin[head + 1]
        base = jnp.sum(jnp.where(lane == head, lse, 0.0), axis=1, keepdims=True)
        inside = (lane >= start) & (lane < end)
        m = jnp.maximum(base, jnp.max(jnp.where(inside, parts, -1e30), axis=1, keepdims=True))
        w = jnp.where(inside, jnp.exp(jnp.where(inside, parts, m) - m), 0.0)
        mine = jnp.exp(base - m)
        l = mine + jnp.sum(w, axis=1, keepdims=True)

        def add(p, o):
            return o + jnp.sum(jnp.where(lane == p, w, 0.0), axis=1, keepdims=True) * partial[p]

        o = lax.fori_loop(start, end, add, mine * o_ref[first + i])
        out[i] = (o / l).astype(out.dtype)
        return jnp.where(lane == head, m + jnp.log(l), lse)

    lse_out[...] = lax.fori_loop(0, late, join, lse_ref[...])


def merge_kernel(heads, early, place, far, here, here_late, lse_here, lse_got, *rest):
    *got, got_late, out, mine, theirs, sems = rest
    copies = [
        pltpu.make_async_copy(here_late, mine.at[pl.ds(early, heads - early)], sems.at[0]),
        pltpu.make_async_copy(got_late, theirs.at[pl.ds(early, heads - early)], sems.at[1]),
    ]
    if early:
        copies.append(pltpu.make_async_copy(here.at[pl.ds(0, early)], mine.at[pl.ds(0, early)], sems.at[2]))
        start = 0
        for i, part in enumerate(got):
            at = theirs.at[pl.ds(start, part.shape[0])]
            copies.append(pltpu.make_async_copy(part, at, sems.at[3 + i]))
            start += part.shape[0]
    for copy in copies:
        copy.start()
    a, b = lse_here[...], lse_got[...]
    m = jnp.maximum(a, b)
    wa, wb = jnp.exp(a - m), jnp.exp(b - m)
    total = wa + wb
    wa, wb = wa / total, wb / total
    for copy in copies:
        copy.wait()
    for head in range(heads):
        joined = wa[:, head : head + 1] * mine[place[head]]
        joined += wb[:, head : head + 1] * theirs[far[head]].astype(jnp.float32)
        out[:, columns(head)] = joined.astype(out.dtype)


def exchange(room, late, planes, queries, keys, values, mate_k, mate_v, sends, takes, where):
    rows, features = queries.shape
    heads = features // HEAD_DIM
    early = heads - late
    f32, bf16, i32 = jnp.float32, jnp.bfloat16, jnp.int32
    shape = jax.ShapeDtypeStruct
    tile = (rows, HEAD_DIM)
    count = planes * OWN
    across = [(d, d ^ 2) for d in range(count)]
    beside = [(d, d ^ 1) for d in range(count)]
    barrier = lax.optimization_barrier

    far_q = lax.ppermute(queries, "seq", across)
    packed = pl.pallas_call(
        functools.partial(pack_kernel, heads, planes, room),
        out_shape=[shape((room, 2) + tile, bf16)] * (planes - 1),
        in_specs=[SMEM] * 2 + [VMEM] * 2,
        out_specs=[VMEM] * (planes - 1),
        compiler_params=params(),
        cost_estimate=cost(4 << 30),
        name="pack",
    )(where, sends, keys, values)
    landed = [
        lax.ppermute(packed[step - 1], "seq", [(d, (d + OWN * step) % count) for d in range(count)])
        for step in range(1, planes)
    ]

    where, takes, *packed = barrier((where, takes, *packed))
    most_pairs = min(2 * (planes - 1) * room, HEAD_DIM)
    pair, begin, order, place, far = pl.pallas_call(
        functools.partial(plan_kernel, heads, planes, room),
        out_shape=[shape((n,), i32) for n in (most_pairs, heads + 1, heads, heads, heads)],
        in_specs=[SMEM] * 2,
        out_specs=[SMEM] * 5,
        compiler_params=params(),
        cost_estimate=cost(4 << 30),
        name="plan",
    )(where, takes)

    def attend_own(q, order, parts):
        return pl.pallas_call(
            own_kernel,
            out_shape=[shape((n,) + tile, kind) for n, kind in parts] + [shape(tile, f32)],
            in_specs=[SMEM] + [VMEM] * 5,
            out_specs=[VMEM] * (len(parts) + 1),
            compiler_params=params(),
            cost_estimate=cost(8 << 30),
            name="own",
        )(order, q, keys, values, mate_k, mate_v)

    here, lse_here = attend_own(queries, order, [(heads, f32)])
    order, here = barrier((order, here))
    *sent, rest, lse_far = attend_own(far_q, order, [(n, bf16) for n in pieces(early)] + [(late, f32)])
    arrived = [lax.ppermute(x, "seq", across) for x in sent]
    *landed, rest, here, lse_far, lse_here, arrived = barrier((*landed, rest, here, lse_far, lse_here, arrived))
    boxes = []
    for got in landed:
        boxes += [got, lax.ppermute(got, "seq", beside)]

    def add_extras(q, o, lse, first, kind):
        return pl.pallas_call(
            functools.partial(late_kernel, late, early, first, room),
            out_shape=[shape((late,) + tile, kind), shape(tile, f32)],
            in_specs=[SMEM] * 3 + [VMEM] * 3 + [HBM] * len(boxes),
            out_specs=[VMEM] * 2,
            scratch_shapes=[
                pltpu.VMEM((len(boxes) * room, 2) + tile, bf16),
                pltpu.VMEM((most_pairs,) + tile, f32),
                pltpu.SemaphoreType.DMA((len(boxes),)),
            ],
            compiler_params=params(),
            cost_estimate=cost(4 << 30),
            name="late",
        )(order, pair, begin, q, o, lse, *boxes)

    far_late, lse_far = add_extras(far_q, rest, lse_far, 0, bf16)
    arrived = [lax.ppermute(lse_far, "seq", across), *arrived, lax.ppermute(far_late, "seq", across)]
    here_late, lse_here = add_extras(queries, here, lse_here, early, f32)

    return pl.pallas_call(
        functools.partial(merge_kernel, heads, early),
        out_shape=shape((rows, features), bf16),
        in_specs=[SMEM] * 2 + [HBM] * 2 + [VMEM] * 2 + [HBM] * (len(arrived) - 1),
        out_specs=VMEM,
        scratch_shapes=[
            pltpu.VMEM((heads,) + tile, f32),
            pltpu.VMEM((heads,) + tile, bf16),
            pltpu.SemaphoreType.DMA((5,)),
        ],
        compiler_params=params(),
        cost_estimate=cost(4 << 30),
        name="merge",
    )(place, far, here, here_late, lse_here, *arrived)


def per_plane(queries, keys, values, kept, counts):
    heads, planes, slots = kept.shape
    device = lax.axis_index("seq").astype(jnp.int32)
    where = jnp.stack([device >> 2, device, (device >> 1) & 1, device & 1])
    beside = [(d, d ^ 1) for d in range(planes * OWN)]
    mate_k = lax.ppermute(keys, "seq", beside)
    mate_v = lax.ppermute(values, "seq", beside)
    shape = jax.ShapeDtypeStruct
    sends, takes, choice = pl.pallas_call(
        functools.partial(lists_kernel, planes, slots),
        out_shape=[
            shape((planes, HEAD_DIM), jnp.int32),
            shape((planes * OWN, HEAD_DIM), jnp.int32),
            shape((1,), jnp.int32),
        ],
        in_specs=[SMEM] + [VMEM] * 2,
        out_specs=[VMEM] * 2 + [SMEM],
        compiler_params=params(),
        name="lists",
    )(where, kept.transpose(1, 2, 0).reshape(planes * slots, heads), counts.T)
    sizes = SIZES + ((heads, heads),)
    return lax.switch(
        choice[0],
        [functools.partial(exchange, room, late, planes) for room, late in sizes],
        queries,
        keys,
        values,
        mate_k,
        mate_v,
        sends,
        takes,
        where,
    )


def attend_tile(query_tile, key_tiles, value_tiles, slot_list, live_count):
    row_count = query_tile.shape[0]
    factor = 1.0 / query_tile.shape[1] ** 0.5
    start_state = (
        jnp.full((row_count,), -1e30, jnp.float32),
        jnp.zeros((row_count,), jnp.float32),
        jnp.zeros((row_count, query_tile.shape[1]), jnp.float32),
    )

    def advance(block_num, state_now):
        running, totals, numerator = state_now
        first = (block_num * GROUP).astype(jnp.int32)
        chosen = lax.dynamic_slice_in_dim(slot_list, first, GROUP)
        key_block = key_tiles[chosen].reshape(GROUP * KTILE, query_tile.shape[1])
        value_block = value_tiles[chosen].reshape(GROUP * KTILE, query_tile.shape[1])
        scores = jnp.dot(query_tile, key_block.T, preferred_element_type=jnp.float32) * factor
        live_mask = jnp.repeat(first + jnp.arange(GROUP, dtype=jnp.int32) < live_count, KTILE)
        scores = jnp.where(live_mask[None, :], scores, -1e30)
        new_max = jnp.maximum(running, jnp.max(scores, axis=1))
        rescale = jnp.exp(running - new_max)
        weights = jnp.exp(scores - new_max[:, None])
        totals = totals * rescale + jnp.sum(weights, axis=1)
        numerator = numerator * rescale[:, None] + jnp.dot(
            weights.astype(jnp.bfloat16), value_block, preferred_element_type=jnp.float32
        )
        return (new_max, totals, numerator)

    block_total = (live_count + GROUP - 1) // GROUP
    running, totals, numerator = lax.fori_loop(jnp.int32(0), block_total, advance, start_state)
    return (numerator / totals[:, None]).astype(jnp.bfloat16)


def per_device(queries, keys, values, kept, counts):
    local_rows, feature_count = queries.shape
    shards = lax.axis_size("seq")
    device = lax.axis_index("seq")
    head_count = feature_count // HEAD_DIM
    replicas = max(1, shards // head_count)
    slots_here = max(1, head_count // shards)
    total_rows = local_rows * shards
    tile_count = counts.shape[1]
    stacked = jnp.stack([queries, keys, values])
    copied = jnp.broadcast_to(
        stacked.reshape(3, local_rows, head_count, 1, HEAD_DIM),
        (3, local_rows, head_count, replicas, HEAD_DIM),
    )
    copied = copied.reshape(3, local_rows, head_count * replicas, HEAD_DIM)
    arrived = lax.all_to_all(copied, "seq", split_axis=2, concat_axis=1, tiled=True)
    head_data = arrived.transpose(2, 0, 1, 3)
    tiles_each = tile_count // replicas
    results = []
    for j in range(slots_here):
        global_slot = device * slots_here + j
        head_id = global_slot // replicas
        replica_id = global_slot % replicas
        slot_rows = lax.dynamic_index_in_dim(kept, head_id, 0, keepdims=False)
        count_row = lax.dynamic_index_in_dim(counts, head_id, 0, keepdims=False)
        all_queries = head_data[j, 0]
        key_tiles = head_data[j, 1].reshape(total_rows // KTILE, KTILE, HEAD_DIM)
        value_tiles = head_data[j, 2].reshape(total_rows // KTILE, KTILE, HEAD_DIM)
        rounds = jnp.arange(tiles_each, dtype=jnp.int32)
        tile_ids = replica_id * tiles_each + rounds

        def process(i, output):
            tile_id = tile_ids[i]
            query_tile = lax.dynamic_slice_in_dim(all_queries, tile_id * QTILE, QTILE, 0)
            finished = attend_tile(
                query_tile, key_tiles, value_tiles, slot_rows[tile_id], count_row[tile_id]
            )
            return lax.dynamic_update_slice_in_dim(output, finished, tile_id * QTILE, 0)

        results.append(
            lax.fori_loop(0, tiles_each, process, jnp.zeros((total_rows, HEAD_DIM), jnp.bfloat16))
        )
    gathered = jnp.stack(results, axis=1)
    returned = lax.all_to_all(gathered, "seq", split_axis=0, concat_axis=1, tiled=True)
    combined = (
        returned.reshape(local_rows, head_count, replicas, HEAD_DIM).astype(jnp.float32).sum(axis=2)
    )
    return combined.astype(jnp.bfloat16).reshape(local_rows, feature_count)


def solution(mesh):
    by_rows = P(("groups", "seq"), None)
    placed = (by_rows, by_rows, by_rows, P("groups", None, None), P("groups", None))

    def step(queries, keys, values, kept, counts):
        heads, planes, slots = kept.shape
        one_tile_each = queries.shape[0] == KTILE and mesh.shape["seq"] == planes * OWN
        fits = heads <= 32 and heads * (slots - OWN) <= HEAD_DIM and planes == 4
        run = per_plane if one_tile_each and fits else per_device
        return run(queries, keys, values, kept, counts)

    return jax.shard_map(step, mesh=mesh, in_specs=placed, out_specs=by_rows, check_vma=False)
```

```python
import functools

import jax
import jax.numpy as jnp
from jax import lax
from jax.experimental import pallas as pl
from jax.experimental.pallas import tpu as pltpu
from jax.sharding import PartitionSpec as P

HEAD_DIM = 128
QTILE = 512
KTILE = 128
GROUP = 4
OWN = QTILE // KTILE
SIZES = ((4, 16), (5, 14), (5, 16), (5, 18), (6, 16), (6, 18), (7, 20), (10, 24))
MIB = 1 << 20
SMEM = pl.BlockSpec(memory_space=pltpu.SMEM)
VMEM = pl.BlockSpec(memory_space=pltpu.VMEM)
HBM = pl.BlockSpec(memory_space=pl.ANY)


def params(mib):
    return pltpu.CompilerParams(vmem_limit_bytes=mib * MIB)


def cost(flops):
    return pl.CostEstimate(flops=flops, bytes_accessed=8 << 20, transcendentals=0)


def halves(late):
    return late // 2, late - late // 2


def columns(head):
    if isinstance(head, int):
        return pl.ds(head * HEAD_DIM, HEAD_DIM)
    return pl.ds(pl.multiple_of(head * HEAD_DIM, HEAD_DIM), HEAD_DIM)


def dot(a, b):
    return jnp.dot(a, b, preferred_element_type=jnp.float32)


def lists_kernel(planes, slots, where, kept, counts, sends, takes, choice):
    plane, pair = where[0], where[1] >> 1
    heads = kept.shape[1]
    shape = (planes * OWN, heads)
    half = (planes * OWN // 2, heads)
    ids = lax.broadcasted_iota(jnp.int32, shape, 0)
    chips = lax.broadcasted_iota(jnp.int32, half, 0)
    bit = jnp.left_shift(jnp.int32(1), lax.broadcasted_iota(jnp.int32, shape, 1))
    most = jnp.zeros((planes * OWN // 2, 1), jnp.int32)
    touched = jnp.zeros((1, 1), jnp.int32)
    taken = jnp.zeros(shape, jnp.int32)
    for t in range(planes):
        hits = jnp.zeros(shape, jnp.int32)
        per_chip = jnp.zeros(half, jnp.int32)
        for j in range(OWN, slots):
            tile = kept[t * slots + j : t * slots + j + 1, :]
            live = counts[t : t + 1, :] > j
            hits = jnp.where((ids == tile) & live, 1, hits)
            per_chip = per_chip + jnp.where((chips == (tile >> 1)) & live, 1, 0)
        most = jnp.maximum(most, jnp.sum(per_chip, axis=1, keepdims=True))
        for side in range(2):
            some = jnp.max(jnp.where(((ids >> 1) & 1) == side, hits, 0), axis=0, keepdims=True)
            touched = jnp.maximum(touched, jnp.sum(some, axis=1, keepdims=True))
        bits = hits * bit
        for turn in range(2):
            mine = jnp.sum(jnp.where(ids == 2 * pair + turn, bits, 0), axis=0, keepdims=True)
            row = jnp.broadcast_to(jnp.sum(mine, axis=1, keepdims=True), (1, HEAD_DIM))
            sends[2 * t + turn : 2 * t + turn + 1, :] = row
        taken = jnp.where(plane == t, bits, taken)
    takes[...] = jnp.broadcast_to(jnp.sum(taken, axis=1, keepdims=True), (planes * OWN, HEAD_DIM))
    top, wide = jnp.max(most), jnp.max(touched)
    index = jnp.int32(len(SIZES))
    for i, (room, late) in reversed(list(enumerate(SIZES))):
        index = jnp.where((top <= 2 * room) & (wide <= late), i, index)
    choice[0] = index


def pack_kernel(heads, planes, room, where, sends, k_ref, v_ref, mate_k, mate_v, *outs):
    plane, core = where[0], where[3]
    for step, out in enumerate(outs, 1):
        used = -core * room
        for turn in range(2):
            bits = sends[2 * lax.rem(plane + step, planes) + turn, 0]

            def look(head, used, out=out, bits=bits, turn=turn):
                hit = (bits >> head) & 1
                inside = (hit == 1) & (used >= 0) & (used < room)

                @pl.when(inside & (core == turn))
                def _():
                    out[used, 0] = k_ref[:, columns(head)].T
                    out[used, 1] = v_ref[:, columns(head)]

                @pl.when(inside & (core != turn))
                def _():
                    out[used, 0] = mate_k[:, columns(head)].T
                    out[used, 1] = mate_v[:, columns(head)]

                return used + hit

            used = lax.fori_loop(0, heads, look, used)


def plan_kernel(heads, planes, room, where, takes, pair, begin, order, far):
    plane, side, core = where[0], where[2], where[3]
    near, other = [], []
    for step in range(1, planes):
        source = lax.rem(plane - step + planes, planes) * OWN
        for turn in range(2):
            near.append(takes[source + 2 * side + turn, 0])
            other.append(takes[source + 2 * (1 - side) + turn, 0])
    any_near = functools.reduce(jnp.bitwise_or, near)
    any_other = functools.reduce(jnp.bitwise_or, other)

    def held(bits):
        return lax.fori_loop(0, heads, lambda h, n: n + ((bits >> h) & 1), jnp.int32(0))

    def put(head, state):
        a, b, c, d, pairs, *used = state
        none, far_none = 1 - ((any_near >> head) & 1), 1 - ((any_other >> head) & 1)
        at = jnp.where(none == 1, a, b)
        order[at] = head
        far[head] = jnp.where(far_none == 1, c, d)
        begin[head] = pairs
        for i, bits in enumerate(near):
            hit = (bits >> head) & 1
            sender = jnp.where(used[i] >= room, 1, 0)
            box = i // 2 * 2 + jnp.where(sender == core, 0, 1)

            @pl.when(hit == 1)
            def _(i=i, pairs=pairs, used=used, sender=sender, box=box):
                pair[pairs] = head * 4096 + box * room + used[i] - sender * room

            pairs = pairs + hit
            used = used[:i] + [used[i] + hit] + used[i + 1 :]
        return (a + none, b + 1 - none, c + far_none, d + 1 - far_none, pairs, *used)

    zero = jnp.int32(0)
    starts = [zero if i % 2 == 0 else held(near[i - 1]) for i in range(len(near))]
    first = (zero, heads - held(any_near), zero, heads - held(any_other), zero, *starts)
    begin[heads] = lax.fori_loop(0, heads, put, first)[4]


def soften(q, k_t, v):
    s = dot(q, k_t) * (1.0 / HEAD_DIM**0.5)
    m = jnp.max(s, axis=1, keepdims=True)
    w = jnp.exp(s - m)
    l = jnp.sum(w, axis=1, keepdims=True)
    return dot(w.astype(jnp.bfloat16), v) / l, m + jnp.log(l)


def here_kernel(heads, q_ref, k_ref, v_ref, mate_k, mate_v, out, lse_out, turned):
    lane = lax.broadcasted_iota(jnp.int32, lse_out.shape, 1)

    def attend(head, lse):
        at = columns(head)
        k_t = jnp.concatenate([k_ref[:, at].T, mate_k[:, at].T], axis=1)
        turned[head] = k_t
        v = jnp.concatenate([v_ref[:, at], mate_v[:, at]], axis=0)
        o, new = soften(q_ref[:, at], k_t, v)
        out[head] = o
        return jnp.where(lane == head, new, lse)

    lse_out[...] = lax.fori_loop(0, heads, attend, jnp.zeros(lse_out.shape, jnp.float32), unroll=4)


def far_kernel(start, order, lse_ref, q_ref, turned, v_ref, mate_v, *outs):
    *parts, lse_out = outs
    lane = lax.broadcasted_iota(jnp.int32, lse_out.shape, 1)
    lse = lse_ref[...]
    for part in parts:

        def attend(i, lse, part=part, start=start):
            head = order[start + i]
            at = columns(head)
            v = jnp.concatenate([v_ref[:, at], mate_v[:, at]], axis=0)
            o, new = soften(q_ref[:, at], turned[head], v)
            part[i] = o.astype(part.dtype)
            return jnp.where(lane == head, new, lse)

        lse = lax.fori_loop(0, part.shape[0], attend, lse, unroll=4)
        start += part.shape[0]
    lse_out[...] = lse


def late_kernel(sends, early, by_head, room, order, pair, begin, q_ref, o_ref, lse_ref, *rest):
    boxes, rest = rest[: sends], rest[sends:]
    *outs, lse_out, tiles, partial, level, sems = rest
    copies = [
        pltpu.make_async_copy(box, tiles.at[pl.ds(b * room, room)], sems.at[b]) for b, box in enumerate(boxes)
    ]
    for copy in copies:
        copy.start()
    heads = order.shape[0]
    shape = lse_out.shape
    most = partial.shape[0]
    lane = lax.broadcasted_iota(jnp.int32, shape, 1)
    total = begin[heads]
    for copy in copies:
        copy.wait()

    def four(i, carry):
        for j in range(4):
            at = jnp.minimum(4 * i + j, total - 1)
            code = pair[at]
            head, tile = code >> 12, code & 4095
            o, new = soften(q_ref[:, columns(head)], tiles[tile, 0], tiles[tile, 1])
            partial[at] = o
            level[at] = jnp.broadcast_to(new, shape)
        return carry

    lax.fori_loop(0, (total + 3) >> 2, four, 0)

    def join(i, lse, out, skip):
        head = order[early + skip + i]
        start, end = begin[head], begin[head + 1]
        base = jnp.sum(jnp.where(lane == head, lse_ref[...], 0.0), axis=1, keepdims=True)
        base = jnp.broadcast_to(base, shape)
        spots = [jnp.minimum(start + e, most - 1) for e in range(4)]
        levels = [jnp.where(start + e < end, level[p], -1e30) for e, p in enumerate(spots)]
        m = functools.reduce(jnp.maximum, levels, base)
        l = jnp.exp(base - m)
        o = l * o_ref[head if by_head else skip + i]
        for e, p in enumerate(spots):
            w = jnp.exp(levels[e] - m)
            l = l + w
            o = o + jnp.where(start + e < end, w * partial[p], 0.0)
        out[i] = (o / l).astype(out.dtype)
        return jnp.where(lane == head, m + jnp.log(l), lse)

    lse, skip = lse_ref[...], 0
    for out in outs:
        lse = lax.fori_loop(0, out.shape[0], functools.partial(join, out=out, skip=skip), lse, unroll=2)
        skip += out.shape[0]
    lse_out[...] = lse


def merge_kernel(heads, early, order, far, here, here_late, lse_here, lse_got, *rest):
    *got, out, mine, theirs, sems = rest
    copies = [pltpu.make_async_copy(here, mine, sems.at[0])]
    start = 0
    for i, part in enumerate(got):
        at = theirs.at[pl.ds(start, part.shape[0])]
        copies.append(pltpu.make_async_copy(part, at, sems.at[1 + i]))
        start += part.shape[0]
    for copy in copies:
        copy.start()
    a, b = lse_here[...], lse_got[...]
    m = jnp.maximum(a, b)
    wa, wb = jnp.exp(a - m), jnp.exp(b - m)
    total = wa + wb
    wa, wb = wa / total, wb / total
    for copy in copies:
        copy.wait()

    def put(i, carry):
        mine[order[early + i]] = here_late[i]
        return carry

    lax.fori_loop(0, heads - early, put, 0)
    for head in range(heads):
        joined = wa[:, head : head + 1] * mine[head]
        joined += wb[:, head : head + 1] * theirs[far[head]].astype(jnp.float32)
        out[:, columns(head)] = joined.astype(out.dtype)


def exchange(room, late, planes, queries, keys, values, mate_k, mate_v, sends, takes, where):
    rows, features = queries.shape
    heads = features // HEAD_DIM
    early = heads - late
    f32, bf16, i32 = jnp.float32, jnp.bfloat16, jnp.int32
    shape = jax.ShapeDtypeStruct
    tile = (rows, HEAD_DIM)
    count = planes * OWN
    across = [(d, d ^ 2) for d in range(count)]
    beside = [(d, d ^ 1) for d in range(count)]
    barrier = lax.optimization_barrier

    far_q = lax.ppermute(queries, "seq", across)
    packed = pl.pallas_call(
        functools.partial(pack_kernel, heads, planes, room),
        out_shape=[shape((room, 2) + tile, bf16)] * (planes - 1),
        in_specs=[SMEM] * 2 + [VMEM] * 4,
        out_specs=[VMEM] * (planes - 1),
        compiler_params=params(8 + room // 4),
        cost_estimate=cost(4 << 30),
        name="pack",
    )(where, sends, keys, values, mate_k, mate_v)
    landed = [
        lax.ppermute(packed[step - 1], "seq", [(d, (d + OWN * step) % count) for d in range(count)])
        for step in range(1, planes)
    ]

    where, takes, *packed = barrier((where, takes, *packed))
    most_pairs = min(4 * (planes - 1) * room, HEAD_DIM)
    pair, begin, order, far = pl.pallas_call(
        functools.partial(plan_kernel, heads, planes, room),
        out_shape=[shape((n,), i32) for n in (most_pairs, heads + 1, heads, heads)],
        in_specs=[SMEM] * 2,
        out_specs=[SMEM] * 4,
        compiler_params=params(4),
        cost_estimate=cost(4 << 30),
        name="plan",
    )(where, takes)
    here, lse_here, turned = pl.pallas_call(
        functools.partial(here_kernel, heads),
        out_shape=[shape((heads,) + tile, f32), shape(tile, f32), shape((heads, HEAD_DIM, 2 * rows), bf16)],
        in_specs=[VMEM] * 5,
        out_specs=[VMEM] * 3,
        compiler_params=params(14),
        cost_estimate=cost(1 << 30),
        name="here",
    )(queries, keys, values, mate_k, mate_v)

    def attend_far(order, lse, start, parts):
        return pl.pallas_call(
            functools.partial(far_kernel, start),
            out_shape=[shape((n,) + tile, kind) for n, kind in parts] + [shape(tile, f32)],
            in_specs=[SMEM] + [VMEM] * 5,
            out_specs=[VMEM] * (len(parts) + 1),
            compiler_params=params(12),
            cost_estimate=cost(1 << 30),
            name="far",
        )(order, lse, far_q, turned, values, mate_v)

    second = min(early, late // 2 + 2)
    parts = [n for n in (early - second, second) if n]
    lse_far, arrived = lse_here, []
    if early:
        *sent, lse_far = attend_far(order, lse_far, 0, [(n, bf16) for n in parts])
        arrived = [lax.ppermute(x, "seq", across) for x in sent]
    rest, lse_far = attend_far(order, lse_far, early, [(late, f32)])
    *landed, rest, lse_far, first = barrier((*landed, rest, lse_far, arrived[:-1]))
    arrived = first + arrived[len(first) :]
    boxes = []
    for got in landed:
        boxes += [got, lax.ppermute(got, "seq", beside)]

    def add_extras(q, o, lse, by_head, parts):
        return pl.pallas_call(
            functools.partial(late_kernel, len(boxes), early, by_head, room),
            out_shape=[shape((n,) + tile, kind) for n, kind in parts] + [shape(tile, f32)],
            in_specs=[SMEM] * 3 + [VMEM] * 3 + [HBM] * len(boxes),
            out_specs=[VMEM] * (len(parts) + 1),
            scratch_shapes=[
                pltpu.VMEM((len(boxes) * room, 2) + tile, bf16),
                pltpu.VMEM((most_pairs,) + tile, f32),
                pltpu.VMEM((most_pairs,) + tile, f32),
                pltpu.SemaphoreType.DMA((len(boxes),)),
            ],
            compiler_params=params(min(8 + 2 * room, 48)),
            cost_estimate=cost(1 << 20),
            name="late",
        )(order, pair, begin, q, o, lse, *boxes)

    *far_late, lse_far = add_extras(far_q, rest, lse_far, False, [(n, bf16) for n in halves(late)])
    arrived = [lax.ppermute(lse_far, "seq", across), *arrived] + [lax.ppermute(x, "seq", across) for x in far_late]
    here_late, lse_here = add_extras(queries, here, lse_here, True, [(late, f32)])

    return pl.pallas_call(
        functools.partial(merge_kernel, heads, early),
        out_shape=shape((rows, features), bf16),
        in_specs=[SMEM] * 2 + [HBM] + [VMEM] * 3 + [HBM] * (len(arrived) - 1),
        out_specs=VMEM,
        scratch_shapes=[
            pltpu.VMEM((heads,) + tile, f32),
            pltpu.VMEM((heads,) + tile, bf16),
            pltpu.SemaphoreType.DMA((5,)),
        ],
        compiler_params=params(12),
        cost_estimate=cost(1 << 20),
        name="merge",
    )(order, far, here, here_late, lse_here, *arrived)


def per_plane(queries, keys, values, kept, counts):
    heads, planes, slots = kept.shape
    device = lax.axis_index("seq").astype(jnp.int32)
    where = jnp.stack([device >> 2, device, (device >> 1) & 1, device & 1])
    beside = [(d, d ^ 1) for d in range(planes * OWN)]
    mate_k = lax.ppermute(keys, "seq", beside)
    mate_v = lax.ppermute(values, "seq", beside)
    shape = jax.ShapeDtypeStruct
    sends, takes, choice = pl.pallas_call(
        functools.partial(lists_kernel, planes, slots),
        out_shape=[
            shape((2 * planes, HEAD_DIM), jnp.int32),
            shape((planes * OWN, HEAD_DIM), jnp.int32),
            shape((1,), jnp.int32),
        ],
        in_specs=[SMEM] + [VMEM] * 2,
        out_specs=[VMEM] * 2 + [SMEM],
        compiler_params=params(4),
        name="lists",
    )(where, kept.transpose(1, 2, 0).reshape(planes * slots, heads), counts.T)
    sizes = SIZES + ((heads, heads),)
    return lax.switch(
        choice[0],
        [functools.partial(exchange, room, late, planes) for room, late in sizes],
        queries,
        keys,
        values,
        mate_k,
        mate_v,
        sends,
        takes,
        where,
    )


def attend_tile(query_tile, key_tiles, value_tiles, slot_list, live_count):
    row_count = query_tile.shape[0]
    factor = 1.0 / query_tile.shape[1] ** 0.5
    start_state = (
        jnp.full((row_count,), -1e30, jnp.float32),
        jnp.zeros((row_count,), jnp.float32),
        jnp.zeros((row_count, query_tile.shape[1]), jnp.float32),
    )

    def advance(block_num, state_now):
        running, totals, numerator = state_now
        first = (block_num * GROUP).astype(jnp.int32)
        chosen = lax.dynamic_slice_in_dim(slot_list, first, GROUP)
        key_block = key_tiles[chosen].reshape(GROUP * KTILE, query_tile.shape[1])
        value_block = value_tiles[chosen].reshape(GROUP * KTILE, query_tile.shape[1])
        scores = jnp.dot(query_tile, key_block.T, preferred_element_type=jnp.float32) * factor
        live_mask = jnp.repeat(first + jnp.arange(GROUP, dtype=jnp.int32) < live_count, KTILE)
        scores = jnp.where(live_mask[None, :], scores, -1e30)
        new_max = jnp.maximum(running, jnp.max(scores, axis=1))
        rescale = jnp.exp(running - new_max)
        weights = jnp.exp(scores - new_max[:, None])
        totals = totals * rescale + jnp.sum(weights, axis=1)
        numerator = numerator * rescale[:, None] + jnp.dot(
            weights.astype(jnp.bfloat16), value_block, preferred_element_type=jnp.float32
        )
        return (new_max, totals, numerator)

    block_total = (live_count + GROUP - 1) // GROUP
    running, totals, numerator = lax.fori_loop(jnp.int32(0), block_total, advance, start_state)
    return (numerator / totals[:, None]).astype(jnp.bfloat16)


def per_device(queries, keys, values, kept, counts):
    local_rows, feature_count = queries.shape
    shards = lax.axis_size("seq")
    device = lax.axis_index("seq")
    head_count = feature_count // HEAD_DIM
    replicas = max(1, shards // head_count)
    slots_here = max(1, head_count // shards)
    total_rows = local_rows * shards
    tile_count = counts.shape[1]
    stacked = jnp.stack([queries, keys, values])
    copied = jnp.broadcast_to(
        stacked.reshape(3, local_rows, head_count, 1, HEAD_DIM),
        (3, local_rows, head_count, replicas, HEAD_DIM),
    )
    copied = copied.reshape(3, local_rows, head_count * replicas, HEAD_DIM)
    arrived = lax.all_to_all(copied, "seq", split_axis=2, concat_axis=1, tiled=True)
    head_data = arrived.transpose(2, 0, 1, 3)
    tiles_each = tile_count // replicas
    results = []
    for j in range(slots_here):
        global_slot = device * slots_here + j
        head_id = global_slot // replicas
        replica_id = global_slot % replicas
        slot_rows = lax.dynamic_index_in_dim(kept, head_id, 0, keepdims=False)
        count_row = lax.dynamic_index_in_dim(counts, head_id, 0, keepdims=False)
        all_queries = head_data[j, 0]
        key_tiles = head_data[j, 1].reshape(total_rows // KTILE, KTILE, HEAD_DIM)
        value_tiles = head_data[j, 2].reshape(total_rows // KTILE, KTILE, HEAD_DIM)
        rounds = jnp.arange(tiles_each, dtype=jnp.int32)
        tile_ids = replica_id * tiles_each + rounds

        def process(i, output):
            tile_id = tile_ids[i]
            query_tile = lax.dynamic_slice_in_dim(all_queries, tile_id * QTILE, QTILE, 0)
            finished = attend_tile(
                query_tile, key_tiles, value_tiles, slot_rows[tile_id], count_row[tile_id]
            )
            return lax.dynamic_update_slice_in_dim(output, finished, tile_id * QTILE, 0)

        results.append(
            lax.fori_loop(0, tiles_each, process, jnp.zeros((total_rows, HEAD_DIM), jnp.bfloat16))
        )
    gathered = jnp.stack(results, axis=1)
    returned = lax.all_to_all(gathered, "seq", split_axis=0, concat_axis=1, tiled=True)
    combined = (
        returned.reshape(local_rows, head_count, replicas, HEAD_DIM).astype(jnp.float32).sum(axis=2)
    )
    return combined.astype(jnp.bfloat16).reshape(local_rows, feature_count)


def solution(mesh):
    by_rows = P(("groups", "seq"), None)
    placed = (by_rows, by_rows, by_rows, P("groups", None, None), P("groups", None))

    def step(queries, keys, values, kept, counts):
        heads, planes, slots = kept.shape
        one_tile_each = queries.shape[0] == KTILE and mesh.shape["seq"] == planes * OWN
        fits = heads <= 32 and heads * (slots - OWN) <= HEAD_DIM and planes == 4
        run = per_plane if one_tile_each and fits else per_device
        return run(queries, keys, values, kept, counts)

    return jax.shard_map(step, mesh=mesh, in_specs=placed, out_specs=by_rows, check_vma=False)
```

```python
import functools

import jax
import jax.numpy as jnp
from jax import lax
from jax.experimental import pallas as pl
from jax.experimental.pallas import tpu as pltpu
from jax.sharding import PartitionSpec as P

HEAD_DIM = 128
QTILE = 512
KTILE = 128
GROUP = 4
OWN = QTILE // KTILE
SIZES = ((5, 16), (6, 18), (7, 20))
MIB = 1 << 20
SMEM = pl.BlockSpec(memory_space=pltpu.SMEM)
VMEM = pl.BlockSpec(memory_space=pltpu.VMEM)
HBM = pl.BlockSpec(memory_space=pl.ANY)


def params(mib):
    return pltpu.CompilerParams(vmem_limit_bytes=mib * MIB)


def cost(flops):
    return pl.CostEstimate(flops=flops, bytes_accessed=8 << 20, transcendentals=0)


def halves(late):
    return late // 2, late - late // 2


def columns(head):
    if isinstance(head, int):
        return pl.ds(head * HEAD_DIM, HEAD_DIM)
    return pl.ds(pl.multiple_of(head * HEAD_DIM, HEAD_DIM), HEAD_DIM)


def dot(a, b):
    return jnp.dot(a, b, preferred_element_type=jnp.float32)


def lists_kernel(planes, slots, where, kept, counts, sends, takes, choice):
    plane, pair = where[0], where[1] >> 1
    heads = kept.shape[1]
    shape = (planes * OWN, heads)
    half = (planes * OWN // 2, heads)
    ids = lax.broadcasted_iota(jnp.int32, shape, 0)
    chips = lax.broadcasted_iota(jnp.int32, half, 0)
    bit = jnp.left_shift(jnp.int32(1), lax.broadcasted_iota(jnp.int32, shape, 1))
    lane = lax.broadcasted_iota(jnp.int32, (1, HEAD_DIM), 1)
    most = jnp.zeros((planes * OWN // 2, 1), jnp.int32)
    touched = jnp.zeros((1, 1), jnp.int32)
    taken = jnp.zeros(shape, jnp.int32)
    for t in range(planes):
        hits = jnp.zeros(shape, jnp.int32)
        per_chip = jnp.zeros(half, jnp.int32)
        for j in range(OWN, slots):
            tile = kept[t * slots + j : t * slots + j + 1, :]
            live = counts[t : t + 1, :] > j
            hits = jnp.where((ids == tile) & live, 1, hits)
            per_chip = per_chip + jnp.where((chips == (tile >> 1)) & live, 1, 0)
        most = jnp.maximum(most, jnp.sum(per_chip, axis=1, keepdims=True))
        for side in range(2):
            some = jnp.max(jnp.where(((ids >> 1) & 1) == side, hits, 0), axis=0, keepdims=True)
            touched = jnp.maximum(touched, jnp.sum(some, axis=1, keepdims=True))
        bits = hits * bit
        for turn in range(2):
            mine = [jnp.sum(jnp.where(ids == 2 * pair + turn, x, 0), axis=0, keepdims=True) for x in (bits, hits)]
            word, count = [jnp.sum(x, axis=1, keepdims=True) for x in mine]
            sends[2 * t + turn : 2 * t + turn + 1, :] = jnp.where(lane == 0, word, count)
        taken = jnp.where(plane == t, bits, taken)
    takes[...] = jnp.where(
        lane == 0,
        jnp.sum(taken, axis=1, keepdims=True),
        jnp.sum(jnp.where(taken != 0, 1, 0), axis=1, keepdims=True),
    )
    top, wide = jnp.max(most), jnp.max(touched)
    index = jnp.int32(len(SIZES))
    for i, (room, late) in reversed(list(enumerate(SIZES))):
        index = jnp.where((top <= 2 * room) & (wide <= late), i, index)
    choice[0] = index


def pack_kernel(heads, planes, room, where, sends, k_ref, v_ref, mate_k, mate_v, *outs):
    plane, core = where[0], where[3]
    rows = [(out, 2 * lax.rem(plane + step, planes)) for step, out in enumerate(outs, 1)]
    bits = [sends[row + turn, 0] for _, row in rows for turn in range(2)]
    begins = [at - core * room for _, row in rows for at in (0, sends[row, 1])]

    def look(head, used):
        for i, (start, held) in enumerate(zip(used, bits)):
            out, turn = outs[i // 2], i % 2
            inside = (((held >> head) & 1) == 1) & (start >= 0) & (start < room)

            @pl.when(inside & (core == turn))
            def _(out=out, start=start):
                out[start, 0] = k_ref[:, columns(head)].T
                out[start, 1] = v_ref[:, columns(head)]

            @pl.when(inside & (core != turn))
            def _(out=out, start=start):
                out[start, 0] = mate_k[:, columns(head)].T
                out[start, 1] = mate_v[:, columns(head)]

        return tuple(start + ((held >> head) & 1) for start, held in zip(used, bits))

    lax.fori_loop(0, heads, look, tuple(begins))


def plan_kernel(heads, planes, room, where, takes, pair, begin, order, far):
    plane, side, core = where[0], where[2], where[3]
    near, other, starts = [], [], []
    for step in range(1, planes):
        source = lax.rem(plane - step + planes, planes) * OWN
        for turn in range(2):
            near.append(takes[source + 2 * side + turn, 0])
            starts.append(takes[source + 2 * side, 1] if turn else jnp.int32(0))
            other.append(takes[source + 2 * (1 - side) + turn, 0])
    any_near = functools.reduce(jnp.bitwise_or, near)
    any_other = functools.reduce(jnp.bitwise_or, other)

    def held(bits):
        return lax.fori_loop(0, heads, lambda h, n: n + ((bits >> h) & 1), jnp.int32(0))

    def put(head, state):
        a, b, c, d, pairs, *used = state
        none, far_none = 1 - ((any_near >> head) & 1), 1 - ((any_other >> head) & 1)
        at = jnp.where(none == 1, a, b)
        order[at] = head
        far[head] = jnp.where(far_none == 1, c, d)
        begin[head] = pairs
        for i, bits in enumerate(near):
            hit = (bits >> head) & 1
            sender = jnp.where(used[i] >= room, 1, 0)
            box = i // 2 * 2 + jnp.where(sender == core, 0, 1)

            @pl.when(hit == 1)
            def _(i=i, pairs=pairs, used=used, sender=sender, box=box):
                pair[pairs] = head * 4096 + box * room + used[i] - sender * room

            pairs = pairs + hit
            used = used[:i] + [used[i] + hit] + used[i + 1 :]
        return (a + none, b + 1 - none, c + far_none, d + 1 - far_none, pairs, *used)

    zero = jnp.int32(0)
    first = (zero, heads - held(any_near), zero, heads - held(any_other), zero, *starts)
    begin[heads] = lax.fori_loop(0, heads, put, first)[4]


def soften(q, k_t, v):
    s = dot(q, k_t) * (1.0 / HEAD_DIM**0.5)
    m = jnp.max(s, axis=1, keepdims=True)
    w = jnp.exp(s - m)
    l = jnp.sum(w, axis=1, keepdims=True)
    return dot(w.astype(jnp.bfloat16), v) / l, m + jnp.log(l)


def here_kernel(heads, q_ref, k_ref, v_ref, mate_k, mate_v, out, lse_out, turned):
    lane = lax.broadcasted_iota(jnp.int32, lse_out.shape, 1)

    def attend(head, lse):
        at = columns(head)
        k_t = jnp.concatenate([k_ref[:, at].T, mate_k[:, at].T], axis=1)
        turned[head] = k_t
        v = jnp.concatenate([v_ref[:, at], mate_v[:, at]], axis=0)
        o, new = soften(q_ref[:, at], k_t, v)
        out[head] = o
        return jnp.where(lane == head, new, lse)

    lse_out[...] = lax.fori_loop(0, heads, attend, jnp.zeros(lse_out.shape, jnp.float32), unroll=4)


def far_kernel(start, order, lse_ref, q_ref, turned, v_ref, mate_v, *outs):
    *parts, lse_out = outs
    lane = lax.broadcasted_iota(jnp.int32, lse_out.shape, 1)
    lse = lse_ref[...]
    for part in parts:

        def attend(i, lse, part=part, start=start):
            head = order[start + i]
            at = columns(head)
            v = jnp.concatenate([v_ref[:, at], mate_v[:, at]], axis=0)
            o, new = soften(q_ref[:, at], turned[head], v)
            part[i] = o.astype(part.dtype)
            return jnp.where(lane == head, new, lse)

        lse = lax.fori_loop(0, part.shape[0], attend, lse, unroll=4)
        start += part.shape[0]
    lse_out[...] = lse


def late_kernel(sends, early, by_head, room, order, pair, begin, q_ref, o_ref, lse_ref, *rest):
    boxes, rest = rest[: sends], rest[sends:]
    *outs, lse_out, tiles, partial, level, sems = rest
    copies = [
        pltpu.make_async_copy(box, tiles.at[pl.ds(b * room, room)], sems.at[b]) for b, box in enumerate(boxes)
    ]
    for copy in copies:
        copy.start()
    heads = order.shape[0]
    shape = lse_out.shape
    most = partial.shape[0]
    lane = lax.broadcasted_iota(jnp.int32, shape, 1)
    total = begin[heads]
    for copy in copies:
        copy.wait()

    def four(i, carry):
        for j in range(4):
            at = jnp.minimum(4 * i + j, total - 1)
            code = pair[at]
            head, tile = code >> 12, code & 4095
            o, new = soften(q_ref[:, columns(head)], tiles[tile, 0], tiles[tile, 1])
            partial[at] = o
            level[at] = jnp.broadcast_to(new, shape)
        return carry

    lax.fori_loop(0, (total + 3) >> 2, four, 0)

    def join(i, lse, out, skip):
        head = order[early + skip + i]
        start, end = begin[head], begin[head + 1]
        base = jnp.sum(jnp.where(lane == head, lse_ref[...], 0.0), axis=1, keepdims=True)
        base = jnp.broadcast_to(base, shape)
        spots = [jnp.minimum(start + e, most - 1) for e in range(4)]
        levels = [jnp.where(start + e < end, level[p], -1e30) for e, p in enumerate(spots)]
        m = functools.reduce(jnp.maximum, levels, base)
        l = jnp.exp(base - m)
        o = l * o_ref[head if by_head else skip + i]
        for e, p in enumerate(spots):
            w = jnp.exp(levels[e] - m)
            l = l + w
            o = o + jnp.where(start + e < end, w * partial[p], 0.0)
        out[i] = (o / l).astype(out.dtype)
        return jnp.where(lane == head, m + jnp.log(l), lse)

    lse, skip = lse_ref[...], 0
    for out in outs:
        lse = lax.fori_loop(0, out.shape[0], functools.partial(join, out=out, skip=skip), lse, unroll=2)
        skip += out.shape[0]
    lse_out[...] = lse


def merge_kernel(heads, early, order, far, here, here_late, lse_here, lse_got, *rest):
    *got, result, mine, theirs, out, sems, out_sems = rest
    copies = [pltpu.make_async_copy(here, mine, sems.at[0])]
    start = 0
    for i, part in enumerate(got):
        at = theirs.at[pl.ds(start, part.shape[0])]
        copies.append(pltpu.make_async_copy(part, at, sems.at[1 + i]))
        start += part.shape[0]
    for copy in copies:
        copy.start()
    a, b = lse_here[...], lse_got[...]
    m = jnp.maximum(a, b)
    wa, wb = jnp.exp(a - m), jnp.exp(b - m)
    total = wa + wb
    wa, wb = wa / total, wb / total
    for copy in copies:
        copy.wait()

    def put(i, carry):
        mine[order[early + i]] = here_late[i]
        return carry

    lax.fori_loop(0, heads - early, put, 0)
    leaving = []
    for head in range(heads):
        joined = wa[:, head : head + 1] * mine[head]
        joined += wb[:, head : head + 1] * theirs[far[head]].astype(jnp.float32)
        out[:, columns(head)] = joined.astype(out.dtype)
        if head % 8 == 7:
            at = pl.ds((head - 7) * HEAD_DIM, 8 * HEAD_DIM)
            leaving.append(pltpu.make_async_copy(out.at[:, at], result.at[:, at], out_sems.at[head // 8]))
            leaving[-1].start()
    for copy in leaving:
        copy.wait()


def exchange(room, late, planes, queries, keys, values, mate_k, mate_v, sends, takes, where):
    rows, features = queries.shape
    heads = features // HEAD_DIM
    early = heads - late
    f32, bf16, i32 = jnp.float32, jnp.bfloat16, jnp.int32
    shape = jax.ShapeDtypeStruct
    tile = (rows, HEAD_DIM)
    count = planes * OWN
    across = [(d, d ^ 2) for d in range(count)]
    beside = [(d, d ^ 1) for d in range(count)]
    barrier = lax.optimization_barrier

    far_q = lax.ppermute(queries, "seq", across)
    packed = pl.pallas_call(
        functools.partial(pack_kernel, heads, planes, room),
        out_shape=[shape((room, 2) + tile, bf16)] * (planes - 1),
        in_specs=[SMEM] * 2 + [VMEM] * 4,
        out_specs=[VMEM] * (planes - 1),
        compiler_params=params(8 + room // 4),
        cost_estimate=cost(4 << 30),
        name="pack",
    )(where, sends, keys, values, mate_k, mate_v)
    landed = [
        lax.ppermute(packed[step - 1], "seq", [(d, (d + OWN * step) % count) for d in range(count)])
        for step in range(1, planes)
    ]

    where, takes, *packed = barrier((where, takes, *packed))
    most_pairs = min(4 * (planes - 1) * room, HEAD_DIM)
    pair, begin, order, far = pl.pallas_call(
        functools.partial(plan_kernel, heads, planes, room),
        out_shape=[shape((n,), i32) for n in (most_pairs, heads + 1, heads, heads)],
        in_specs=[SMEM] * 2,
        out_specs=[SMEM] * 4,
        compiler_params=params(4),
        cost_estimate=cost(4 << 30),
        name="plan",
    )(where, takes)
    here, lse_here, turned = pl.pallas_call(
        functools.partial(here_kernel, heads),
        out_shape=[shape((heads,) + tile, f32), shape(tile, f32), shape((heads, HEAD_DIM, 2 * rows), bf16)],
        in_specs=[VMEM] * 5,
        out_specs=[VMEM] * 3,
        compiler_params=params(14),
        cost_estimate=cost(1 << 30),
        name="here",
    )(queries, keys, values, mate_k, mate_v)

    def attend_far(order, lse, start, parts):
        return pl.pallas_call(
            functools.partial(far_kernel, start),
            out_shape=[shape((n,) + tile, kind) for n, kind in parts] + [shape(tile, f32)],
            in_specs=[SMEM] + [VMEM] * 5,
            out_specs=[VMEM] * (len(parts) + 1),
            compiler_params=params(12),
            cost_estimate=cost(1 << 30),
            name="far",
        )(order, lse, far_q, turned, values, mate_v)

    second = min(early, late // 2 + 2)
    parts = [n for n in (early - second, second) if n]
    lse_far, arrived = lse_here, []
    if early:
        sent, lse_far = attend_far(order, lse_far, 0, [(parts[0], bf16)])
        arrived = [lax.ppermute(sent, "seq", across)]
    kinds = [(n, bf16) for n in parts[1:]] + [(late, f32)]
    *sent, rest, lse_far = attend_far(order, lse_far, early - sum(parts[1:]), kinds)
    arrived += [lax.ppermute(x, "seq", across) for x in sent]
    *landed, rest, lse_far, first = barrier((*landed, rest, lse_far, arrived[:-1]))
    arrived = first + arrived[len(first) :]
    boxes = []
    for got in landed:
        boxes += [got, lax.ppermute(got, "seq", beside)]

    def add_extras(q, o, lse, by_head, parts):
        return pl.pallas_call(
            functools.partial(late_kernel, len(boxes), early, by_head, room),
            out_shape=[shape((n,) + tile, kind) for n, kind in parts] + [shape(tile, f32)],
            in_specs=[SMEM] * 3 + [VMEM] * 3 + [HBM] * len(boxes),
            out_specs=[VMEM] * (len(parts) + 1),
            scratch_shapes=[
                pltpu.VMEM((len(boxes) * room, 2) + tile, bf16),
                pltpu.VMEM((most_pairs,) + tile, f32),
                pltpu.VMEM((most_pairs,) + tile, f32),
                pltpu.SemaphoreType.DMA((len(boxes),)),
            ],
            compiler_params=params(min(8 + 2 * room, 48)),
            cost_estimate=cost(1 << 20),
            name="late",
        )(order, pair, begin, q, o, lse, *boxes)

    *far_late, lse_far = add_extras(far_q, rest, lse_far, False, [(n, bf16) for n in halves(late)])
    arrived = [lax.ppermute(lse_far, "seq", across), *arrived] + [lax.ppermute(x, "seq", across) for x in far_late]
    here_late, lse_here = add_extras(queries, here, lse_here, True, [(late, f32)])

    return pl.pallas_call(
        functools.partial(merge_kernel, heads, early),
        out_shape=shape((rows, features), bf16),
        in_specs=[SMEM] * 2 + [HBM] + [VMEM] * 3 + [HBM] * (len(arrived) - 1),
        out_specs=pl.BlockSpec(memory_space=pltpu.HBM),
        scratch_shapes=[
            pltpu.VMEM((heads,) + tile, f32),
            pltpu.VMEM((heads,) + tile, bf16),
            pltpu.VMEM((rows, features), bf16),
            pltpu.SemaphoreType.DMA((5,)),
            pltpu.SemaphoreType.DMA((heads // 8,)),
        ],
        compiler_params=params(12),
        cost_estimate=cost(1 << 20),
        name="merge",
    )(order, far, here, here_late, lse_here, *arrived)


def per_plane(queries, keys, values, kept, counts):
    heads, planes, slots = kept.shape
    device = lax.axis_index("seq").astype(jnp.int32)
    where = jnp.stack([device >> 2, device, (device >> 1) & 1, device & 1])
    beside = [(d, d ^ 1) for d in range(planes * OWN)]
    mate_k = lax.ppermute(keys, "seq", beside)
    mate_v = lax.ppermute(values, "seq", beside)
    shape = jax.ShapeDtypeStruct
    sends, takes, choice = pl.pallas_call(
        functools.partial(lists_kernel, planes, slots),
        out_shape=[
            shape((2 * planes, HEAD_DIM), jnp.int32),
            shape((planes * OWN, HEAD_DIM), jnp.int32),
            shape((1,), jnp.int32),
        ],
        in_specs=[SMEM] + [VMEM] * 2,
        out_specs=[VMEM] * 2 + [SMEM],
        compiler_params=params(60),
        name="lists",
    )(where, kept.transpose(1, 2, 0).reshape(planes * slots, heads), counts.T)
    sizes = SIZES + ((heads, heads),)
    return lax.switch(
        choice[0],
        [functools.partial(exchange, room, late, planes) for room, late in sizes],
        queries,
        keys,
        values,
        mate_k,
        mate_v,
        sends,
        takes,
        where,
    )


def attend_tile(query_tile, key_tiles, value_tiles, slot_list, live_count):
    row_count = query_tile.shape[0]
    factor = 1.0 / query_tile.shape[1] ** 0.5
    start_state = (
        jnp.full((row_count,), -1e30, jnp.float32),
        jnp.zeros((row_count,), jnp.float32),
        jnp.zeros((row_count, query_tile.shape[1]), jnp.float32),
    )

    def advance(block_num, state_now):
        running, totals, numerator = state_now
        first = (block_num * GROUP).astype(jnp.int32)
        chosen = lax.dynamic_slice_in_dim(slot_list, first, GROUP)
        key_block = key_tiles[chosen].reshape(GROUP * KTILE, query_tile.shape[1])
        value_block = value_tiles[chosen].reshape(GROUP * KTILE, query_tile.shape[1])
        scores = jnp.dot(query_tile, key_block.T, preferred_element_type=jnp.float32) * factor
        live_mask = jnp.repeat(first + jnp.arange(GROUP, dtype=jnp.int32) < live_count, KTILE)
        scores = jnp.where(live_mask[None, :], scores, -1e30)
        new_max = jnp.maximum(running, jnp.max(scores, axis=1))
        rescale = jnp.exp(running - new_max)
        weights = jnp.exp(scores - new_max[:, None])
        totals = totals * rescale + jnp.sum(weights, axis=1)
        numerator = numerator * rescale[:, None] + jnp.dot(
            weights.astype(jnp.bfloat16), value_block, preferred_element_type=jnp.float32
        )
        return (new_max, totals, numerator)

    block_total = (live_count + GROUP - 1) // GROUP
    running, totals, numerator = lax.fori_loop(jnp.int32(0), block_total, advance, start_state)
    return (numerator / totals[:, None]).astype(jnp.bfloat16)


def per_device(queries, keys, values, kept, counts):
    local_rows, feature_count = queries.shape
    shards = lax.axis_size("seq")
    device = lax.axis_index("seq")
    head_count = feature_count // HEAD_DIM
    replicas = max(1, shards // head_count)
    slots_here = max(1, head_count // shards)
    total_rows = local_rows * shards
    tile_count = counts.shape[1]
    stacked = jnp.stack([queries, keys, values])
    copied = jnp.broadcast_to(
        stacked.reshape(3, local_rows, head_count, 1, HEAD_DIM),
        (3, local_rows, head_count, replicas, HEAD_DIM),
    )
    copied = copied.reshape(3, local_rows, head_count * replicas, HEAD_DIM)
    arrived = lax.all_to_all(copied, "seq", split_axis=2, concat_axis=1, tiled=True)
    head_data = arrived.transpose(2, 0, 1, 3)
    tiles_each = tile_count // replicas
    results = []
    for j in range(slots_here):
        global_slot = device * slots_here + j
        head_id = global_slot // replicas
        replica_id = global_slot % replicas
        slot_rows = lax.dynamic_index_in_dim(kept, head_id, 0, keepdims=False)
        count_row = lax.dynamic_index_in_dim(counts, head_id, 0, keepdims=False)
        all_queries = head_data[j, 0]
        key_tiles = head_data[j, 1].reshape(total_rows // KTILE, KTILE, HEAD_DIM)
        value_tiles = head_data[j, 2].reshape(total_rows // KTILE, KTILE, HEAD_DIM)
        rounds = jnp.arange(tiles_each, dtype=jnp.int32)
        tile_ids = replica_id * tiles_each + rounds

        def process(i, output):
            tile_id = tile_ids[i]
            query_tile = lax.dynamic_slice_in_dim(all_queries, tile_id * QTILE, QTILE, 0)
            finished = attend_tile(
                query_tile, key_tiles, value_tiles, slot_rows[tile_id], count_row[tile_id]
            )
            return lax.dynamic_update_slice_in_dim(output, finished, tile_id * QTILE, 0)

        results.append(
            lax.fori_loop(0, tiles_each, process, jnp.zeros((total_rows, HEAD_DIM), jnp.bfloat16))
        )
    gathered = jnp.stack(results, axis=1)
    returned = lax.all_to_all(gathered, "seq", split_axis=0, concat_axis=1, tiled=True)
    combined = (
        returned.reshape(local_rows, head_count, replicas, HEAD_DIM).astype(jnp.float32).sum(axis=2)
    )
    return combined.astype(jnp.bfloat16).reshape(local_rows, feature_count)


def solution(mesh):
    by_rows = P(("groups", "seq"), None)
    placed = (by_rows, by_rows, by_rows, P("groups", None, None), P("groups", None))

    def step(queries, keys, values, kept, counts):
        heads, planes, slots = kept.shape
        one_tile_each = queries.shape[0] == KTILE and mesh.shape["seq"] == planes * OWN
        fits = heads % 8 == 0 and heads <= 32 and heads * (slots - OWN) <= HEAD_DIM and planes == 4
        run = per_plane if one_tile_each and fits else per_device
        return run(queries, keys, values, kept, counts)

    return jax.shard_map(step, mesh=mesh, in_specs=placed, out_specs=by_rows, check_vma=False)
```

```python
import functools

import jax
import jax.numpy as jnp
from jax import lax
from jax.experimental import pallas as pl
from jax.experimental.pallas import tpu as pltpu
from jax.sharding import PartitionSpec as P

HEAD_DIM = 128
QTILE = 512
KTILE = 128
GROUP = 4
OWN = QTILE // KTILE
SIZES = ((5, 16), (6, 18), (7, 20))
MIB = 1 << 20
SMEM = pl.BlockSpec(memory_space=pltpu.SMEM)
VMEM = pl.BlockSpec(memory_space=pltpu.VMEM)
HBM = pl.BlockSpec(memory_space=pl.ANY)


def params(mib):
    return pltpu.CompilerParams(vmem_limit_bytes=mib * MIB)


def cost(flops):
    return pl.CostEstimate(flops=flops, bytes_accessed=8 << 20, transcendentals=0)


def thirds(late):
    return late // 3, late // 3, late - 2 * (late // 3)


def columns(head):
    if isinstance(head, int):
        return pl.ds(head * HEAD_DIM, HEAD_DIM)
    return pl.ds(pl.multiple_of(head * HEAD_DIM, HEAD_DIM), HEAD_DIM)


def dot(a, b):
    return jnp.dot(a, b, preferred_element_type=jnp.float32)


def lists_kernel(planes, slots, where, kept, counts, sends, takes, choice):
    plane, pair = where[0], where[1] >> 1
    heads = kept.shape[1]
    shape = (planes * OWN, heads)
    half = (planes * OWN // 2, heads)
    ids = lax.broadcasted_iota(jnp.int32, shape, 0)
    chips = lax.broadcasted_iota(jnp.int32, half, 0)
    bit = jnp.left_shift(jnp.int32(1), lax.broadcasted_iota(jnp.int32, shape, 1))
    lane = lax.broadcasted_iota(jnp.int32, (1, HEAD_DIM), 1)
    most = jnp.zeros((planes * OWN // 2, 1), jnp.int32)
    touched = jnp.zeros((1, 1), jnp.int32)
    taken = jnp.zeros(shape, jnp.int32)
    for t in range(planes):
        hits = jnp.zeros(shape, jnp.int32)
        per_chip = jnp.zeros(half, jnp.int32)
        for j in range(OWN, slots):
            tile = kept[t * slots + j : t * slots + j + 1, :]
            live = counts[t : t + 1, :] > j
            hits = jnp.where((ids == tile) & live, 1, hits)
            per_chip = per_chip + jnp.where((chips == (tile >> 1)) & live, 1, 0)
        most = jnp.maximum(most, jnp.sum(per_chip, axis=1, keepdims=True))
        for side in range(2):
            some = jnp.max(jnp.where(((ids >> 1) & 1) == side, hits, 0), axis=0, keepdims=True)
            touched = jnp.maximum(touched, jnp.sum(some, axis=1, keepdims=True))
        bits = hits * bit
        for turn in range(2):
            mine = [jnp.sum(jnp.where(ids == 2 * pair + turn, x, 0), axis=0, keepdims=True) for x in (bits, hits)]
            word, count = [jnp.sum(x, axis=1, keepdims=True) for x in mine]
            sends[2 * t + turn : 2 * t + turn + 1, :] = jnp.where(lane == 0, word, count)
        taken = jnp.where(plane == t, bits, taken)
    takes[...] = jnp.where(
        lane == 0,
        jnp.sum(taken, axis=1, keepdims=True),
        jnp.sum(jnp.where(taken != 0, 1, 0), axis=1, keepdims=True),
    )
    top, wide = jnp.max(most), jnp.max(touched)
    index = jnp.int32(len(SIZES))
    for i, (room, late) in reversed(list(enumerate(SIZES))):
        index = jnp.where((top <= 2 * room) & (wide <= late), i, index)
    choice[0] = index


def pack_kernel(heads, planes, room, where, sends, k_ref, v_ref, mate_k, mate_v, *outs):
    plane, core = where[0], where[3]
    rows = [(out, 2 * lax.rem(plane + step, planes)) for step, out in enumerate(outs, 1)]
    bits = [sends[row + turn, 0] for _, row in rows for turn in range(2)]
    begins = [at - core * room for _, row in rows for at in (0, sends[row, 1])]

    def look(head, used):
        for i, (start, held) in enumerate(zip(used, bits)):
            out, turn = outs[i // 2], i % 2
            inside = (((held >> head) & 1) == 1) & (start >= 0) & (start < room)

            @pl.when(inside & (core == turn))
            def _(out=out, start=start):
                out[start, 0] = k_ref[:, columns(head)].T
                out[start, 1] = v_ref[:, columns(head)]

            @pl.when(inside & (core != turn))
            def _(out=out, start=start):
                out[start, 0] = mate_k[:, columns(head)].T
                out[start, 1] = mate_v[:, columns(head)]

        return tuple(start + ((held >> head) & 1) for start, held in zip(used, bits))

    lax.fori_loop(0, heads, look, tuple(begins))


def plan_kernel(heads, planes, room, where, takes, pair, begin, order, far):
    plane, side, core = where[0], where[2], where[3]
    near, other, starts = [], [], []
    for step in range(1, planes):
        source = lax.rem(plane - step + planes, planes) * OWN
        for turn in range(2):
            near.append(takes[source + 2 * side + turn, 0])
            starts.append(takes[source + 2 * side, 1] if turn else jnp.int32(0))
            other.append(takes[source + 2 * (1 - side) + turn, 0])
    any_near = functools.reduce(jnp.bitwise_or, near)
    any_other = functools.reduce(jnp.bitwise_or, other)

    def held(bits):
        return lax.fori_loop(0, heads, lambda h, n: n + ((bits >> h) & 1), jnp.int32(0))

    def put(head, state):
        a, b, c, d, pairs, *used = state
        none, far_none = 1 - ((any_near >> head) & 1), 1 - ((any_other >> head) & 1)
        at = jnp.where(none == 1, a, b)
        order[at] = head
        far[head] = jnp.where(far_none == 1, c, d)
        begin[head] = pairs
        for i, bits in enumerate(near):
            hit = (bits >> head) & 1
            sender = jnp.where(used[i] >= room, 1, 0)
            box = i // 2 * 2 + jnp.where(sender == core, 0, 1)

            @pl.when(hit == 1)
            def _(i=i, pairs=pairs, used=used, sender=sender, box=box):
                pair[pairs] = head * 4096 + box * room + used[i] - sender * room

            pairs = pairs + hit
            used = used[:i] + [used[i] + hit] + used[i + 1 :]
        return (a + none, b + 1 - none, c + far_none, d + 1 - far_none, pairs, *used)

    zero = jnp.int32(0)
    first = (zero, heads - held(any_near), zero, heads - held(any_other), zero, *starts)
    begin[heads] = lax.fori_loop(0, heads, put, first)[4]


def soften(q, k_t, v):
    s = dot(q, k_t) * (1.0 / HEAD_DIM**0.5)
    m = jnp.max(s, axis=1, keepdims=True)
    w = jnp.exp(s - m)
    l = jnp.sum(w, axis=1, keepdims=True)
    return dot(w.astype(jnp.bfloat16), v) / l, m + jnp.log(l)


def here_kernel(heads, q_ref, k_ref, v_ref, mate_k, mate_v, out, lse_out, turned):
    lane = lax.broadcasted_iota(jnp.int32, lse_out.shape, 1)

    def attend(head, lse):
        at = columns(head)
        k_t = jnp.concatenate([k_ref[:, at].T, mate_k[:, at].T], axis=1)
        turned[head] = k_t
        v = jnp.concatenate([v_ref[:, at], mate_v[:, at]], axis=0)
        o, new = soften(q_ref[:, at], k_t, v)
        out[head] = o
        return jnp.where(lane == head, new, lse)

    lse_out[...] = lax.fori_loop(0, heads, attend, jnp.zeros(lse_out.shape, jnp.float32), unroll=4)


def far_kernel(start, order, lse_ref, q_ref, turned, v_ref, mate_v, *outs):
    *parts, lse_out = outs
    lane = lax.broadcasted_iota(jnp.int32, lse_out.shape, 1)
    lse = lse_ref[...]
    for part in parts:

        def attend(i, lse, part=part, start=start):
            head = order[start + i]
            at = columns(head)
            v = jnp.concatenate([v_ref[:, at], mate_v[:, at]], axis=0)
            o, new = soften(q_ref[:, at], turned[head], v)
            part[i] = o.astype(part.dtype)
            return jnp.where(lane == head, new, lse)

        lse = lax.fori_loop(0, part.shape[0], attend, lse, unroll=4)
        start += part.shape[0]
    lse_out[...] = lse


def late_kernel(sends, early, by_head, room, order, pair, begin, q_ref, o_ref, lse_ref, *rest):
    boxes, rest = rest[: sends], rest[sends:]
    *outs, lse_out, tiles, partial, level, sems = rest
    copies = [
        pltpu.make_async_copy(box, tiles.at[pl.ds(b * room, room)], sems.at[b]) for b, box in enumerate(boxes)
    ]
    for copy in copies:
        copy.start()
    heads = order.shape[0]
    shape = lse_out.shape
    most = partial.shape[0]
    lane = lax.broadcasted_iota(jnp.int32, shape, 1)
    total = begin[heads]
    for copy in copies:
        copy.wait()

    def four(i, carry):
        for j in range(4):
            at = jnp.minimum(4 * i + j, total - 1)
            code = pair[at]
            head, tile = code >> 12, code & 4095
            o, new = soften(q_ref[:, columns(head)], tiles[tile, 0], tiles[tile, 1])
            partial[at] = o
            level[at] = jnp.broadcast_to(new, shape)
        return carry

    lax.fori_loop(0, (total + 3) >> 2, four, 0)

    def join(i, lse, out, skip):
        head = order[early + skip + i]
        start, end = begin[head], begin[head + 1]
        base = jnp.sum(jnp.where(lane == head, lse_ref[...], 0.0), axis=1, keepdims=True)
        base = jnp.broadcast_to(base, shape)
        spots = [jnp.minimum(start + e, most - 1) for e in range(4)]
        levels = [jnp.where(start + e < end, level[p], -1e30) for e, p in enumerate(spots)]
        m = functools.reduce(jnp.maximum, levels, base)
        l = jnp.exp(base - m)
        o = l * o_ref[head if by_head else skip + i]
        for e, p in enumerate(spots):
            w = jnp.exp(levels[e] - m)
            l = l + w
            o = o + jnp.where(start + e < end, w * partial[p], 0.0)
        out[i] = (o / l).astype(out.dtype)
        return jnp.where(lane == head, m + jnp.log(l), lse)

    lse, skip = lse_ref[...], 0
    for out in outs:
        lse = lax.fori_loop(0, out.shape[0], functools.partial(join, out=out, skip=skip), lse, unroll=2)
        skip += out.shape[0]
    lse_out[...] = lse


def merge_kernel(heads, early, order, far, here, here_late, lse_here, lse_got, *rest):
    *got, result, mine, theirs, out, sems, out_sems = rest
    copies = [pltpu.make_async_copy(here, mine, sems.at[0])]
    start = 0
    for i, part in enumerate(got):
        at = theirs.at[pl.ds(start, part.shape[0])]
        copies.append(pltpu.make_async_copy(part, at, sems.at[1 + i]))
        start += part.shape[0]
    for copy in copies:
        copy.start()
    a, b = lse_here[...], lse_got[...]
    m = jnp.maximum(a, b)
    wa, wb = jnp.exp(a - m), jnp.exp(b - m)
    total = wa + wb
    wa, wb = wa / total, wb / total
    for copy in copies:
        copy.wait()

    def put(i, carry):
        mine[order[early + i]] = here_late[i]
        return carry

    lax.fori_loop(0, heads - early, put, 0)
    leaving = []
    for head in range(heads):
        joined = wa[:, head : head + 1] * mine[head]
        joined += wb[:, head : head + 1] * theirs[far[head]].astype(jnp.float32)
        out[:, columns(head)] = joined.astype(out.dtype)
        if head % 8 == 7:
            at = pl.ds((head - 7) * HEAD_DIM, 8 * HEAD_DIM)
            leaving.append(pltpu.make_async_copy(out.at[:, at], result.at[:, at], out_sems.at[head // 8]))
            leaving[-1].start()
    for copy in leaving:
        copy.wait()


def exchange(room, late, planes, queries, keys, values, mate_k, sends, takes, where):
    rows, features = queries.shape
    heads = features // HEAD_DIM
    early = heads - late
    f32, bf16, i32 = jnp.float32, jnp.bfloat16, jnp.int32
    shape = jax.ShapeDtypeStruct
    tile = (rows, HEAD_DIM)
    count = planes * OWN
    across = [(d, d ^ 2) for d in range(count)]
    beside = [(d, d ^ 1) for d in range(count)]
    barrier = lax.optimization_barrier

    mate_v = lax.ppermute(values, "seq", beside)
    far_q = lax.ppermute(queries, "seq", across)
    packed = pl.pallas_call(
        functools.partial(pack_kernel, heads, planes, room),
        out_shape=[shape((room, 2) + tile, bf16)] * (planes - 1),
        in_specs=[SMEM] * 2 + [VMEM] * 4,
        out_specs=[VMEM] * (planes - 1),
        compiler_params=params(8 + room // 4),
        cost_estimate=cost(4 << 30),
        name="pack",
    )(where, sends, keys, values, mate_k, mate_v)
    landed = [
        lax.ppermute(packed[step - 1], "seq", [(d, (d + OWN * step) % count) for d in range(count)])
        for step in range(1, planes)
    ]

    where, takes, *packed = barrier((where, takes, *packed))
    most_pairs = min(4 * (planes - 1) * room, HEAD_DIM)
    pair, begin, order, far = pl.pallas_call(
        functools.partial(plan_kernel, heads, planes, room),
        out_shape=[shape((n,), i32) for n in (most_pairs, heads + 1, heads, heads)],
        in_specs=[SMEM] * 2,
        out_specs=[SMEM] * 4,
        compiler_params=params(4),
        cost_estimate=cost(4 << 30),
        name="plan",
    )(where, takes)
    here, lse_here, turned = pl.pallas_call(
        functools.partial(here_kernel, heads),
        out_shape=[shape((heads,) + tile, f32), shape(tile, f32), shape((heads, HEAD_DIM, 2 * rows), bf16)],
        in_specs=[VMEM] * 5,
        out_specs=[VMEM] * 3,
        compiler_params=params(14),
        cost_estimate=cost(1 << 30),
        name="here",
    )(queries, keys, values, mate_k, mate_v)

    def attend_far(order, lse, start, parts):
        return pl.pallas_call(
            functools.partial(far_kernel, start),
            out_shape=[shape((n,) + tile, kind) for n, kind in parts] + [shape(tile, f32)],
            in_specs=[SMEM] + [VMEM] * 5,
            out_specs=[VMEM] * (len(parts) + 1),
            compiler_params=params(12),
            cost_estimate=cost(1 << 30),
            name="far",
        )(order, lse, far_q, turned, values, mate_v)

    second = min(early, late // 3 + 3)
    parts = [n for n in (early - second, second) if n]
    lse_far, arrived = lse_here, []
    if early:
        sent, lse_far = attend_far(order, lse_far, 0, [(parts[0], bf16)])
        arrived = [lax.ppermute(sent, "seq", across)]
    kinds = [(n, bf16) for n in parts[1:]] + [(late, f32)]
    *sent, rest, lse_far = attend_far(order, lse_far, early - sum(parts[1:]), kinds)
    arrived += [lax.ppermute(x, "seq", across) for x in sent]
    *landed, rest, lse_far, first = barrier((*landed, rest, lse_far, arrived[:-1]))
    arrived = first + arrived[len(first) :]
    boxes = []
    for got in landed:
        boxes += [got, lax.ppermute(got, "seq", beside)]

    def add_extras(q, o, lse, by_head, parts):
        return pl.pallas_call(
            functools.partial(late_kernel, len(boxes), early, by_head, room),
            out_shape=[shape((n,) + tile, kind) for n, kind in parts] + [shape(tile, f32)],
            in_specs=[SMEM] * 3 + [VMEM] * 3 + [HBM] * len(boxes),
            out_specs=[VMEM] * (len(parts) + 1),
            scratch_shapes=[
                pltpu.VMEM((len(boxes) * room, 2) + tile, bf16),
                pltpu.VMEM((most_pairs,) + tile, f32),
                pltpu.VMEM((most_pairs,) + tile, f32),
                pltpu.SemaphoreType.DMA((len(boxes),)),
            ],
            compiler_params=params(min(8 + 2 * room, 48)),
            cost_estimate=cost(1 << 20),
            name="late",
        )(order, pair, begin, q, o, lse, *boxes)

    *far_late, lse_far = add_extras(far_q, rest, lse_far, False, [(n, bf16) for n in thirds(late)])
    arrived = [lax.ppermute(lse_far, "seq", across), *arrived] + [lax.ppermute(x, "seq", across) for x in far_late]
    here_late, lse_here = add_extras(queries, here, lse_here, True, [(late, f32)])

    return pl.pallas_call(
        functools.partial(merge_kernel, heads, early),
        out_shape=pltpu.HBM((rows, features), bf16),
        in_specs=[SMEM] * 2 + [HBM] + [VMEM] * 3 + [HBM] * (len(arrived) - 1),
        out_specs=pl.BlockSpec(memory_space=pltpu.HBM),
        scratch_shapes=[
            pltpu.VMEM((heads,) + tile, f32),
            pltpu.VMEM((heads,) + tile, bf16),
            pltpu.VMEM((rows, features), bf16),
            pltpu.SemaphoreType.DMA((6,)),
            pltpu.SemaphoreType.DMA((heads // 8,)),
        ],
        compiler_params=params(12),
        cost_estimate=cost(1 << 20),
        name="merge",
    )(order, far, here, here_late, lse_here, *arrived)


def per_plane(queries, keys, values, kept, counts):
    heads, planes, slots = kept.shape
    device = lax.axis_index("seq").astype(jnp.int32)
    where = jnp.stack([device >> 2, device, (device >> 1) & 1, device & 1])
    beside = [(d, d ^ 1) for d in range(planes * OWN)]
    mate_k = lax.ppermute(keys, "seq", beside)
    shape = jax.ShapeDtypeStruct
    sends, takes, choice = pl.pallas_call(
        functools.partial(lists_kernel, planes, slots),
        out_shape=[
            shape((2 * planes, HEAD_DIM), jnp.int32),
            shape((planes * OWN, HEAD_DIM), jnp.int32),
            shape((1,), jnp.int32),
        ],
        in_specs=[SMEM] + [VMEM] * 2,
        out_specs=[VMEM] * 2 + [SMEM],
        compiler_params=params(60),
        name="lists",
    )(where, kept.transpose(1, 2, 0).reshape(planes * slots, heads), counts.T)
    sizes = SIZES + ((heads, heads),)
    return lax.switch(
        choice[0],
        [functools.partial(exchange, room, late, planes) for room, late in sizes],
        queries,
        keys,
        values,
        mate_k,
        sends,
        takes,
        where,
    )


def attend_tile(query_tile, key_tiles, value_tiles, slot_list, live_count):
    row_count = query_tile.shape[0]
    factor = 1.0 / query_tile.shape[1] ** 0.5
    start_state = (
        jnp.full((row_count,), -1e30, jnp.float32),
        jnp.zeros((row_count,), jnp.float32),
        jnp.zeros((row_count, query_tile.shape[1]), jnp.float32),
    )

    def advance(block_num, state_now):
        running, totals, numerator = state_now
        first = (block_num * GROUP).astype(jnp.int32)
        chosen = lax.dynamic_slice_in_dim(slot_list, first, GROUP)
        key_block = key_tiles[chosen].reshape(GROUP * KTILE, query_tile.shape[1])
        value_block = value_tiles[chosen].reshape(GROUP * KTILE, query_tile.shape[1])
        scores = jnp.dot(query_tile, key_block.T, preferred_element_type=jnp.float32) * factor
        live_mask = jnp.repeat(first + jnp.arange(GROUP, dtype=jnp.int32) < live_count, KTILE)
        scores = jnp.where(live_mask[None, :], scores, -1e30)
        new_max = jnp.maximum(running, jnp.max(scores, axis=1))
        rescale = jnp.exp(running - new_max)
        weights = jnp.exp(scores - new_max[:, None])
        totals = totals * rescale + jnp.sum(weights, axis=1)
        numerator = numerator * rescale[:, None] + jnp.dot(
            weights.astype(jnp.bfloat16), value_block, preferred_element_type=jnp.float32
        )
        return (new_max, totals, numerator)

    block_total = (live_count + GROUP - 1) // GROUP
    running, totals, numerator = lax.fori_loop(jnp.int32(0), block_total, advance, start_state)
    return (numerator / totals[:, None]).astype(jnp.bfloat16)


def per_device(queries, keys, values, kept, counts):
    local_rows, feature_count = queries.shape
    shards = lax.axis_size("seq")
    device = lax.axis_index("seq")
    head_count = feature_count // HEAD_DIM
    replicas = max(1, shards // head_count)
    slots_here = max(1, head_count // shards)
    total_rows = local_rows * shards
    tile_count = counts.shape[1]
    stacked = jnp.stack([queries, keys, values])
    copied = jnp.broadcast_to(
        stacked.reshape(3, local_rows, head_count, 1, HEAD_DIM),
        (3, local_rows, head_count, replicas, HEAD_DIM),
    )
    copied = copied.reshape(3, local_rows, head_count * replicas, HEAD_DIM)
    arrived = lax.all_to_all(copied, "seq", split_axis=2, concat_axis=1, tiled=True)
    head_data = arrived.transpose(2, 0, 1, 3)
    tiles_each = tile_count // replicas
    results = []
    for j in range(slots_here):
        global_slot = device * slots_here + j
        head_id = global_slot // replicas
        replica_id = global_slot % replicas
        slot_rows = lax.dynamic_index_in_dim(kept, head_id, 0, keepdims=False)
        count_row = lax.dynamic_index_in_dim(counts, head_id, 0, keepdims=False)
        all_queries = head_data[j, 0]
        key_tiles = head_data[j, 1].reshape(total_rows // KTILE, KTILE, HEAD_DIM)
        value_tiles = head_data[j, 2].reshape(total_rows // KTILE, KTILE, HEAD_DIM)
        rounds = jnp.arange(tiles_each, dtype=jnp.int32)
        tile_ids = replica_id * tiles_each + rounds

        def process(i, output):
            tile_id = tile_ids[i]
            query_tile = lax.dynamic_slice_in_dim(all_queries, tile_id * QTILE, QTILE, 0)
            finished = attend_tile(
                query_tile, key_tiles, value_tiles, slot_rows[tile_id], count_row[tile_id]
            )
            return lax.dynamic_update_slice_in_dim(output, finished, tile_id * QTILE, 0)

        results.append(
            lax.fori_loop(0, tiles_each, process, jnp.zeros((total_rows, HEAD_DIM), jnp.bfloat16))
        )
    gathered = jnp.stack(results, axis=1)
    returned = lax.all_to_all(gathered, "seq", split_axis=0, concat_axis=1, tiled=True)
    combined = (
        returned.reshape(local_rows, head_count, replicas, HEAD_DIM).astype(jnp.float32).sum(axis=2)
    )
    return combined.astype(jnp.bfloat16).reshape(local_rows, feature_count)


def solution(mesh):
    by_rows = P(("groups", "seq"), None)
    placed = (by_rows, by_rows, by_rows, P("groups", None, None), P("groups", None))

    def step(queries, keys, values, kept, counts):
        heads, planes, slots = kept.shape
        one_tile_each = queries.shape[0] == KTILE and mesh.shape["seq"] == planes * OWN
        fits = heads % 8 == 0 and heads <= 32 and heads * (slots - OWN) <= HEAD_DIM and planes == 4
        run = per_plane if one_tile_each and fits else per_device
        return run(queries, keys, values, kept, counts)

    return jax.shard_map(step, mesh=mesh, in_specs=placed, out_specs=by_rows, check_vma=False)
```

```python
import functools

import jax
import jax.numpy as jnp
from jax import lax
from jax.experimental import pallas as pl
from jax.experimental.pallas import tpu as pltpu
from jax.sharding import PartitionSpec as P

HEAD_DIM = 128
QTILE = 512
KTILE = 128
GROUP = 4
OWN = QTILE // KTILE
SIZES = ((5, 16), (6, 18), (7, 20))
MIB = 1 << 20
SMEM = pl.BlockSpec(memory_space=pltpu.SMEM)
VMEM = pl.BlockSpec(memory_space=pltpu.VMEM)
HBM = pl.BlockSpec(memory_space=pl.ANY)


def params(mib):
    return pltpu.CompilerParams(vmem_limit_bytes=mib * MIB)


def cost(flops):
    return pl.CostEstimate(flops=flops, bytes_accessed=8 << 20, transcendentals=0)


def thirds(late):
    return late // 3, late // 3, late - 2 * (late // 3)


def columns(head):
    if isinstance(head, int):
        return pl.ds(head * HEAD_DIM, HEAD_DIM)
    return pl.ds(pl.multiple_of(head * HEAD_DIM, HEAD_DIM), HEAD_DIM)


def dot(a, b):
    return jnp.dot(a, b, preferred_element_type=jnp.float32)


def lists_kernel(planes, slots, where, kept, counts, sends, takes, choice):
    plane, pair = where[0], where[1] >> 1
    heads = kept.shape[1]
    shape = (planes * OWN, heads)
    half = (planes * OWN // 2, heads)
    ids = lax.broadcasted_iota(jnp.int32, shape, 0)
    chips = lax.broadcasted_iota(jnp.int32, half, 0)
    bit = jnp.left_shift(jnp.int32(1), lax.broadcasted_iota(jnp.int32, shape, 1))
    lane = lax.broadcasted_iota(jnp.int32, (1, HEAD_DIM), 1)
    most = jnp.zeros((planes * OWN // 2, 1), jnp.int32)
    touched = jnp.zeros((1, 1), jnp.int32)
    taken = jnp.zeros(shape, jnp.int32)
    wanted = []
    for t in range(planes):
        hits = jnp.zeros(shape, jnp.int32)
        per_chip = jnp.zeros(half, jnp.int32)
        for j in range(OWN, slots):
            tile = kept[t * slots + j : t * slots + j + 1, :]
            live = counts[t : t + 1, :] > j
            hits = jnp.where((ids == tile) & live, 1, hits)
            per_chip = per_chip + jnp.where((chips == (tile >> 1)) & live, 1, 0)
        most = jnp.maximum(most, jnp.sum(per_chip, axis=1, keepdims=True))
        for side in range(2):
            some = jnp.max(jnp.where(((ids >> 1) & 1) == side, hits, 0), axis=0, keepdims=True)
            touched = jnp.maximum(touched, jnp.sum(some, axis=1, keepdims=True))
        bits = hits * bit
        for turn in range(2):
            wanted.append(jnp.sum(jnp.where(ids == 2 * pair + turn, hits, 0), axis=0, keepdims=True))
        taken = jnp.where(plane == t, bits, taken)
    square = (heads, heads)
    at, head = lax.broadcasted_iota(jnp.int32, square, 0), lax.broadcasted_iota(jnp.int32, square, 1)
    before = jnp.where(at < head, 1.0, 0.0)
    named = jnp.concatenate(wanted, axis=0)
    rank = dot(named.astype(jnp.float32), before).astype(jnp.int32)
    rows = jnp.zeros((heads, HEAD_DIM), jnp.int32)
    count = jnp.zeros((1, HEAD_DIM), jnp.int32)
    for i in range(2 * planes):
        here = (at == rank[i : i + 1, :]) & (named[i : i + 1, :] == 1)
        rows = jnp.where(lane == i, jnp.sum(jnp.where(here, head, 0), axis=1, keepdims=True), rows)
        count = jnp.where(lane == i, jnp.sum(named[i : i + 1, :], axis=1, keepdims=True), count)
    sends[0:heads, :] = rows
    sends[heads : heads + 8, :] = jnp.broadcast_to(count, (8, HEAD_DIM))
    takes[...] = jnp.where(
        lane == 0,
        jnp.sum(taken, axis=1, keepdims=True),
        jnp.sum(jnp.where(taken != 0, 1, 0), axis=1, keepdims=True),
    )
    top, wide = jnp.max(most), jnp.max(touched)
    index = jnp.int32(len(SIZES))
    for i, (room, late) in reversed(list(enumerate(SIZES))):
        index = jnp.where((top <= 2 * room) & (wide <= late), i, index)
    choice[0] = index


def pack_kernel(heads, planes, room, where, sends, k_ref, v_ref, mate_k, mate_v, *outs):
    plane, core = where[0], where[3]
    for step, out in enumerate(outs, 1):
        lane = 2 * lax.rem(plane + step, planes)
        first, both = sends[heads, lane], sends[heads, lane] + sends[heads, lane + 1]

        def take(slot, carry, out=out, lane=lane, first=first):
            at = core * room + slot
            turn = jnp.where(at >= first, 1, 0)
            head = sends[at - turn * first, lane + turn]

            @pl.when(core == turn)
            def _():
                out[slot, 0] = k_ref[:, columns(head)].T
                out[slot, 1] = v_ref[:, columns(head)]

            @pl.when(core != turn)
            def _():
                out[slot, 0] = mate_k[:, columns(head)].T
                out[slot, 1] = mate_v[:, columns(head)]

            return carry

        lax.fori_loop(0, jnp.clip(both - core * room, 0, room), take, 0)


def plan_kernel(heads, planes, room, where, takes, pair, begin, order, far):
    plane, side, core = where[0], where[2], where[3]
    near, other, starts = [], [], []
    for step in range(1, planes):
        source = lax.rem(plane - step + planes, planes) * OWN
        for turn in range(2):
            near.append(takes[source + 2 * side + turn, 0])
            starts.append(takes[source + 2 * side, 1] if turn else jnp.int32(0))
            other.append(takes[source + 2 * (1 - side) + turn, 0])
    any_near = functools.reduce(jnp.bitwise_or, near)
    any_other = functools.reduce(jnp.bitwise_or, other)

    def held(bits):
        return lax.fori_loop(0, heads, lambda h, n: n + ((bits >> h) & 1), jnp.int32(0))

    def put(head, state):
        a, b, c, d, pairs, *used = state
        none, far_none = 1 - ((any_near >> head) & 1), 1 - ((any_other >> head) & 1)
        at = jnp.where(none == 1, a, b)
        order[at] = head
        far[head] = jnp.where(far_none == 1, c, d)
        begin[head] = pairs
        for i, bits in enumerate(near):
            hit = (bits >> head) & 1
            sender = jnp.where(used[i] >= room, 1, 0)
            box = i // 2 * 2 + jnp.where(sender == core, 0, 1)

            @pl.when(hit == 1)
            def _(i=i, pairs=pairs, used=used, sender=sender, box=box):
                pair[pairs] = head * 4096 + box * room + used[i] - sender * room

            pairs = pairs + hit
            used = used[:i] + [used[i] + hit] + used[i + 1 :]
        return (a + none, b + 1 - none, c + far_none, d + 1 - far_none, pairs, *used)

    zero = jnp.int32(0)
    first = (zero, heads - held(any_near), zero, heads - held(any_other), zero, *starts)
    begin[heads] = lax.fori_loop(0, heads, put, first)[4]


def soften(q, k_t, v):
    s = dot(q, k_t) * (1.0 / HEAD_DIM**0.5)
    m = jnp.max(s, axis=1, keepdims=True)
    w = jnp.exp(s - m)
    l = jnp.sum(w, axis=1, keepdims=True)
    return dot(w.astype(jnp.bfloat16), v) / l, m + jnp.log(l)


def here_kernel(heads, q_ref, k_ref, v_ref, mate_k, mate_v, out, lse_out, turned):
    lane = lax.broadcasted_iota(jnp.int32, lse_out.shape, 1)

    def attend(head, lse):
        at = columns(head)
        k_t = jnp.concatenate([k_ref[:, at].T, mate_k[:, at].T], axis=1)
        turned[head] = k_t
        v = jnp.concatenate([v_ref[:, at], mate_v[:, at]], axis=0)
        o, new = soften(q_ref[:, at], k_t, v)
        out[head] = o
        return jnp.where(lane == head, new, lse)

    lse_out[...] = lax.fori_loop(0, heads, attend, jnp.zeros(lse_out.shape, jnp.float32), unroll=4)


def far_kernel(start, order, lse_ref, q_ref, turned, v_ref, mate_v, *outs):
    *parts, lse_out = outs
    lane = lax.broadcasted_iota(jnp.int32, lse_out.shape, 1)
    lse = lse_ref[...]
    for part in parts:

        def attend(i, lse, part=part, start=start):
            head = order[start + i]
            at = columns(head)
            v = jnp.concatenate([v_ref[:, at], mate_v[:, at]], axis=0)
            o, new = soften(q_ref[:, at], turned[head], v)
            part[i] = o.astype(part.dtype)
            return jnp.where(lane == head, new, lse)

        lse = lax.fori_loop(0, part.shape[0], attend, lse, unroll=4)
        start += part.shape[0]
    lse_out[...] = lse


def late_kernel(sends, early, by_head, room, order, pair, begin, q_ref, o_ref, lse_ref, *rest):
    boxes, rest = rest[: sends], rest[sends:]
    *outs, lse_out, tiles, partial, level, sems = rest
    copies = [
        pltpu.make_async_copy(box, tiles.at[pl.ds(b * room, room)], sems.at[b]) for b, box in enumerate(boxes)
    ]
    for copy in copies:
        copy.start()
    heads = order.shape[0]
    shape = lse_ref.shape
    most = partial.shape[0]
    lane = lax.broadcasted_iota(jnp.int32, shape, 1)
    total = begin[heads]
    for copy in copies:
        copy.wait()

    def four(i, carry):
        for j in range(4):
            at = jnp.minimum(4 * i + j, total - 1)
            code = pair[at]
            head, tile = code >> 12, code & 4095
            o, new = soften(q_ref[:, columns(head)], tiles[tile, 0], tiles[tile, 1])
            partial[at] = o
            level[at] = jnp.broadcast_to(new, shape)
        return carry

    lax.fori_loop(0, (total + 3) >> 2, four, 0)

    def join(i, lse, out, skip):
        head = order[early + skip + i]
        start, end = begin[head], begin[head + 1]
        base = jnp.sum(jnp.where(lane == head, lse_ref[...], 0.0), axis=1, keepdims=True)
        base = jnp.broadcast_to(base, shape)
        spots = [jnp.minimum(start + e, most - 1) for e in range(4)]
        levels = [jnp.where(start + e < end, level[p], -1e30) for e, p in enumerate(spots)]
        m = functools.reduce(jnp.maximum, levels, base)
        l = jnp.exp(base - m)
        o = l * o_ref[head if by_head else skip + i]
        for e, p in enumerate(spots):
            w = jnp.exp(levels[e] - m)
            l = l + w
            o = o + jnp.where(start + e < end, w * partial[p], 0.0)
        out[i] = (o / l).astype(out.dtype)
        return jnp.where(lane == head, m + jnp.log(l), lse)

    lse, skip = lse_ref[...], 0
    for out in outs:
        lse = lax.fori_loop(0, out.shape[0], functools.partial(join, out=out, skip=skip), lse, unroll=2)
        skip += out.shape[0]
    lse_out[...] = lse if by_head else lse.T[:heads]


def merge_kernel(heads, early, order, far, here, here_late, lse_here, lse_got, *rest):
    *got, result, mine, theirs, out, sems, out_sems = rest
    copies = [pltpu.make_async_copy(here, mine, sems.at[0])]
    start = 0
    for i, part in enumerate(got):
        at = theirs.at[pl.ds(start, part.shape[0])]
        copies.append(pltpu.make_async_copy(part, at, sems.at[1 + i]))
        start += part.shape[0]
    for copy in copies:
        copy.start()
    a, b = lse_here[...], lse_got[...]
    b = jnp.concatenate([b, jnp.zeros((a.shape[1] - heads, a.shape[0]), b.dtype)], axis=0).T
    m = jnp.maximum(a, b)
    wa, wb = jnp.exp(a - m), jnp.exp(b - m)
    total = wa + wb
    wa, wb = wa / total, wb / total
    for copy in copies:
        copy.wait()

    def put(i, carry):
        mine[order[early + i]] = here_late[i]
        return carry

    lax.fori_loop(0, heads - early, put, 0)
    leaving = []
    for head in range(heads):
        joined = wa[:, head : head + 1] * mine[head]
        joined += wb[:, head : head + 1] * theirs[far[head]].astype(jnp.float32)
        out[:, columns(head)] = joined.astype(out.dtype)
        if head % 8 == 7:
            at = pl.ds((head - 7) * HEAD_DIM, 8 * HEAD_DIM)
            leaving.append(pltpu.make_async_copy(out.at[:, at], result.at[:, at], out_sems.at[head // 8]))
            leaving[-1].start()
    for copy in leaving:
        copy.wait()


def exchange(room, late, planes, queries, keys, values, mate_k, sends, takes, where):
    rows, features = queries.shape
    heads = features // HEAD_DIM
    early = heads - late
    f32, bf16, i32 = jnp.float32, jnp.bfloat16, jnp.int32
    shape = jax.ShapeDtypeStruct
    tile = (rows, HEAD_DIM)
    count = planes * OWN
    across = [(d, d ^ 2) for d in range(count)]
    beside = [(d, d ^ 1) for d in range(count)]
    barrier = lax.optimization_barrier

    mate_v = lax.ppermute(values, "seq", beside)
    far_q = lax.ppermute(queries, "seq", across)
    packed = pl.pallas_call(
        functools.partial(pack_kernel, heads, planes, room),
        out_shape=[shape((room, 2) + tile, bf16)] * (planes - 1),
        in_specs=[SMEM] * 2 + [VMEM] * 4,
        out_specs=[VMEM] * (planes - 1),
        compiler_params=params(8 + room // 4),
        cost_estimate=cost(4 << 30),
        name="pack",
    )(where, sends, keys, values, mate_k, mate_v)
    landed = [
        lax.ppermute(packed[step - 1], "seq", [(d, (d + OWN * step) % count) for d in range(count)])
        for step in range(1, planes)
    ]

    where, takes, *packed = barrier((where, takes, *packed))
    most_pairs = min(4 * (planes - 1) * room, HEAD_DIM)
    pair, begin, order, far = pl.pallas_call(
        functools.partial(plan_kernel, heads, planes, room),
        out_shape=[shape((n,), i32) for n in (most_pairs, heads + 1, heads, heads)],
        in_specs=[SMEM] * 2,
        out_specs=[SMEM] * 4,
        compiler_params=params(4),
        cost_estimate=cost(4 << 30),
        name="plan",
    )(where, takes)
    here, lse_here, turned = pl.pallas_call(
        functools.partial(here_kernel, heads),
        out_shape=[shape((heads,) + tile, f32), shape(tile, f32), shape((heads, HEAD_DIM, 2 * rows), bf16)],
        in_specs=[VMEM] * 5,
        out_specs=[VMEM] * 3,
        compiler_params=params(14),
        cost_estimate=cost(1 << 30),
        name="here",
    )(queries, keys, values, mate_k, mate_v)

    def attend_far(order, lse, start, parts):
        return pl.pallas_call(
            functools.partial(far_kernel, start),
            out_shape=[shape((n,) + tile, kind) for n, kind in parts] + [shape(tile, f32)],
            in_specs=[SMEM] + [VMEM] * 5,
            out_specs=[VMEM] * (len(parts) + 1),
            compiler_params=params(12),
            cost_estimate=cost(1 << 30),
            name="far",
        )(order, lse, far_q, turned, values, mate_v)

    second = early * 3 // 8
    parts = [n for n in (early - second, second) if n]
    lse_far, arrived = lse_here, []
    if early:
        sent, lse_far = attend_far(order, lse_far, 0, [(parts[0], bf16)])
        arrived = [lax.ppermute(sent, "seq", across)]
    kinds = [(n, bf16) for n in parts[1:]] + [(late, f32)]
    *sent, rest, lse_far = attend_far(order, lse_far, early - sum(parts[1:]), kinds)
    arrived += [lax.ppermute(x, "seq", across) for x in sent]
    *landed, rest, lse_far, arrived = barrier((*landed, rest, lse_far, arrived))
    boxes = []
    for got in landed:
        boxes += [got, lax.ppermute(got, "seq", beside)]

    def add_extras(q, o, lse, by_head, parts):
        return pl.pallas_call(
            functools.partial(late_kernel, len(boxes), early, by_head, room),
            out_shape=[shape((n,) + tile, kind) for n, kind in parts] + [shape(tile if by_head else (heads, rows), f32)],
            in_specs=[SMEM] * 3 + [VMEM] * 3 + [HBM] * len(boxes),
            out_specs=[VMEM] * (len(parts) + 1),
            scratch_shapes=[
                pltpu.VMEM((len(boxes) * room, 2) + tile, bf16),
                pltpu.VMEM((most_pairs,) + tile, f32),
                pltpu.VMEM((most_pairs,) + tile, f32),
                pltpu.SemaphoreType.DMA((len(boxes),)),
            ],
            compiler_params=params(min(8 + 2 * room, 48)),
            cost_estimate=cost(1 << 20),
            name="late",
        )(order, pair, begin, q, o, lse, *boxes)

    *far_late, lse_far = add_extras(far_q, rest, lse_far, False, [(n, bf16) for n in thirds(late)])
    arrived = [lax.ppermute(lse_far, "seq", across), *arrived] + [lax.ppermute(x, "seq", across) for x in far_late]
    here_late, lse_here = add_extras(queries, here, lse_here, True, [(late, f32)])

    return pl.pallas_call(
        functools.partial(merge_kernel, heads, early),
        out_shape=pltpu.HBM((rows, features), bf16),
        in_specs=[SMEM] * 2 + [HBM] + [VMEM] * 3 + [HBM] * (len(arrived) - 1),
        out_specs=pl.BlockSpec(memory_space=pltpu.HBM),
        scratch_shapes=[
            pltpu.VMEM((heads,) + tile, f32),
            pltpu.VMEM((heads,) + tile, bf16),
            pltpu.VMEM((rows, features), bf16),
            pltpu.SemaphoreType.DMA((6,)),
            pltpu.SemaphoreType.DMA((heads // 8,)),
        ],
        compiler_params=params(12),
        cost_estimate=cost(1 << 20),
        name="merge",
    )(order, far, here, here_late, lse_here, *arrived)


def per_plane(queries, keys, values, kept, counts):
    heads, planes, slots = kept.shape
    device = lax.axis_index("seq").astype(jnp.int32)
    where = jnp.stack([device >> 2, device, (device >> 1) & 1, device & 1])
    beside = [(d, d ^ 1) for d in range(planes * OWN)]
    mate_k = lax.ppermute(keys, "seq", beside)
    shape = jax.ShapeDtypeStruct
    sends, takes, choice = pl.pallas_call(
        functools.partial(lists_kernel, planes, slots),
        out_shape=[
            shape((heads + 8, HEAD_DIM), jnp.int32),
            shape((planes * OWN, HEAD_DIM), jnp.int32),
            shape((1,), jnp.int32),
        ],
        in_specs=[SMEM] + [VMEM] * 2,
        out_specs=[VMEM] * 2 + [SMEM],
        compiler_params=params(60),
        name="lists",
    )(where, kept.transpose(1, 2, 0).reshape(planes * slots, heads), counts.T)
    sizes = SIZES + ((heads, heads),)
    return lax.switch(
        choice[0],
        [functools.partial(exchange, room, late, planes) for room, late in sizes],
        queries,
        keys,
        values,
        mate_k,
        sends,
        takes,
        where,
    )


def attend_tile(query_tile, key_tiles, value_tiles, slot_list, live_count):
    row_count = query_tile.shape[0]
    factor = 1.0 / query_tile.shape[1] ** 0.5
    start_state = (
        jnp.full((row_count,), -1e30, jnp.float32),
        jnp.zeros((row_count,), jnp.float32),
        jnp.zeros((row_count, query_tile.shape[1]), jnp.float32),
    )

    def advance(block_num, state_now):
        running, totals, numerator = state_now
        first = (block_num * GROUP).astype(jnp.int32)
        chosen = lax.dynamic_slice_in_dim(slot_list, first, GROUP)
        key_block = key_tiles[chosen].reshape(GROUP * KTILE, query_tile.shape[1])
        value_block = value_tiles[chosen].reshape(GROUP * KTILE, query_tile.shape[1])
        scores = jnp.dot(query_tile, key_block.T, preferred_element_type=jnp.float32) * factor
        live_mask = jnp.repeat(first + jnp.arange(GROUP, dtype=jnp.int32) < live_count, KTILE)
        scores = jnp.where(live_mask[None, :], scores, -1e30)
        new_max = jnp.maximum(running, jnp.max(scores, axis=1))
        rescale = jnp.exp(running - new_max)
        weights = jnp.exp(scores - new_max[:, None])
        totals = totals * rescale + jnp.sum(weights, axis=1)
        numerator = numerator * rescale[:, None] + jnp.dot(
            weights.astype(jnp.bfloat16), value_block, preferred_element_type=jnp.float32
        )
        return (new_max, totals, numerator)

    block_total = (live_count + GROUP - 1) // GROUP
    running, totals, numerator = lax.fori_loop(jnp.int32(0), block_total, advance, start_state)
    return (numerator / totals[:, None]).astype(jnp.bfloat16)


def per_device(queries, keys, values, kept, counts):
    local_rows, feature_count = queries.shape
    shards = lax.axis_size("seq")
    device = lax.axis_index("seq")
    head_count = feature_count // HEAD_DIM
    replicas = max(1, shards // head_count)
    slots_here = max(1, head_count // shards)
    total_rows = local_rows * shards
    tile_count = counts.shape[1]
    stacked = jnp.stack([queries, keys, values])
    copied = jnp.broadcast_to(
        stacked.reshape(3, local_rows, head_count, 1, HEAD_DIM),
        (3, local_rows, head_count, replicas, HEAD_DIM),
    )
    copied = copied.reshape(3, local_rows, head_count * replicas, HEAD_DIM)
    arrived = lax.all_to_all(copied, "seq", split_axis=2, concat_axis=1, tiled=True)
    head_data = arrived.transpose(2, 0, 1, 3)
    tiles_each = tile_count // replicas
    results = []
    for j in range(slots_here):
        global_slot = device * slots_here + j
        head_id = global_slot // replicas
        replica_id = global_slot % replicas
        slot_rows = lax.dynamic_index_in_dim(kept, head_id, 0, keepdims=False)
        count_row = lax.dynamic_index_in_dim(counts, head_id, 0, keepdims=False)
        all_queries = head_data[j, 0]
        key_tiles = head_data[j, 1].reshape(total_rows // KTILE, KTILE, HEAD_DIM)
        value_tiles = head_data[j, 2].reshape(total_rows // KTILE, KTILE, HEAD_DIM)
        rounds = jnp.arange(tiles_each, dtype=jnp.int32)
        tile_ids = replica_id * tiles_each + rounds

        def process(i, output):
            tile_id = tile_ids[i]
            query_tile = lax.dynamic_slice_in_dim(all_queries, tile_id * QTILE, QTILE, 0)
            finished = attend_tile(
                query_tile, key_tiles, value_tiles, slot_rows[tile_id], count_row[tile_id]
            )
            return lax.dynamic_update_slice_in_dim(output, finished, tile_id * QTILE, 0)

        results.append(
            lax.fori_loop(0, tiles_each, process, jnp.zeros((total_rows, HEAD_DIM), jnp.bfloat16))
        )
    gathered = jnp.stack(results, axis=1)
    returned = lax.all_to_all(gathered, "seq", split_axis=0, concat_axis=1, tiled=True)
    combined = (
        returned.reshape(local_rows, head_count, replicas, HEAD_DIM).astype(jnp.float32).sum(axis=2)
    )
    return combined.astype(jnp.bfloat16).reshape(local_rows, feature_count)


def solution(mesh):
    by_rows = P(("groups", "seq"), None)
    placed = (by_rows, by_rows, by_rows, P("groups", None, None), P("groups", None))

    def step(queries, keys, values, kept, counts):
        heads, planes, slots = kept.shape
        one_tile_each = queries.shape[0] == KTILE and mesh.shape["seq"] == planes * OWN
        fits = heads % 8 == 0 and heads <= 32 and heads * (slots - OWN) <= HEAD_DIM and planes == 4
        run = per_plane if one_tile_each and fits else per_device
        return run(queries, keys, values, kept, counts)

    return jax.shard_map(step, mesh=mesh, in_specs=placed, out_specs=by_rows, check_vma=False)
```

```python
import functools

import jax
import jax.numpy as jnp
from jax import lax
from jax.experimental import pallas as pl
from jax.experimental.pallas import tpu as pltpu
from jax.sharding import PartitionSpec as P

HEAD_DIM = 128
QTILE = 512
KTILE = 128
GROUP = 4
OWN = QTILE // KTILE
SIZES = ((5, 16), (6, 18), (7, 20))
MIB = 1 << 20
SMEM = pl.BlockSpec(memory_space=pltpu.SMEM)
VMEM = pl.BlockSpec(memory_space=pltpu.VMEM)
HBM = pl.BlockSpec(memory_space=pl.ANY)


def params(mib):
    return pltpu.CompilerParams(vmem_limit_bytes=mib * MIB)


def cost(flops):
    return pl.CostEstimate(flops=flops, bytes_accessed=8 << 20, transcendentals=0)


def thirds(late):
    return late // 3, late // 3, late - 2 * (late // 3)


def columns(head):
    if isinstance(head, int):
        return pl.ds(head * HEAD_DIM, HEAD_DIM)
    return pl.ds(pl.multiple_of(head * HEAD_DIM, HEAD_DIM), HEAD_DIM)


def dot(a, b):
    return jnp.dot(a, b, preferred_element_type=jnp.float32)


def lists_kernel(planes, slots, where, kept, counts, sends, takes, choice):
    plane, pair = where[0], where[1] >> 1
    heads = kept.shape[1]
    shape = (planes * OWN, heads)
    half = (planes * OWN // 2, heads)
    ids = lax.broadcasted_iota(jnp.int32, shape, 0)
    chips = lax.broadcasted_iota(jnp.int32, half, 0)
    bit = jnp.left_shift(jnp.int32(1), lax.broadcasted_iota(jnp.int32, shape, 1))
    lane = lax.broadcasted_iota(jnp.int32, (1, HEAD_DIM), 1)
    most = jnp.zeros((planes * OWN // 2, 1), jnp.int32)
    touched = jnp.zeros((1, 1), jnp.int32)
    taken = jnp.zeros(shape, jnp.int32)
    wanted = []
    for t in range(planes):
        hits = jnp.zeros(shape, jnp.int32)
        per_chip = jnp.zeros(half, jnp.int32)
        for j in range(OWN, slots):
            tile = kept[t * slots + j : t * slots + j + 1, :]
            live = counts[t : t + 1, :] > j
            hits = jnp.where((ids == tile) & live, 1, hits)
            per_chip = per_chip + jnp.where((chips == (tile >> 1)) & live, 1, 0)
        most = jnp.maximum(most, jnp.sum(per_chip, axis=1, keepdims=True))
        for side in range(2):
            some = jnp.max(jnp.where(((ids >> 1) & 1) == side, hits, 0), axis=0, keepdims=True)
            touched = jnp.maximum(touched, jnp.sum(some, axis=1, keepdims=True))
        bits = hits * bit
        for turn in range(2):
            wanted.append(jnp.sum(jnp.where(ids == 2 * pair + turn, hits, 0), axis=0, keepdims=True))
        taken = jnp.where(plane == t, bits, taken)
    square = (heads, heads)
    at, head = lax.broadcasted_iota(jnp.int32, square, 0), lax.broadcasted_iota(jnp.int32, square, 1)
    before = jnp.where(at < head, 1.0, 0.0)
    named = jnp.concatenate(wanted, axis=0)
    rank = dot(named.astype(jnp.float32), before).astype(jnp.int32)
    rows = jnp.zeros((heads, HEAD_DIM), jnp.int32)
    count = jnp.zeros((1, HEAD_DIM), jnp.int32)
    for i in range(2 * planes):
        here = (at == rank[i : i + 1, :]) & (named[i : i + 1, :] == 1)
        rows = jnp.where(lane == i, jnp.sum(jnp.where(here, head, 0), axis=1, keepdims=True), rows)
        count = jnp.where(lane == i, jnp.sum(named[i : i + 1, :], axis=1, keepdims=True), count)
    sends[0:heads, :] = rows
    sends[heads : heads + 8, :] = jnp.broadcast_to(count, (8, HEAD_DIM))
    takes[...] = jnp.where(
        lane == 0,
        jnp.sum(taken, axis=1, keepdims=True),
        jnp.sum(jnp.where(taken != 0, 1, 0), axis=1, keepdims=True),
    )
    top, wide = jnp.max(most), jnp.max(touched)
    index = jnp.int32(len(SIZES))
    for i, (room, late) in reversed(list(enumerate(SIZES))):
        index = jnp.where((top <= 2 * room) & (wide <= late), i, index)
    choice[0] = index


def pack_kernel(heads, planes, room, where, sends, k_ref, v_ref, mate_k, mate_v, *outs):
    plane, core = where[0], where[3]
    for step, out in enumerate(outs, 1):
        lane = 2 * lax.rem(plane + step, planes)
        first, both = sends[heads, lane], sends[heads, lane] + sends[heads, lane + 1]

        def take(slot, carry, out=out, lane=lane, first=first):
            at = core * room + slot
            turn = jnp.where(at >= first, 1, 0)
            head = sends[at - turn * first, lane + turn]

            @pl.when(core == turn)
            def _():
                out[slot, 0] = k_ref[:, columns(head)].T
                out[slot, 1] = v_ref[:, columns(head)]

            @pl.when(core != turn)
            def _():
                out[slot, 0] = mate_k[:, columns(head)].T
                out[slot, 1] = mate_v[:, columns(head)]

            return carry

        lax.fori_loop(0, jnp.clip(both - core * room, 0, room), take, 0)


def plan_kernel(heads, planes, room, where, takes, pair, begin, order, far):
    plane, side, core = where[0], where[2], where[3]
    near, other, starts = [], [], []
    for step in range(1, planes):
        source = lax.rem(plane - step + planes, planes) * OWN
        for turn in range(2):
            near.append(takes[source + 2 * side + turn, 0])
            starts.append(takes[source + 2 * side, 1] if turn else jnp.int32(0))
            other.append(takes[source + 2 * (1 - side) + turn, 0])
    any_near = functools.reduce(jnp.bitwise_or, near)
    any_other = functools.reduce(jnp.bitwise_or, other)

    def held(bits):
        return lax.fori_loop(0, heads, lambda h, n: n + ((bits >> h) & 1), jnp.int32(0))

    def put(head, state):
        a, b, c, d, pairs, *used = state
        none, far_none = 1 - ((any_near >> head) & 1), 1 - ((any_other >> head) & 1)
        at = jnp.where(none == 1, a, b)
        order[at] = head
        far[head] = jnp.where(far_none == 1, c, d)
        begin[head] = pairs
        for i, bits in enumerate(near):
            hit = (bits >> head) & 1
            sender = jnp.where(used[i] >= room, 1, 0)
            box = i // 2 * 2 + jnp.where(sender == core, 0, 1)

            @pl.when(hit == 1)
            def _(i=i, pairs=pairs, used=used, sender=sender, box=box):
                pair[pairs] = head * 4096 + box * room + used[i] - sender * room

            pairs = pairs + hit
            used = used[:i] + [used[i] + hit] + used[i + 1 :]
        return (a + none, b + 1 - none, c + far_none, d + 1 - far_none, pairs, *used)

    zero = jnp.int32(0)
    first = (zero, heads - held(any_near), zero, heads - held(any_other), zero, *starts)
    begin[heads] = lax.fori_loop(0, heads, put, first)[4]


def soften(q, k_t, v):
    s = dot(q, k_t) * (1.0 / HEAD_DIM**0.5)
    m = jnp.max(s, axis=1, keepdims=True)
    w = jnp.exp(s - m)
    l = jnp.sum(w, axis=1, keepdims=True)
    return dot(w.astype(jnp.bfloat16), v) / l, m + jnp.log(l)


def here_kernel(heads, q_ref, k_ref, v_ref, mate_k, mate_v, out, lse_out, turned):
    lane = lax.broadcasted_iota(jnp.int32, lse_out.shape, 1)

    def attend(head, lse):
        at = columns(head)
        k_t = jnp.concatenate([k_ref[:, at].T, mate_k[:, at].T], axis=1)
        turned[head] = k_t
        v = jnp.concatenate([v_ref[:, at], mate_v[:, at]], axis=0)
        o, new = soften(q_ref[:, at], k_t, v)
        out[head] = o
        return jnp.where(lane == head, new, lse)

    lse_out[...] = lax.fori_loop(0, heads, attend, jnp.zeros(lse_out.shape, jnp.float32), unroll=4)


def far_kernel(start, order, lse_ref, q_ref, turned, v_ref, mate_v, *outs):
    *parts, lse_out = outs
    lane = lax.broadcasted_iota(jnp.int32, lse_out.shape, 1)
    lse = lse_ref[...]
    for part in parts:

        def attend(i, lse, part=part, start=start):
            head = order[start + i]
            at = columns(head)
            v = jnp.concatenate([v_ref[:, at], mate_v[:, at]], axis=0)
            o, new = soften(q_ref[:, at], turned[head], v)
            part[i] = o.astype(part.dtype)
            return jnp.where(lane == head, new, lse)

        lse = lax.fori_loop(0, part.shape[0], attend, lse, unroll=4)
        start += part.shape[0]
    lse_out[...] = lse


def late_kernel(sends, early, by_head, room, order, pair, begin, q_ref, o_ref, lse_ref, *rest):
    boxes, rest = rest[: sends], rest[sends:]
    *outs, lse_out, tiles, partial, level, sems = rest
    copies = [
        pltpu.make_async_copy(box, tiles.at[pl.ds(b * room, room)], sems.at[b]) for b, box in enumerate(boxes)
    ]
    for copy in copies:
        copy.start()
    heads = order.shape[0]
    shape = lse_ref.shape
    most = partial.shape[0]
    lane = lax.broadcasted_iota(jnp.int32, shape, 1)
    total = begin[heads]
    for copy in copies:
        copy.wait()

    def four(i, carry):
        for j in range(4):
            at = jnp.minimum(4 * i + j, total - 1)
            code = pair[at]
            head, tile = code >> 12, code & 4095
            o, new = soften(q_ref[:, columns(head)], tiles[tile, 0], tiles[tile, 1])
            partial[at] = o
            level[at] = jnp.broadcast_to(new, shape)
        return carry

    lax.fori_loop(0, (total + 3) >> 2, four, 0)

    def join(i, lse, out, skip):
        head = order[early + skip + i]
        start, end = begin[head], begin[head + 1]
        base = jnp.sum(jnp.where(lane == head, lse_ref[...], 0.0), axis=1, keepdims=True)
        base = jnp.broadcast_to(base, shape)
        spots = [jnp.minimum(start + e, most - 1) for e in range(4)]
        levels = [jnp.where(start + e < end, level[p], -1e30) for e, p in enumerate(spots)]
        m = functools.reduce(jnp.maximum, levels, base)
        l = jnp.exp(base - m)
        o = l * o_ref[head if by_head else skip + i]
        for e, p in enumerate(spots):
            w = jnp.exp(levels[e] - m)
            l = l + w
            o = o + jnp.where(start + e < end, w * partial[p], 0.0)
        out[i] = (o / l).astype(out.dtype)
        return jnp.where(lane == head, m + jnp.log(l), lse)

    lse, skip = lse_ref[...], 0
    for out in outs:
        lse = lax.fori_loop(0, out.shape[0], functools.partial(join, out=out, skip=skip), lse, unroll=2)
        skip += out.shape[0]
    lse_out[...] = lse if by_head else lse.T[:heads]


def merge_kernel(heads, early, order, far, here, here_late, lse_here, lse_got, *rest):
    *got, result, mine, theirs, out, sems, out_sems = rest
    copies = [pltpu.make_async_copy(here, mine, sems.at[0])]
    start = 0
    for i, part in enumerate(got):
        at = theirs.at[pl.ds(start, part.shape[0])]
        copies.append(pltpu.make_async_copy(part, at, sems.at[1 + i]))
        start += part.shape[0]
    for copy in copies:
        copy.start()
    a, b = lse_here[...], lse_got[...]
    b = jnp.concatenate([b, jnp.zeros((a.shape[1] - heads, a.shape[0]), b.dtype)], axis=0).T
    m = jnp.maximum(a, b)
    wa, wb = jnp.exp(a - m), jnp.exp(b - m)
    total = wa + wb
    wa, wb = wa / total, wb / total
    for copy in copies:
        copy.wait()

    def put(i, carry):
        mine[order[early + i]] = here_late[i]
        return carry

    lax.fori_loop(0, heads - early, put, 0)
    leaving = []
    for head in range(heads):
        joined = wa[:, head : head + 1] * mine[head]
        joined += wb[:, head : head + 1] * theirs[far[head]].astype(jnp.float32)
        out[:, columns(head)] = joined.astype(out.dtype)
        if head % 8 == 7:
            at = pl.ds((head - 7) * HEAD_DIM, 8 * HEAD_DIM)
            leaving.append(pltpu.make_async_copy(out.at[:, at], result.at[:, at], out_sems.at[head // 8]))
            leaving[-1].start()
    for copy in leaving:
        copy.wait()


def exchange(room, late, planes, queries, keys, values, mate_k, sends, takes, where):
    rows, features = queries.shape
    heads = features // HEAD_DIM
    early = heads - late
    f32, bf16, i32 = jnp.float32, jnp.bfloat16, jnp.int32
    shape = jax.ShapeDtypeStruct
    tile = (rows, HEAD_DIM)
    count = planes * OWN
    across = [(d, d ^ 2) for d in range(count)]
    beside = [(d, d ^ 1) for d in range(count)]
    barrier = lax.optimization_barrier

    mate_v = lax.ppermute(values, "seq", beside)
    far_q = lax.ppermute(queries, "seq", across)
    packed = pl.pallas_call(
        functools.partial(pack_kernel, heads, planes, room),
        out_shape=[shape((room, 2) + tile, bf16)] * (planes - 1),
        in_specs=[SMEM] * 2 + [VMEM] * 4,
        out_specs=[VMEM] * (planes - 1),
        compiler_params=params(8 + room // 4),
        cost_estimate=cost(4 << 30),
        name="pack",
    )(where, sends, keys, values, mate_k, mate_v)
    landed = [
        lax.ppermute(packed[step - 1], "seq", [(d, (d + OWN * step) % count) for d in range(count)])
        for step in range(1, planes)
    ]

    where, takes, *packed = barrier((where, takes, *packed))
    most_pairs = min(4 * (planes - 1) * room, HEAD_DIM)
    pair, begin, order, far = pl.pallas_call(
        functools.partial(plan_kernel, heads, planes, room),
        out_shape=[shape((n,), i32) for n in (most_pairs, heads + 1, heads, heads)],
        in_specs=[SMEM] * 2,
        out_specs=[SMEM] * 4,
        compiler_params=params(4),
        cost_estimate=cost(4 << 30),
        name="plan",
    )(where, takes)
    here, lse_here, turned = pl.pallas_call(
        functools.partial(here_kernel, heads),
        out_shape=[shape((heads,) + tile, f32), shape(tile, f32), shape((heads, HEAD_DIM, 2 * rows), bf16)],
        in_specs=[VMEM] * 5,
        out_specs=[VMEM] * 3,
        compiler_params=params(14),
        cost_estimate=cost(1 << 30),
        name="here",
    )(queries, keys, values, mate_k, mate_v)

    def attend_far(order, lse, start, parts):
        return pl.pallas_call(
            functools.partial(far_kernel, start),
            out_shape=[shape((n,) + tile, kind) for n, kind in parts] + [shape(tile, f32)],
            in_specs=[SMEM] + [VMEM] * 5,
            out_specs=[VMEM] * (len(parts) + 1),
            compiler_params=params(12),
            cost_estimate=cost(1 << 30),
            name="far",
        )(order, lse, far_q, turned, values, mate_v)

    second = min(early, thirds(late)[-1] + 1)
    parts = [n for n in (early - second, second) if n]
    lse_far, arrived = lse_here, []
    if early:
        sent, lse_far = attend_far(order, lse_far, 0, [(parts[0], bf16)])
        arrived = [lax.ppermute(sent, "seq", across)]
    kinds = [(n, bf16) for n in parts[1:]] + [(late, f32)]
    *sent, rest, lse_far = attend_far(order, lse_far, early - sum(parts[1:]), kinds)
    arrived += [lax.ppermute(x, "seq", across) for x in sent]
    *landed, rest, lse_far, first = barrier((*landed, rest, lse_far, arrived[:-1]))
    arrived = first + arrived[len(first) :]
    boxes = []
    for got in landed:
        boxes += [got, lax.ppermute(got, "seq", beside)]

    def add_extras(q, o, lse, by_head, parts):
        return pl.pallas_call(
            functools.partial(late_kernel, len(boxes), early, by_head, room),
            out_shape=[shape((n,) + tile, kind) for n, kind in parts] + [shape(tile if by_head else (heads, rows), f32)],
            in_specs=[SMEM] * 3 + [VMEM] * 3 + [HBM] * len(boxes),
            out_specs=[VMEM] * (len(parts) + 1),
            scratch_shapes=[
                pltpu.VMEM((len(boxes) * room, 2) + tile, bf16),
                pltpu.VMEM((most_pairs,) + tile, f32),
                pltpu.VMEM((most_pairs,) + tile, f32),
                pltpu.SemaphoreType.DMA((len(boxes),)),
            ],
            compiler_params=params(min(8 + 2 * room, 48)),
            cost_estimate=cost(1 << 20),
            name="late",
        )(order, pair, begin, q, o, lse, *boxes)

    *far_late, lse_far = add_extras(far_q, rest, lse_far, False, [(n, bf16) for n in thirds(late)])
    arrived = [lax.ppermute(lse_far, "seq", across), *arrived] + [lax.ppermute(x, "seq", across) for x in far_late]
    here_late, lse_here = add_extras(queries, here, lse_here, True, [(late, f32)])

    return pl.pallas_call(
        functools.partial(merge_kernel, heads, early),
        out_shape=pltpu.HBM((rows, features), bf16),
        in_specs=[SMEM] * 2 + [HBM] + [VMEM] * 3 + [HBM] * (len(arrived) - 1),
        out_specs=pl.BlockSpec(memory_space=pltpu.HBM),
        scratch_shapes=[
            pltpu.VMEM((heads,) + tile, f32),
            pltpu.VMEM((heads,) + tile, bf16),
            pltpu.VMEM((rows, features), bf16),
            pltpu.SemaphoreType.DMA((6,)),
            pltpu.SemaphoreType.DMA((heads // 8,)),
        ],
        compiler_params=params(12),
        cost_estimate=cost(1 << 20),
        name="merge",
    )(order, far, here, here_late, lse_here, *arrived)


def per_plane(queries, keys, values, kept, counts):
    heads, planes, slots = kept.shape
    device = lax.axis_index("seq").astype(jnp.int32)
    where = jnp.stack([device >> 2, device, (device >> 1) & 1, device & 1])
    beside = [(d, d ^ 1) for d in range(planes * OWN)]
    mate_k = lax.ppermute(keys, "seq", beside)
    shape = jax.ShapeDtypeStruct
    sends, takes, choice = pl.pallas_call(
        functools.partial(lists_kernel, planes, slots),
        out_shape=[
            shape((heads + 8, HEAD_DIM), jnp.int32),
            shape((planes * OWN, HEAD_DIM), jnp.int32),
            shape((1,), jnp.int32),
        ],
        in_specs=[SMEM] + [VMEM] * 2,
        out_specs=[VMEM] * 2 + [SMEM],
        compiler_params=params(60),
        name="lists",
    )(where, kept.transpose(1, 2, 0).reshape(planes * slots, heads), counts.T)
    sizes = SIZES + ((heads, heads),)
    return lax.switch(
        choice[0],
        [functools.partial(exchange, room, late, planes) for room, late in sizes],
        queries,
        keys,
        values,
        mate_k,
        sends,
        takes,
        where,
    )


def attend_tile(query_tile, key_tiles, value_tiles, slot_list, live_count):
    row_count = query_tile.shape[0]
    factor = 1.0 / query_tile.shape[1] ** 0.5
    start_state = (
        jnp.full((row_count,), -1e30, jnp.float32),
        jnp.zeros((row_count,), jnp.float32),
        jnp.zeros((row_count, query_tile.shape[1]), jnp.float32),
    )

    def advance(block_num, state_now):
        running, totals, numerator = state_now
        first = (block_num * GROUP).astype(jnp.int32)
        chosen = lax.dynamic_slice_in_dim(slot_list, first, GROUP)
        key_block = key_tiles[chosen].reshape(GROUP * KTILE, query_tile.shape[1])
        value_block = value_tiles[chosen].reshape(GROUP * KTILE, query_tile.shape[1])
        scores = jnp.dot(query_tile, key_block.T, preferred_element_type=jnp.float32) * factor
        live_mask = jnp.repeat(first + jnp.arange(GROUP, dtype=jnp.int32) < live_count, KTILE)
        scores = jnp.where(live_mask[None, :], scores, -1e30)
        new_max = jnp.maximum(running, jnp.max(scores, axis=1))
        rescale = jnp.exp(running - new_max)
        weights = jnp.exp(scores - new_max[:, None])
        totals = totals * rescale + jnp.sum(weights, axis=1)
        numerator = numerator * rescale[:, None] + jnp.dot(
            weights.astype(jnp.bfloat16), value_block, preferred_element_type=jnp.float32
        )
        return (new_max, totals, numerator)

    block_total = (live_count + GROUP - 1) // GROUP
    running, totals, numerator = lax.fori_loop(jnp.int32(0), block_total, advance, start_state)
    return (numerator / totals[:, None]).astype(jnp.bfloat16)


def per_device(queries, keys, values, kept, counts):
    local_rows, feature_count = queries.shape
    shards = lax.axis_size("seq")
    device = lax.axis_index("seq")
    head_count = feature_count // HEAD_DIM
    replicas = max(1, shards // head_count)
    slots_here = max(1, head_count // shards)
    total_rows = local_rows * shards
    tile_count = counts.shape[1]
    stacked = jnp.stack([queries, keys, values])
    copied = jnp.broadcast_to(
        stacked.reshape(3, local_rows, head_count, 1, HEAD_DIM),
        (3, local_rows, head_count, replicas, HEAD_DIM),
    )
    copied = copied.reshape(3, local_rows, head_count * replicas, HEAD_DIM)
    arrived = lax.all_to_all(copied, "seq", split_axis=2, concat_axis=1, tiled=True)
    head_data = arrived.transpose(2, 0, 1, 3)
    tiles_each = tile_count // replicas
    results = []
    for j in range(slots_here):
        global_slot = device * slots_here + j
        head_id = global_slot // replicas
        replica_id = global_slot % replicas
        slot_rows = lax.dynamic_index_in_dim(kept, head_id, 0, keepdims=False)
        count_row = lax.dynamic_index_in_dim(counts, head_id, 0, keepdims=False)
        all_queries = head_data[j, 0]
        key_tiles = head_data[j, 1].reshape(total_rows // KTILE, KTILE, HEAD_DIM)
        value_tiles = head_data[j, 2].reshape(total_rows // KTILE, KTILE, HEAD_DIM)
        rounds = jnp.arange(tiles_each, dtype=jnp.int32)
        tile_ids = replica_id * tiles_each + rounds

        def process(i, output):
            tile_id = tile_ids[i]
            query_tile = lax.dynamic_slice_in_dim(all_queries, tile_id * QTILE, QTILE, 0)
            finished = attend_tile(
                query_tile, key_tiles, value_tiles, slot_rows[tile_id], count_row[tile_id]
            )
            return lax.dynamic_update_slice_in_dim(output, finished, tile_id * QTILE, 0)

        results.append(
            lax.fori_loop(0, tiles_each, process, jnp.zeros((total_rows, HEAD_DIM), jnp.bfloat16))
        )
    gathered = jnp.stack(results, axis=1)
    returned = lax.all_to_all(gathered, "seq", split_axis=0, concat_axis=1, tiled=True)
    combined = (
        returned.reshape(local_rows, head_count, replicas, HEAD_DIM).astype(jnp.float32).sum(axis=2)
    )
    return combined.astype(jnp.bfloat16).reshape(local_rows, feature_count)


def solution(mesh):
    by_rows = P(("groups", "seq"), None)
    placed = (by_rows, by_rows, by_rows, P("groups", None, None), P("groups", None))

    def step(queries, keys, values, kept, counts):
        heads, planes, slots = kept.shape
        one_tile_each = queries.shape[0] == KTILE and mesh.shape["seq"] == planes * OWN
        fits = heads % 8 == 0 and heads <= 32 and heads * (slots - OWN) <= HEAD_DIM and planes == 4
        run = per_plane if one_tile_each and fits else per_device
        return run(queries, keys, values, kept, counts)

    return jax.shard_map(step, mesh=mesh, in_specs=placed, out_specs=by_rows, check_vma=False)
```

```python
import functools

import jax
import jax.numpy as jnp
from jax import lax
from jax.experimental import pallas as pl
from jax.experimental.pallas import tpu as pltpu
from jax.sharding import PartitionSpec as P

HEAD_DIM = 128
QTILE = 512
KTILE = 128
GROUP = 4
OWN = QTILE // KTILE
SIZES = ((5, 16), (6, 18), (7, 20))
MIB = 1 << 20
SMEM = pl.BlockSpec(memory_space=pltpu.SMEM)
VMEM = pl.BlockSpec(memory_space=pltpu.VMEM)
HBM = pl.BlockSpec(memory_space=pl.ANY)


def params(mib):
    return pltpu.CompilerParams(vmem_limit_bytes=mib * MIB)


def cost(flops):
    return pl.CostEstimate(flops=flops, bytes_accessed=8 << 20, transcendentals=0)


def thirds(late):
    return late // 3, late // 3, late - 2 * (late // 3)


def columns(head):
    if isinstance(head, int):
        return pl.ds(head * HEAD_DIM, HEAD_DIM)
    return pl.ds(pl.multiple_of(head * HEAD_DIM, HEAD_DIM), HEAD_DIM)


def dot(a, b):
    return jnp.dot(a, b, preferred_element_type=jnp.float32)


def lists_kernel(planes, slots, where, kept, counts, sends, takes, choice):
    plane, pair = where[0], where[1] >> 1
    heads = kept.shape[1]
    shape = (planes * OWN, heads)
    half = (planes * OWN // 2, heads)
    ids = lax.broadcasted_iota(jnp.int32, shape, 0)
    chips = lax.broadcasted_iota(jnp.int32, half, 0)
    bit = jnp.left_shift(jnp.int32(1), lax.broadcasted_iota(jnp.int32, shape, 1))
    lane = lax.broadcasted_iota(jnp.int32, (1, HEAD_DIM), 1)
    most = jnp.zeros((planes * OWN // 2, 1), jnp.int32)
    touched = jnp.zeros((1, 1), jnp.int32)
    taken = jnp.zeros(shape, jnp.int32)
    wanted = []
    for t in range(planes):
        hits = jnp.zeros(shape, jnp.int32)
        per_chip = jnp.zeros(half, jnp.int32)
        for j in range(OWN, slots):
            tile = kept[t * slots + j : t * slots + j + 1, :]
            live = counts[t : t + 1, :] > j
            hits = jnp.where((ids == tile) & live, 1, hits)
            per_chip = per_chip + jnp.where((chips == (tile >> 1)) & live, 1, 0)
        most = jnp.maximum(most, jnp.sum(per_chip, axis=1, keepdims=True))
        for side in range(2):
            some = jnp.max(jnp.where(((ids >> 1) & 1) == side, hits, 0), axis=0, keepdims=True)
            touched = jnp.maximum(touched, jnp.sum(some, axis=1, keepdims=True))
        bits = hits * bit
        for turn in range(2):
            wanted.append(jnp.sum(jnp.where(ids == 2 * pair + turn, hits, 0), axis=0, keepdims=True))
        taken = jnp.where(plane == t, bits, taken)
    square = (heads, heads)
    at, head = lax.broadcasted_iota(jnp.int32, square, 0), lax.broadcasted_iota(jnp.int32, square, 1)
    before = jnp.where(at < head, 1.0, 0.0)
    named = jnp.concatenate(wanted, axis=0)
    rank = dot(named.astype(jnp.float32), before).astype(jnp.int32)
    rows = jnp.zeros((heads, HEAD_DIM), jnp.int32)
    count = jnp.zeros((1, HEAD_DIM), jnp.int32)
    for i in range(2 * planes):
        here = (at == rank[i : i + 1, :]) & (named[i : i + 1, :] == 1)
        rows = jnp.where(lane == i, jnp.sum(jnp.where(here, head, 0), axis=1, keepdims=True), rows)
        count = jnp.where(lane == i, jnp.sum(named[i : i + 1, :], axis=1, keepdims=True), count)
    sends[0:heads, :] = rows
    sends[heads : heads + 8, :] = jnp.broadcast_to(count, (8, HEAD_DIM))
    takes[...] = jnp.where(
        lane == 0,
        jnp.sum(taken, axis=1, keepdims=True),
        jnp.sum(jnp.where(taken != 0, 1, 0), axis=1, keepdims=True),
    )
    top, wide = jnp.max(most), jnp.max(touched)
    index = jnp.int32(len(SIZES))
    for i, (room, late) in reversed(list(enumerate(SIZES))):
        index = jnp.where((top <= 2 * room) & (wide <= late), i, index)
    choice[0] = index


def pack_kernel(heads, planes, room, where, sends, k_ref, v_ref, mate_k, mate_v, *outs):
    plane, core = where[0], where[3]
    for step, out in enumerate(outs, 1):
        lane = 2 * lax.rem(plane + step, planes)
        first, both = sends[heads, lane], sends[heads, lane] + sends[heads, lane + 1]

        def take(slot, carry, out=out, lane=lane, first=first):
            at = core * room + slot
            turn = jnp.where(at >= first, 1, 0)
            head = sends[at - turn * first, lane + turn]

            @pl.when(core == turn)
            def _():
                out[slot, 0] = k_ref[:, columns(head)].T
                out[slot, 1] = v_ref[:, columns(head)]

            @pl.when(core != turn)
            def _():
                out[slot, 0] = mate_k[:, columns(head)].T
                out[slot, 1] = mate_v[:, columns(head)]

            return carry

        lax.fori_loop(0, jnp.clip(both - core * room, 0, room), take, 0)


def plan_kernel(heads, planes, room, where, takes, pair, begin, order, far):
    plane, side, core = where[0], where[2], where[3]
    near, other, starts = [], [], []
    for step in range(1, planes):
        source = lax.rem(plane - step + planes, planes) * OWN
        for turn in range(2):
            near.append(takes[source + 2 * side + turn, 0])
            starts.append(takes[source + 2 * side, 1] if turn else jnp.int32(0))
            other.append(takes[source + 2 * (1 - side) + turn, 0])
    any_near = functools.reduce(jnp.bitwise_or, near)
    any_other = functools.reduce(jnp.bitwise_or, other)

    def held(bits):
        return lax.fori_loop(0, heads, lambda h, n: n + ((bits >> h) & 1), jnp.int32(0))

    def put(head, state):
        a, b, c, d, pairs, *used = state
        none, far_none = 1 - ((any_near >> head) & 1), 1 - ((any_other >> head) & 1)
        at = jnp.where(none == 1, a, b)
        order[at] = head
        far[head] = jnp.where(far_none == 1, c, d)
        begin[head] = pairs
        for i, bits in enumerate(near):
            hit = (bits >> head) & 1
            sender = jnp.where(used[i] >= room, 1, 0)
            box = i // 2 * 2 + jnp.where(sender == core, 0, 1)

            @pl.when(hit == 1)
            def _(i=i, pairs=pairs, used=used, sender=sender, box=box):
                pair[pairs] = head * 4096 + box * room + used[i] - sender * room

            pairs = pairs + hit
            used = used[:i] + [used[i] + hit] + used[i + 1 :]
        return (a + none, b + 1 - none, c + far_none, d + 1 - far_none, pairs, *used)

    zero = jnp.int32(0)
    first = (zero, heads - held(any_near), zero, heads - held(any_other), zero, *starts)
    begin[heads] = lax.fori_loop(0, heads, put, first)[4]


def soften(q, k_t, v):
    s = dot(q, k_t) * (1.0 / HEAD_DIM**0.5)
    m = jnp.max(s, axis=1, keepdims=True)
    w = jnp.exp(s - m)
    l = jnp.sum(w, axis=1, keepdims=True)
    return dot(w.astype(jnp.bfloat16), v) / l, m + jnp.log(l)


def here_kernel(heads, q_ref, k_ref, v_ref, mate_k, mate_v, out, lse_out, turned):
    lane = lax.broadcasted_iota(jnp.int32, lse_out.shape, 1)

    def attend(head, lse):
        at = columns(head)
        k_t = jnp.concatenate([k_ref[:, at].T, mate_k[:, at].T], axis=1)
        turned[head] = k_t
        v = jnp.concatenate([v_ref[:, at], mate_v[:, at]], axis=0)
        o, new = soften(q_ref[:, at], k_t, v)
        out[head] = o
        return jnp.where(lane == head, new, lse)

    lse_out[...] = lax.fori_loop(0, heads, attend, jnp.zeros(lse_out.shape, jnp.float32), unroll=4)


def far_kernel(start, order, lse_ref, q_ref, turned, v_ref, mate_v, *outs):
    *parts, lse_out = outs
    lane = lax.broadcasted_iota(jnp.int32, lse_out.shape, 1)
    lse = lse_ref[...]
    for part in parts:

        def attend(i, lse, part=part, start=start):
            head = order[start + i]
            at = columns(head)
            v = jnp.concatenate([v_ref[:, at], mate_v[:, at]], axis=0)
            o, new = soften(q_ref[:, at], turned[head], v)
            part[i] = o.astype(part.dtype)
            return jnp.where(lane == head, new, lse)

        lse = lax.fori_loop(0, part.shape[0], attend, lse, unroll=4)
        start += part.shape[0]
    lse_out[...] = lse


def late_kernel(sends, early, by_head, room, order, pair, begin, q_ref, o_ref, lse_ref, *rest):
    boxes, rest = rest[: sends], rest[sends:]
    *outs, lse_out, tiles, partial, level, sems = rest
    copies = [
        pltpu.make_async_copy(box, tiles.at[pl.ds(b * room, room)], sems.at[b]) for b, box in enumerate(boxes)
    ]
    for copy in copies:
        copy.start()
    heads = order.shape[0]
    shape = lse_ref.shape
    most = partial.shape[0]
    lane = lax.broadcasted_iota(jnp.int32, shape, 1)
    total = begin[heads]
    for copy in copies:
        copy.wait()

    if by_head:
        outs[0][...] = o_ref[...]
    wide = not by_head and heads - early <= 18
    width = 8 if wide else 4

    def several(i, carry):
        for j in range(width):
            at = jnp.minimum(width * i + j, total - 1)
            code = pair[at]
            head, tile = code >> 12, code & 4095
            o, new = soften(q_ref[:, columns(head)], tiles[tile, 0], tiles[tile, 1])
            partial[at] = o
            level[at] = jnp.broadcast_to(new, shape)
        return carry

    lax.fori_loop(0, lax.div(total + width - 1, width), several, 0)

    def join(i, lse, out, skip):
        head = order[early + skip + i]
        start, end = begin[head], begin[head + 1]
        base = jnp.sum(jnp.where(lane == head, lse_ref[...], 0.0), axis=1, keepdims=True)
        base = jnp.broadcast_to(base, shape)
        spots = [jnp.minimum(start + e, most - 1) for e in range(4)]
        levels = [jnp.where(start + e < end, level[p], -1e30) for e, p in enumerate(spots)]
        m = functools.reduce(jnp.maximum, levels, base)
        l = jnp.exp(base - m)
        o = l * o_ref[head if by_head else skip + i]
        for e, p in enumerate(spots):
            w = jnp.exp(levels[e] - m)
            l = l + w
            o = o + jnp.where(start + e < end, w * partial[p], 0.0)
        out[head if by_head else i] = (o / l).astype(out.dtype)
        return jnp.where(lane == head, m + jnp.log(l), lse)

    lse, skip = lse_ref[...], 0
    for out in outs:
        count = heads - early if by_head else out.shape[0]
        unroll = count if wide else 2
        lse = lax.fori_loop(0, count, functools.partial(join, out=out, skip=skip), lse, unroll=unroll)
        skip += out.shape[0]
    lse_out[...] = lse if by_head else lse.T[:heads]


def merge_kernel(heads, far, mine, lse_here, lse_got, *rest):
    *got, result, theirs, out, sems, out_sems = rest
    copies, start = [], 0
    for i, part in enumerate(got):
        copies.append(pltpu.make_async_copy(part, theirs.at[pl.ds(start, part.shape[0])], sems.at[i]))
        start += part.shape[0]
    for copy in copies:
        copy.start()
    a, b = lse_here[...], lse_got[...]
    b = jnp.concatenate([b, jnp.zeros((a.shape[1] - heads, a.shape[0]), b.dtype)], axis=0).T
    m = jnp.maximum(a, b)
    wa, wb = jnp.exp(a - m), jnp.exp(b - m)
    total = wa + wb
    wa, wb = wa / total, wb / total
    for copy in copies:
        copy.wait()

    leaving = []
    for head in range(heads):
        joined = wa[:, head : head + 1] * mine[head]
        joined += wb[:, head : head + 1] * theirs[far[head]].astype(jnp.float32)
        out[:, columns(head)] = joined.astype(out.dtype)
        if head % 8 == 7:
            at = pl.ds((head - 7) * HEAD_DIM, 8 * HEAD_DIM)
            leaving.append(pltpu.make_async_copy(out.at[:, at], result.at[:, at], out_sems.at[head // 8]))
            leaving[-1].start()
    for copy in leaving:
        copy.wait()


def exchange(room, late, planes, queries, keys, values, mate_k, sends, takes, where):
    rows, features = queries.shape
    heads = features // HEAD_DIM
    early = heads - late
    f32, bf16, i32 = jnp.float32, jnp.bfloat16, jnp.int32
    shape = jax.ShapeDtypeStruct
    tile = (rows, HEAD_DIM)
    count = planes * OWN
    across = [(d, d ^ 2) for d in range(count)]
    beside = [(d, d ^ 1) for d in range(count)]
    barrier = lax.optimization_barrier

    mate_v = lax.ppermute(values, "seq", beside)
    far_q = lax.ppermute(queries, "seq", across)
    packed = pl.pallas_call(
        functools.partial(pack_kernel, heads, planes, room),
        out_shape=[shape((room, 2) + tile, bf16)] * (planes - 1),
        in_specs=[SMEM] * 2 + [VMEM] * 4,
        out_specs=[VMEM] * (planes - 1),
        compiler_params=params(8 + room // 4),
        cost_estimate=cost(4 << 30),
        name="pack",
    )(where, sends, keys, values, mate_k, mate_v)
    landed = [
        lax.ppermute(packed[step - 1], "seq", [(d, (d + OWN * step) % count) for d in range(count)])
        for step in range(1, planes)
    ]

    where, takes, *packed = barrier((where, takes, *packed))
    most_pairs = min(4 * (planes - 1) * room, HEAD_DIM)
    pair, begin, order, far = pl.pallas_call(
        functools.partial(plan_kernel, heads, planes, room),
        out_shape=[shape((n,), i32) for n in (most_pairs, heads + 1, heads, heads)],
        in_specs=[SMEM] * 2,
        out_specs=[SMEM] * 4,
        compiler_params=params(4),
        cost_estimate=cost(4 << 30),
        name="plan",
    )(where, takes)
    here, lse_here, turned = pl.pallas_call(
        functools.partial(here_kernel, heads),
        out_shape=[shape((heads,) + tile, f32), shape(tile, f32), shape((heads, HEAD_DIM, 2 * rows), bf16)],
        in_specs=[VMEM] * 5,
        out_specs=[VMEM] * 3,
        compiler_params=params(14),
        cost_estimate=cost(1 << 30),
        name="here",
    )(queries, keys, values, mate_k, mate_v)

    def attend_far(order, lse, start, parts):
        return pl.pallas_call(
            functools.partial(far_kernel, start),
            out_shape=[shape((n,) + tile, kind) for n, kind in parts] + [shape(tile, f32)],
            in_specs=[SMEM] + [VMEM] * 5,
            out_specs=[VMEM] * (len(parts) + 1),
            compiler_params=params(12),
            cost_estimate=cost(1 << 30),
            name="far",
        )(order, lse, far_q, turned, values, mate_v)

    second = min(early, thirds(late)[-1] + 1)
    parts = [n for n in (early - second, second) if n]
    lse_far, arrived = lse_here, []
    if early:
        sent, lse_far = attend_far(order, lse_far, 0, [(parts[0], bf16)])
        arrived = [lax.ppermute(sent, "seq", across)]
    kinds = [(n, bf16) for n in parts[1:]] + [(late, f32)]
    *sent, rest, lse_far = attend_far(order, lse_far, early - sum(parts[1:]), kinds)
    arrived += [lax.ppermute(x, "seq", across) for x in sent]
    *landed, rest, lse_far, first = barrier((*landed, rest, lse_far, arrived[:-1]))
    arrived = first + arrived[len(first) :]
    boxes = []
    for got in landed:
        boxes += [got, lax.ppermute(got, "seq", beside)]

    def add_extras(q, o, lse, by_head, parts):
        return pl.pallas_call(
            functools.partial(late_kernel, len(boxes), early, by_head, room),
            out_shape=[shape((n,) + tile, kind) for n, kind in parts] + [shape(tile if by_head else (heads, rows), f32)],
            in_specs=[SMEM] * 3 + [VMEM] * 3 + [HBM] * len(boxes),
            out_specs=[VMEM] * (len(parts) + 1),
            scratch_shapes=[
                pltpu.VMEM((len(boxes) * room, 2) + tile, bf16),
                pltpu.VMEM((most_pairs,) + tile, f32),
                pltpu.VMEM((most_pairs,) + tile, f32),
                pltpu.SemaphoreType.DMA((len(boxes),)),
            ],
            compiler_params=params(min(8 + 2 * room, 48)),
            cost_estimate=cost(1 << 20),
            name="late",
        )(order, pair, begin, q, o, lse, *boxes)

    *far_late, lse_far = add_extras(far_q, rest, lse_far, False, [(n, bf16) for n in thirds(late)])
    arrived = [lax.ppermute(lse_far, "seq", across), *arrived] + [lax.ppermute(x, "seq", across) for x in far_late]
    here, lse_here = add_extras(queries, here, lse_here, True, [(heads, f32)])

    return pl.pallas_call(
        functools.partial(merge_kernel, heads),
        out_shape=pltpu.HBM((rows, features), bf16),
        in_specs=[SMEM] + [VMEM] * 3 + [HBM] * (len(arrived) - 1),
        out_specs=pl.BlockSpec(memory_space=pltpu.HBM),
        scratch_shapes=[
            pltpu.VMEM((heads,) + tile, bf16),
            pltpu.VMEM((rows, features), bf16),
            pltpu.SemaphoreType.DMA((len(arrived) - 1,)),
            pltpu.SemaphoreType.DMA((heads // 8,)),
        ],
        compiler_params=params(12),
        cost_estimate=cost(1 << 20),
        name="merge",
    )(far, here, lse_here, *arrived)


def per_plane(queries, keys, values, kept, counts):
    heads, planes, slots = kept.shape
    device = lax.axis_index("seq").astype(jnp.int32)
    where = jnp.stack([device >> 2, device, (device >> 1) & 1, device & 1])
    beside = [(d, d ^ 1) for d in range(planes * OWN)]
    mate_k = lax.ppermute(keys, "seq", beside)
    shape = jax.ShapeDtypeStruct
    sends, takes, choice = pl.pallas_call(
        functools.partial(lists_kernel, planes, slots),
        out_shape=[
            shape((heads + 8, HEAD_DIM), jnp.int32),
            shape((planes * OWN, HEAD_DIM), jnp.int32),
            shape((1,), jnp.int32),
        ],
        in_specs=[SMEM] + [VMEM] * 2,
        out_specs=[VMEM] * 2 + [SMEM],
        compiler_params=params(60),
        name="lists",
    )(where, kept.transpose(1, 2, 0).reshape(planes * slots, heads), counts.T)
    sizes = SIZES + ((heads, heads),)
    return lax.switch(
        choice[0],
        [functools.partial(exchange, room, late, planes) for room, late in sizes],
        queries,
        keys,
        values,
        mate_k,
        sends,
        takes,
        where,
    )


def attend_tile(query_tile, key_tiles, value_tiles, slot_list, live_count):
    row_count = query_tile.shape[0]
    factor = 1.0 / query_tile.shape[1] ** 0.5
    start_state = (
        jnp.full((row_count,), -1e30, jnp.float32),
        jnp.zeros((row_count,), jnp.float32),
        jnp.zeros((row_count, query_tile.shape[1]), jnp.float32),
    )

    def advance(block_num, state_now):
        running, totals, numerator = state_now
        first = (block_num * GROUP).astype(jnp.int32)
        chosen = lax.dynamic_slice_in_dim(slot_list, first, GROUP)
        key_block = key_tiles[chosen].reshape(GROUP * KTILE, query_tile.shape[1])
        value_block = value_tiles[chosen].reshape(GROUP * KTILE, query_tile.shape[1])
        scores = jnp.dot(query_tile, key_block.T, preferred_element_type=jnp.float32) * factor
        live_mask = jnp.repeat(first + jnp.arange(GROUP, dtype=jnp.int32) < live_count, KTILE)
        scores = jnp.where(live_mask[None, :], scores, -1e30)
        new_max = jnp.maximum(running, jnp.max(scores, axis=1))
        rescale = jnp.exp(running - new_max)
        weights = jnp.exp(scores - new_max[:, None])
        totals = totals * rescale + jnp.sum(weights, axis=1)
        numerator = numerator * rescale[:, None] + jnp.dot(
            weights.astype(jnp.bfloat16), value_block, preferred_element_type=jnp.float32
        )
        return (new_max, totals, numerator)

    block_total = (live_count + GROUP - 1) // GROUP
    running, totals, numerator = lax.fori_loop(jnp.int32(0), block_total, advance, start_state)
    return (numerator / totals[:, None]).astype(jnp.bfloat16)


def per_device(queries, keys, values, kept, counts):
    local_rows, feature_count = queries.shape
    shards = lax.axis_size("seq")
    device = lax.axis_index("seq")
    head_count = feature_count // HEAD_DIM
    replicas = max(1, shards // head_count)
    slots_here = max(1, head_count // shards)
    total_rows = local_rows * shards
    tile_count = counts.shape[1]
    stacked = jnp.stack([queries, keys, values])
    copied = jnp.broadcast_to(
        stacked.reshape(3, local_rows, head_count, 1, HEAD_DIM),
        (3, local_rows, head_count, replicas, HEAD_DIM),
    )
    copied = copied.reshape(3, local_rows, head_count * replicas, HEAD_DIM)
    arrived = lax.all_to_all(copied, "seq", split_axis=2, concat_axis=1, tiled=True)
    head_data = arrived.transpose(2, 0, 1, 3)
    tiles_each = tile_count // replicas
    results = []
    for j in range(slots_here):
        global_slot = device * slots_here + j
        head_id = global_slot // replicas
        replica_id = global_slot % replicas
        slot_rows = lax.dynamic_index_in_dim(kept, head_id, 0, keepdims=False)
        count_row = lax.dynamic_index_in_dim(counts, head_id, 0, keepdims=False)
        all_queries = head_data[j, 0]
        key_tiles = head_data[j, 1].reshape(total_rows // KTILE, KTILE, HEAD_DIM)
        value_tiles = head_data[j, 2].reshape(total_rows // KTILE, KTILE, HEAD_DIM)
        rounds = jnp.arange(tiles_each, dtype=jnp.int32)
        tile_ids = replica_id * tiles_each + rounds

        def process(i, output):
            tile_id = tile_ids[i]
            query_tile = lax.dynamic_slice_in_dim(all_queries, tile_id * QTILE, QTILE, 0)
            finished = attend_tile(
                query_tile, key_tiles, value_tiles, slot_rows[tile_id], count_row[tile_id]
            )
            return lax.dynamic_update_slice_in_dim(output, finished, tile_id * QTILE, 0)

        results.append(
            lax.fori_loop(0, tiles_each, process, jnp.zeros((total_rows, HEAD_DIM), jnp.bfloat16))
        )
    gathered = jnp.stack(results, axis=1)
    returned = lax.all_to_all(gathered, "seq", split_axis=0, concat_axis=1, tiled=True)
    combined = (
        returned.reshape(local_rows, head_count, replicas, HEAD_DIM).astype(jnp.float32).sum(axis=2)
    )
    return combined.astype(jnp.bfloat16).reshape(local_rows, feature_count)


def solution(mesh):
    by_rows = P(("groups", "seq"), None)
    placed = (by_rows, by_rows, by_rows, P("groups", None, None), P("groups", None))

    def step(queries, keys, values, kept, counts):
        heads, planes, slots = kept.shape
        one_tile_each = queries.shape[0] == KTILE and mesh.shape["seq"] == planes * OWN
        fits = heads % 8 == 0 and heads <= 32 and heads * (slots - OWN) <= HEAD_DIM and planes == 4
        run = per_plane if one_tile_each and fits else per_device
        return run(queries, keys, values, kept, counts)

    return jax.shard_map(step, mesh=mesh, in_specs=placed, out_specs=by_rows, check_vma=False)
```

```python
import functools

import jax
import jax.numpy as jnp
from jax import lax
from jax.experimental import pallas as pl
from jax.experimental.pallas import tpu as pltpu
from jax.sharding import PartitionSpec as P

HEAD_DIM = 128
QTILE = 512
KTILE = 128
GROUP = 4
OWN = QTILE // KTILE
SIZES = ((5, 16), (6, 18), (7, 20))
MIB = 1 << 20
SMEM = pl.BlockSpec(memory_space=pltpu.SMEM)
VMEM = pl.BlockSpec(memory_space=pltpu.VMEM)
HBM = pl.BlockSpec(memory_space=pl.ANY)


def params(mib):
    return pltpu.CompilerParams(vmem_limit_bytes=mib * MIB)


def cost(flops):
    return pl.CostEstimate(flops=flops, bytes_accessed=8 << 20, transcendentals=0)


def thirds(late):
    return late // 3, late // 3, late - 2 * (late // 3)


def columns(head):
    if isinstance(head, int):
        return pl.ds(head * HEAD_DIM, HEAD_DIM)
    return pl.ds(pl.multiple_of(head * HEAD_DIM, HEAD_DIM), HEAD_DIM)


def dot(a, b):
    return jnp.dot(a, b, preferred_element_type=jnp.float32)


def lists_kernel(planes, slots, where, kept, counts, sends, takes, choice):
    plane, pair = where[0], where[1] >> 1
    heads = kept.shape[1]
    shape = (planes * OWN, heads)
    half = (planes * OWN // 2, heads)
    ids = lax.broadcasted_iota(jnp.int32, shape, 0)
    chips = lax.broadcasted_iota(jnp.int32, half, 0)
    bit = jnp.left_shift(jnp.int32(1), lax.broadcasted_iota(jnp.int32, shape, 1))
    lane = lax.broadcasted_iota(jnp.int32, (1, HEAD_DIM), 1)
    most = jnp.zeros((planes * OWN // 2, 1), jnp.int32)
    touched = jnp.zeros((1, 1), jnp.int32)
    taken = jnp.zeros(shape, jnp.int32)
    wanted = []
    for t in range(planes):
        hits = jnp.zeros(shape, jnp.int32)
        per_chip = jnp.zeros(half, jnp.int32)
        for j in range(OWN, slots):
            tile = kept[t * slots + j : t * slots + j + 1, :]
            live = counts[t : t + 1, :] > j
            hits = jnp.where((ids == tile) & live, 1, hits)
            per_chip = per_chip + jnp.where((chips == (tile >> 1)) & live, 1, 0)
        most = jnp.maximum(most, jnp.sum(per_chip, axis=1, keepdims=True))
        for side in range(2):
            some = jnp.max(jnp.where(((ids >> 1) & 1) == side, hits, 0), axis=0, keepdims=True)
            touched = jnp.maximum(touched, jnp.sum(some, axis=1, keepdims=True))
        bits = hits * bit
        for turn in range(2):
            wanted.append(jnp.sum(jnp.where(ids == 2 * pair + turn, hits, 0), axis=0, keepdims=True))
        taken = jnp.where(plane == t, bits, taken)
    square = (heads, heads)
    at, head = lax.broadcasted_iota(jnp.int32, square, 0), lax.broadcasted_iota(jnp.int32, square, 1)
    before = jnp.where(at < head, 1.0, 0.0)
    named = jnp.concatenate(wanted, axis=0)
    rank = dot(named.astype(jnp.float32), before).astype(jnp.int32)
    rows = jnp.zeros((heads, HEAD_DIM), jnp.int32)
    count = jnp.zeros((1, HEAD_DIM), jnp.int32)
    for i in range(2 * planes):
        here = (at == rank[i : i + 1, :]) & (named[i : i + 1, :] == 1)
        rows = jnp.where(lane == i, jnp.sum(jnp.where(here, head, 0), axis=1, keepdims=True), rows)
        count = jnp.where(lane == i, jnp.sum(named[i : i + 1, :], axis=1, keepdims=True), count)
    sends[0:heads, :] = rows
    sends[heads : heads + 8, :] = jnp.broadcast_to(count, (8, HEAD_DIM))
    takes[...] = jnp.where(
        lane == 0,
        jnp.sum(taken, axis=1, keepdims=True),
        jnp.sum(jnp.where(taken != 0, 1, 0), axis=1, keepdims=True),
    )
    top, wide = jnp.max(most), jnp.max(touched)
    index = jnp.int32(len(SIZES))
    for i, (room, late) in reversed(list(enumerate(SIZES))):
        index = jnp.where((top <= 2 * room) & (wide <= late), i, index)
    choice[0] = index


def pack_kernel(heads, planes, room, where, sends, k_ref, v_ref, mate_k, mate_v, *outs):
    plane, core = where[0], where[3]
    for step, out in enumerate(outs, 1):
        lane = 2 * lax.rem(plane + step, planes)
        first, both = sends[heads, lane], sends[heads, lane] + sends[heads, lane + 1]

        def take(slot, carry, out=out, lane=lane, first=first):
            at = core * room + slot
            turn = jnp.where(at >= first, 1, 0)
            head = sends[at - turn * first, lane + turn]

            @pl.when(core == turn)
            def _():
                out[slot, 0] = k_ref[:, columns(head)].T
                out[slot, 1] = v_ref[:, columns(head)]

            @pl.when(core != turn)
            def _():
                out[slot, 0] = mate_k[:, columns(head)].T
                out[slot, 1] = mate_v[:, columns(head)]

            return carry

        lax.fori_loop(0, jnp.clip(both - core * room, 0, room), take, 0)


def plan_kernel(heads, planes, room, where, takes, pair, begin, order, far):
    plane, side, core = where[0], where[2], where[3]
    near, other, starts = [], [], []
    for step in range(1, planes):
        source = lax.rem(plane - step + planes, planes) * OWN
        for turn in range(2):
            near.append(takes[source + 2 * side + turn, 0])
            starts.append(takes[source + 2 * side, 1] if turn else jnp.int32(0))
            other.append(takes[source + 2 * (1 - side) + turn, 0])
    any_near = functools.reduce(jnp.bitwise_or, near)
    any_other = functools.reduce(jnp.bitwise_or, other)

    def held(bits):
        return lax.fori_loop(0, heads, lambda h, n: n + ((bits >> h) & 1), jnp.int32(0))

    def put(head, state):
        a, b, c, d, pairs, *used = state
        none, far_none = 1 - ((any_near >> head) & 1), 1 - ((any_other >> head) & 1)
        at = jnp.where(none == 1, a, b)
        order[at] = head
        far[jnp.where(far_none == 1, c, d)] = head
        begin[head] = pairs
        for i, bits in enumerate(near):
            hit = (bits >> head) & 1
            sender = jnp.where(used[i] >= room, 1, 0)
            box = i // 2 * 2 + jnp.where(sender == core, 0, 1)

            @pl.when(hit == 1)
            def _(i=i, pairs=pairs, used=used, sender=sender, box=box):
                pair[pairs] = head * 4096 + box * room + used[i] - sender * room

            pairs = pairs + hit
            used = used[:i] + [used[i] + hit] + used[i + 1 :]
        return (a + none, b + 1 - none, c + far_none, d + 1 - far_none, pairs, *used)

    zero = jnp.int32(0)
    first = (zero, heads - held(any_near), zero, heads - held(any_other), zero, *starts)
    begin[heads] = lax.fori_loop(0, heads, put, first)[4]


def soften(q, k_t, v):
    s = dot(q, k_t) * (1.0 / HEAD_DIM**0.5)
    m = jnp.max(s, axis=1, keepdims=True)
    w = jnp.exp(s - m)
    l = jnp.sum(w, axis=1, keepdims=True)
    return dot(w.astype(jnp.bfloat16), v) / l, m + jnp.log(l)


def here_kernel(heads, q_ref, k_ref, v_ref, mate_k, mate_v, out, lse_out, turned):
    lane = lax.broadcasted_iota(jnp.int32, lse_out.shape, 1)

    def attend(head, lse):
        at = columns(head)
        k_t = jnp.concatenate([k_ref[:, at].T, mate_k[:, at].T], axis=1)
        turned[head] = k_t
        v = jnp.concatenate([v_ref[:, at], mate_v[:, at]], axis=0)
        o, new = soften(q_ref[:, at], k_t, v)
        out[head] = o
        return jnp.where(lane == head, new, lse)

    lse_out[...] = lax.fori_loop(0, heads, attend, jnp.zeros(lse_out.shape, jnp.float32), unroll=4)


def far_kernel(start, order, lse_ref, q_ref, turned, v_ref, mate_v, *outs):
    *parts, lse_out = outs
    lane = lax.broadcasted_iota(jnp.int32, lse_out.shape, 1)
    lse = lse_ref[...]
    for part in parts:

        def attend(i, lse, part=part, start=start):
            head = order[start + i]
            at = columns(head)
            v = jnp.concatenate([v_ref[:, at], mate_v[:, at]], axis=0)
            o, new = soften(q_ref[:, at], turned[head], v)
            part[i] = o.astype(part.dtype)
            return jnp.where(lane == head, new, lse)

        lse = lax.fori_loop(0, part.shape[0], attend, lse, unroll=4)
        start += part.shape[0]
    lse_out[...] = lse


def late_kernel(sends, early, by_head, room, order, pair, begin, q_ref, o_ref, lse_ref, *rest):
    boxes, rest = rest[: sends], rest[sends:]
    *outs, lse_out, tiles, partial, level, sems = rest
    copies = [
        pltpu.make_async_copy(box, tiles.at[pl.ds(b * room, room)], sems.at[b]) for b, box in enumerate(boxes)
    ]
    for copy in copies:
        copy.start()
    heads = order.shape[0]
    shape = lse_ref.shape
    most = partial.shape[0]
    lane = lax.broadcasted_iota(jnp.int32, shape, 1)
    total = begin[heads]
    for copy in copies:
        copy.wait()

    if by_head:
        outs[0][...] = o_ref[...]
    wide = not by_head and heads - early <= 18
    width = 8 if wide else 4

    def several(i, carry):
        for j in range(width):
            at = jnp.minimum(width * i + j, total - 1)
            code = pair[at]
            head, tile = code >> 12, code & 4095
            o, new = soften(q_ref[:, columns(head)], tiles[tile, 0], tiles[tile, 1])
            partial[at] = o
            level[at] = jnp.broadcast_to(new, shape)
        return carry

    lax.fori_loop(0, lax.div(total + width - 1, width), several, 0)

    def join(i, lse, out, skip):
        head = order[early + skip + i]
        start, end = begin[head], begin[head + 1]
        base = jnp.sum(jnp.where(lane == head, lse_ref[...], 0.0), axis=1, keepdims=True)
        base = jnp.broadcast_to(base, shape)
        spots = [jnp.minimum(start + e, most - 1) for e in range(4)]
        levels = [jnp.where(start + e < end, level[p], -1e30) for e, p in enumerate(spots)]
        m = functools.reduce(jnp.maximum, levels, base)
        l = jnp.exp(base - m)
        o = l * o_ref[head if by_head else skip + i]
        for e, p in enumerate(spots):
            w = jnp.exp(levels[e] - m)
            l = l + w
            o = o + jnp.where(start + e < end, w * partial[p], 0.0)
        out[head if by_head else i] = (o / l).astype(out.dtype)
        return jnp.where(lane == head, m + jnp.log(l), lse)

    lse, skip = lse_ref[...], 0
    for out in outs:
        count = heads - early if by_head else out.shape[0]
        unroll = count if wide else 2
        lse = lax.fori_loop(0, count, functools.partial(join, out=out, skip=skip), lse, unroll=unroll)
        skip += out.shape[0]
    lse_out[...] = lse if by_head else lse.T[:heads]


def merge_kernel(far, mine, lse_here, lse_got, *rest):
    *got, result, out, sems = rest
    a, b = lse_here[...], lse_got[...]
    heads = b.shape[0]
    b = jnp.concatenate([b, jnp.zeros((a.shape[1] - heads, a.shape[0]), b.dtype)], axis=0).T
    m = jnp.maximum(a, b)
    wa, wb = jnp.exp(a - m), jnp.exp(b - m)
    share = wb / (wa + wb)
    lane = lax.broadcasted_iota(jnp.int32, a.shape, 1)
    leaving = []
    for part in got:
        for i in range(part.shape[0]):
            slot = len(leaving)
            head = far[slot]
            at = columns(head)
            weight = jnp.sum(jnp.where(lane == head, share, 0.0), axis=1, keepdims=True)
            own = mine[head]
            out[:, at] = (own + weight * (part[i].astype(jnp.float32) - own)).astype(out.dtype)
            leaving.append(pltpu.make_async_copy(out.at[:, at], result.at[:, at], sems.at[slot]))
            leaving[-1].start()
    for copy in leaving:
        copy.wait()


def exchange(room, late, planes, queries, keys, values, mate_k, sends, takes, where):
    rows, features = queries.shape
    heads = features // HEAD_DIM
    early = heads - late
    f32, bf16, i32 = jnp.float32, jnp.bfloat16, jnp.int32
    shape = jax.ShapeDtypeStruct
    tile = (rows, HEAD_DIM)
    count = planes * OWN
    across = [(d, d ^ 2) for d in range(count)]
    beside = [(d, d ^ 1) for d in range(count)]
    barrier = lax.optimization_barrier

    mate_v = lax.ppermute(values, "seq", beside)
    far_q = lax.ppermute(queries, "seq", across)
    packed = pl.pallas_call(
        functools.partial(pack_kernel, heads, planes, room),
        out_shape=[shape((room, 2) + tile, bf16)] * (planes - 1),
        in_specs=[SMEM] * 2 + [VMEM] * 4,
        out_specs=[VMEM] * (planes - 1),
        compiler_params=params(8 + room // 4),
        cost_estimate=cost(4 << 30),
        name="pack",
    )(where, sends, keys, values, mate_k, mate_v)
    landed = [
        lax.ppermute(packed[step - 1], "seq", [(d, (d + OWN * step) % count) for d in range(count)])
        for step in range(1, planes)
    ]

    where, takes, *packed = barrier((where, takes, *packed))
    most_pairs = min(4 * (planes - 1) * room, HEAD_DIM)
    pair, begin, order, far = pl.pallas_call(
        functools.partial(plan_kernel, heads, planes, room),
        out_shape=[shape((n,), i32) for n in (most_pairs, heads + 1, heads, heads)],
        in_specs=[SMEM] * 2,
        out_specs=[SMEM] * 4,
        compiler_params=params(4),
        cost_estimate=cost(4 << 30),
        name="plan",
    )(where, takes)
    here, lse_here, turned = pl.pallas_call(
        functools.partial(here_kernel, heads),
        out_shape=[shape((heads,) + tile, f32), shape(tile, f32), shape((heads, HEAD_DIM, 2 * rows), bf16)],
        in_specs=[VMEM] * 5,
        out_specs=[VMEM] * 3,
        compiler_params=params(14),
        cost_estimate=cost(1 << 30),
        name="here",
    )(queries, keys, values, mate_k, mate_v)

    def attend_far(order, lse, start, parts):
        return pl.pallas_call(
            functools.partial(far_kernel, start),
            out_shape=[shape((n,) + tile, kind) for n, kind in parts] + [shape(tile, f32)],
            in_specs=[SMEM] + [VMEM] * 5,
            out_specs=[VMEM] * (len(parts) + 1),
            compiler_params=params(12),
            cost_estimate=cost(1 << 30),
            name="far",
        )(order, lse, far_q, turned, values, mate_v)

    second = min(early, thirds(late)[-1] + 1)
    parts = [n for n in (early - second, second) if n]
    lse_far, arrived = lse_here, []
    if early:
        sent, lse_far = attend_far(order, lse_far, 0, [(parts[0], bf16)])
        arrived = [lax.ppermute(sent, "seq", across)]
    kinds = [(n, bf16) for n in parts[1:]] + [(late, f32)]
    *sent, rest, lse_far = attend_far(order, lse_far, early - sum(parts[1:]), kinds)
    arrived += [lax.ppermute(x, "seq", across) for x in sent]
    *landed, rest, lse_far, first = barrier((*landed, rest, lse_far, arrived[:-1]))
    arrived = first + arrived[len(first) :]
    boxes = []
    for got in landed:
        boxes += [got, lax.ppermute(got, "seq", beside)]

    def add_extras(q, o, lse, by_head, parts):
        return pl.pallas_call(
            functools.partial(late_kernel, len(boxes), early, by_head, room),
            out_shape=[shape((n,) + tile, kind) for n, kind in parts] + [shape(tile if by_head else (heads, rows), f32)],
            in_specs=[SMEM] * 3 + [VMEM] * 3 + [HBM] * len(boxes),
            out_specs=[VMEM] * (len(parts) + 1),
            scratch_shapes=[
                pltpu.VMEM((len(boxes) * room, 2) + tile, bf16),
                pltpu.VMEM((most_pairs,) + tile, f32),
                pltpu.VMEM((most_pairs,) + tile, f32),
                pltpu.SemaphoreType.DMA((len(boxes),)),
            ],
            compiler_params=params(min(8 + 2 * room, 48)),
            cost_estimate=cost(1 << 20),
            name="late",
        )(order, pair, begin, q, o, lse, *boxes)

    *far_late, lse_far = add_extras(far_q, rest, lse_far, False, [(n, bf16) for n in thirds(late)])
    arrived = [lax.ppermute(lse_far, "seq", across), *arrived] + [lax.ppermute(x, "seq", across) for x in far_late]
    here, lse_here = add_extras(queries, here, lse_here, True, [(heads, f32)])

    return pl.pallas_call(
        merge_kernel,
        out_shape=pltpu.HBM((rows, features), bf16),
        in_specs=[SMEM] + [VMEM] * (2 + len(arrived)),
        out_specs=pl.BlockSpec(memory_space=pltpu.HBM),
        scratch_shapes=[
            pltpu.VMEM((rows, features), bf16),
            pltpu.SemaphoreType.DMA((heads,)),
        ],
        compiler_params=params(12),
        cost_estimate=cost(1 << 20),
        name="merge",
    )(far, here, lse_here, *arrived)


def per_plane(queries, keys, values, kept, counts):
    heads, planes, slots = kept.shape
    device = lax.axis_index("seq").astype(jnp.int32)
    where = jnp.stack([device >> 2, device, (device >> 1) & 1, device & 1])
    beside = [(d, d ^ 1) for d in range(planes * OWN)]
    mate_k = lax.ppermute(keys, "seq", beside)
    shape = jax.ShapeDtypeStruct
    sends, takes, choice = pl.pallas_call(
        functools.partial(lists_kernel, planes, slots),
        out_shape=[
            shape((heads + 8, HEAD_DIM), jnp.int32),
            shape((planes * OWN, HEAD_DIM), jnp.int32),
            shape((1,), jnp.int32),
        ],
        in_specs=[SMEM] + [VMEM] * 2,
        out_specs=[VMEM] * 2 + [SMEM],
        compiler_params=params(60),
        name="lists",
    )(where, kept.transpose(1, 2, 0).reshape(planes * slots, heads), counts.T)
    sizes = SIZES + ((heads, heads),)
    return lax.switch(
        choice[0],
        [functools.partial(exchange, room, late, planes) for room, late in sizes],
        queries,
        keys,
        values,
        mate_k,
        sends,
        takes,
        where,
    )


def attend_tile(query_tile, key_tiles, value_tiles, slot_list, live_count):
    row_count = query_tile.shape[0]
    factor = 1.0 / query_tile.shape[1] ** 0.5
    start_state = (
        jnp.full((row_count,), -1e30, jnp.float32),
        jnp.zeros((row_count,), jnp.float32),
        jnp.zeros((row_count, query_tile.shape[1]), jnp.float32),
    )

    def advance(block_num, state_now):
        running, totals, numerator = state_now
        first = (block_num * GROUP).astype(jnp.int32)
        chosen = lax.dynamic_slice_in_dim(slot_list, first, GROUP)
        key_block = key_tiles[chosen].reshape(GROUP * KTILE, query_tile.shape[1])
        value_block = value_tiles[chosen].reshape(GROUP * KTILE, query_tile.shape[1])
        scores = jnp.dot(query_tile, key_block.T, preferred_element_type=jnp.float32) * factor
        live_mask = jnp.repeat(first + jnp.arange(GROUP, dtype=jnp.int32) < live_count, KTILE)
        scores = jnp.where(live_mask[None, :], scores, -1e30)
        new_max = jnp.maximum(running, jnp.max(scores, axis=1))
        rescale = jnp.exp(running - new_max)
        weights = jnp.exp(scores - new_max[:, None])
        totals = totals * rescale + jnp.sum(weights, axis=1)
        numerator = numerator * rescale[:, None] + jnp.dot(
            weights.astype(jnp.bfloat16), value_block, preferred_element_type=jnp.float32
        )
        return (new_max, totals, numerator)

    block_total = (live_count + GROUP - 1) // GROUP
    running, totals, numerator = lax.fori_loop(jnp.int32(0), block_total, advance, start_state)
    return (numerator / totals[:, None]).astype(jnp.bfloat16)


def per_device(queries, keys, values, kept, counts):
    local_rows, feature_count = queries.shape
    shards = lax.axis_size("seq")
    device = lax.axis_index("seq")
    head_count = feature_count // HEAD_DIM
    replicas = max(1, shards // head_count)
    slots_here = max(1, head_count // shards)
    total_rows = local_rows * shards
    tile_count = counts.shape[1]
    stacked = jnp.stack([queries, keys, values])
    copied = jnp.broadcast_to(
        stacked.reshape(3, local_rows, head_count, 1, HEAD_DIM),
        (3, local_rows, head_count, replicas, HEAD_DIM),
    )
    copied = copied.reshape(3, local_rows, head_count * replicas, HEAD_DIM)
    arrived = lax.all_to_all(copied, "seq", split_axis=2, concat_axis=1, tiled=True)
    head_data = arrived.transpose(2, 0, 1, 3)
    tiles_each = tile_count // replicas
    results = []
    for j in range(slots_here):
        global_slot = device * slots_here + j
        head_id = global_slot // replicas
        replica_id = global_slot % replicas
        slot_rows = lax.dynamic_index_in_dim(kept, head_id, 0, keepdims=False)
        count_row = lax.dynamic_index_in_dim(counts, head_id, 0, keepdims=False)
        all_queries = head_data[j, 0]
        key_tiles = head_data[j, 1].reshape(total_rows // KTILE, KTILE, HEAD_DIM)
        value_tiles = head_data[j, 2].reshape(total_rows // KTILE, KTILE, HEAD_DIM)
        rounds = jnp.arange(tiles_each, dtype=jnp.int32)
        tile_ids = replica_id * tiles_each + rounds

        def process(i, output):
            tile_id = tile_ids[i]
            query_tile = lax.dynamic_slice_in_dim(all_queries, tile_id * QTILE, QTILE, 0)
            finished = attend_tile(
                query_tile, key_tiles, value_tiles, slot_rows[tile_id], count_row[tile_id]
            )
            return lax.dynamic_update_slice_in_dim(output, finished, tile_id * QTILE, 0)

        results.append(
            lax.fori_loop(0, tiles_each, process, jnp.zeros((total_rows, HEAD_DIM), jnp.bfloat16))
        )
    gathered = jnp.stack(results, axis=1)
    returned = lax.all_to_all(gathered, "seq", split_axis=0, concat_axis=1, tiled=True)
    combined = (
        returned.reshape(local_rows, head_count, replicas, HEAD_DIM).astype(jnp.float32).sum(axis=2)
    )
    return combined.astype(jnp.bfloat16).reshape(local_rows, feature_count)


def solution(mesh):
    by_rows = P(("groups", "seq"), None)
    placed = (by_rows, by_rows, by_rows, P("groups", None, None), P("groups", None))

    def step(queries, keys, values, kept, counts):
        heads, planes, slots = kept.shape
        one_tile_each = queries.shape[0] == KTILE and mesh.shape["seq"] == planes * OWN
        fits = heads % 8 == 0 and heads <= 32 and heads * (slots - OWN) <= HEAD_DIM and planes == 4
        run = per_plane if one_tile_each and fits else per_device
        return run(queries, keys, values, kept, counts)

    return jax.shard_map(step, mesh=mesh, in_specs=placed, out_specs=by_rows, check_vma=False)
```

```python
import functools

import jax
import jax.numpy as jnp
from jax import lax
from jax.experimental import pallas as pl
from jax.experimental.pallas import tpu as pltpu
from jax.sharding import PartitionSpec as P

HEAD_DIM = 128
QTILE = 512
KTILE = 128
GROUP = 4
OWN = QTILE // KTILE
SIZES = ((5, 14), (5, 16), (6, 18), (7, 20))
MIB = 1 << 20
SMEM = pl.BlockSpec(memory_space=pltpu.SMEM)
VMEM = pl.BlockSpec(memory_space=pltpu.VMEM)
HBM = pl.BlockSpec(memory_space=pl.ANY)


def params(mib):
    return pltpu.CompilerParams(vmem_limit_bytes=mib * MIB)


def cost(flops):
    return pl.CostEstimate(flops=flops, bytes_accessed=8 << 20, transcendentals=0)


def thirds(late):
    return late // 3, late // 3, late - 2 * (late // 3)


def columns(head):
    if isinstance(head, int):
        return pl.ds(head * HEAD_DIM, HEAD_DIM)
    return pl.ds(pl.multiple_of(head * HEAD_DIM, HEAD_DIM), HEAD_DIM)


def dot(a, b):
    return jnp.dot(a, b, preferred_element_type=jnp.float32)


def lists_kernel(planes, slots, where, kept, counts, sends, takes, choice):
    plane, pair = where[0], where[1] >> 1
    heads = kept.shape[1]
    shape = (planes * OWN, heads)
    half = (planes * OWN // 2, heads)
    ids = lax.broadcasted_iota(jnp.int32, shape, 0)
    chips = lax.broadcasted_iota(jnp.int32, half, 0)
    bit = jnp.left_shift(jnp.int32(1), lax.broadcasted_iota(jnp.int32, shape, 1))
    lane = lax.broadcasted_iota(jnp.int32, (1, HEAD_DIM), 1)
    most = jnp.zeros((planes * OWN // 2, 1), jnp.int32)
    touched = jnp.zeros((1, 1), jnp.int32)
    taken = jnp.zeros(shape, jnp.int32)
    wanted = []
    for t in range(planes):
        hits = jnp.zeros(shape, jnp.int32)
        per_chip = jnp.zeros(half, jnp.int32)
        for j in range(OWN, slots):
            tile = kept[t * slots + j : t * slots + j + 1, :]
            live = counts[t : t + 1, :] > j
            hits = jnp.where((ids == tile) & live, 1, hits)
            per_chip = per_chip + jnp.where((chips == (tile >> 1)) & live, 1, 0)
        most = jnp.maximum(most, jnp.sum(per_chip, axis=1, keepdims=True))
        for side in range(2):
            some = jnp.max(jnp.where(((ids >> 1) & 1) == side, hits, 0), axis=0, keepdims=True)
            touched = jnp.maximum(touched, jnp.sum(some, axis=1, keepdims=True))
        bits = hits * bit
        for turn in range(2):
            wanted.append(jnp.sum(jnp.where(ids == 2 * pair + turn, hits, 0), axis=0, keepdims=True))
        taken = jnp.where(plane == t, bits, taken)
    square = (heads, heads)
    at, head = lax.broadcasted_iota(jnp.int32, square, 0), lax.broadcasted_iota(jnp.int32, square, 1)
    before = jnp.where(at < head, 1.0, 0.0)
    named = jnp.concatenate(wanted, axis=0)
    rank = dot(named.astype(jnp.float32), before).astype(jnp.int32)
    rows = jnp.zeros((heads, HEAD_DIM), jnp.int32)
    count = jnp.zeros((1, HEAD_DIM), jnp.int32)
    for i in range(2 * planes):
        here = (at == rank[i : i + 1, :]) & (named[i : i + 1, :] == 1)
        rows = jnp.where(lane == i, jnp.sum(jnp.where(here, head, 0), axis=1, keepdims=True), rows)
        count = jnp.where(lane == i, jnp.sum(named[i : i + 1, :], axis=1, keepdims=True), count)
    sends[0:heads, :] = rows
    sends[heads : heads + 8, :] = jnp.broadcast_to(count, (8, HEAD_DIM))
    takes[...] = jnp.where(
        lane == 0,
        jnp.sum(taken, axis=1, keepdims=True),
        jnp.sum(jnp.where(taken != 0, 1, 0), axis=1, keepdims=True),
    )
    top, wide = jnp.max(most), jnp.max(touched)
    index = jnp.int32(len(SIZES))
    for i, (room, late) in reversed(list(enumerate(SIZES))):
        index = jnp.where((top <= 2 * room) & (wide <= late), i, index)
    choice[0] = index


def pack_kernel(heads, planes, room, where, sends, k_ref, v_ref, mate_k, mate_v, *outs):
    plane, core = where[0], where[3]
    for step, out in enumerate(outs, 1):
        lane = 2 * lax.rem(plane + step, planes)
        first, both = sends[heads, lane], sends[heads, lane] + sends[heads, lane + 1]

        def take(slot, carry, out=out, lane=lane, first=first):
            at = core * room + slot
            turn = jnp.where(at >= first, 1, 0)
            head = sends[at - turn * first, lane + turn]

            @pl.when(core == turn)
            def _():
                out[slot, 0] = k_ref[:, columns(head)].T
                out[slot, 1] = v_ref[:, columns(head)]

            @pl.when(core != turn)
            def _():
                out[slot, 0] = mate_k[:, columns(head)].T
                out[slot, 1] = mate_v[:, columns(head)]

            return carry

        lax.fori_loop(0, jnp.clip(both - core * room, 0, room), take, 0)


def plan_kernel(heads, planes, room, where, takes, pair, begin, order, far):
    plane, side, core = where[0], where[2], where[3]
    near, other, starts = [], [], []
    for step in range(1, planes):
        source = lax.rem(plane - step + planes, planes) * OWN
        for turn in range(2):
            near.append(takes[source + 2 * side + turn, 0])
            starts.append(takes[source + 2 * side, 1] if turn else jnp.int32(0))
            other.append(takes[source + 2 * (1 - side) + turn, 0])
    any_near = functools.reduce(jnp.bitwise_or, near)
    any_other = functools.reduce(jnp.bitwise_or, other)

    def held(bits):
        return lax.fori_loop(0, heads, lambda h, n: n + ((bits >> h) & 1), jnp.int32(0))

    def put(head, state):
        a, b, c, d, pairs, *used = state
        none, far_none = 1 - ((any_near >> head) & 1), 1 - ((any_other >> head) & 1)
        at = jnp.where(none == 1, a, b)
        order[at] = head
        far[jnp.where(far_none == 1, c, d)] = head
        begin[head] = pairs
        for i, bits in enumerate(near):
            hit = (bits >> head) & 1
            sender = jnp.where(used[i] >= room, 1, 0)
            box = i // 2 * 2 + jnp.where(sender == core, 0, 1)

            @pl.when(hit == 1)
            def _(i=i, pairs=pairs, used=used, sender=sender, box=box):
                pair[pairs] = head * 4096 + box * room + used[i] - sender * room

            pairs = pairs + hit
            used = used[:i] + [used[i] + hit] + used[i + 1 :]
        return (a + none, b + 1 - none, c + far_none, d + 1 - far_none, pairs, *used)

    zero = jnp.int32(0)
    first = (zero, heads - held(any_near), zero, heads - held(any_other), zero, *starts)
    begin[heads] = lax.fori_loop(0, heads, put, first)[4]


def soften(q, k_t, v):
    s = dot(q, k_t) * (1.0 / HEAD_DIM**0.5)
    m = jnp.max(s, axis=1, keepdims=True)
    w = jnp.exp(s - m)
    l = jnp.sum(w, axis=1, keepdims=True)
    return dot(w.astype(jnp.bfloat16), v) / l, m + jnp.log(l)


def here_kernel(heads, q_ref, k_ref, v_ref, mate_k, mate_v, out, lse_out, turned):
    lane = lax.broadcasted_iota(jnp.int32, lse_out.shape, 1)

    def attend(head, lse):
        at = columns(head)
        k_t = jnp.concatenate([k_ref[:, at].T, mate_k[:, at].T], axis=1)
        turned[head] = k_t
        v = jnp.concatenate([v_ref[:, at], mate_v[:, at]], axis=0)
        o, new = soften(q_ref[:, at], k_t, v)
        out[head] = o
        return jnp.where(lane == head, new, lse)

    lse_out[...] = lax.fori_loop(0, heads, attend, jnp.zeros(lse_out.shape, jnp.float32), unroll=4)


def far_kernel(start, order, lse_ref, q_ref, turned, v_ref, mate_v, *outs):
    *parts, lse_out = outs
    lane = lax.broadcasted_iota(jnp.int32, lse_out.shape, 1)
    lse = lse_ref[...]
    for part in parts:

        def attend(i, lse, part=part, start=start):
            head = order[start + i]
            at = columns(head)
            v = jnp.concatenate([v_ref[:, at], mate_v[:, at]], axis=0)
            o, new = soften(q_ref[:, at], turned[head], v)
            part[i] = o.astype(part.dtype)
            return jnp.where(lane == head, new, lse)

        lse = lax.fori_loop(0, part.shape[0], attend, lse, unroll=4)
        start += part.shape[0]
    lse_out[...] = lse


def late_kernel(sends, early, by_head, room, order, pair, begin, q_ref, o_ref, lse_ref, *rest):
    boxes, rest = rest[: sends], rest[sends:]
    *outs, lse_out, tiles, partial, level, sems = rest
    copies = [
        pltpu.make_async_copy(box, tiles.at[pl.ds(b * room, room)], sems.at[b]) for b, box in enumerate(boxes)
    ]
    for copy in copies:
        copy.start()
    heads = order.shape[0]
    shape = lse_ref.shape
    most = partial.shape[0]
    lane = lax.broadcasted_iota(jnp.int32, shape, 1)
    total = begin[heads]
    for copy in copies:
        copy.wait()

    if by_head:
        outs[0][...] = o_ref[...]
    wide = not by_head and heads - early <= 18
    width = 8 if wide else 4

    def several(i, carry):
        for j in range(width):
            at = jnp.minimum(width * i + j, total - 1)
            code = pair[at]
            head, tile = code >> 12, code & 4095
            o, new = soften(q_ref[:, columns(head)], tiles[tile, 0], tiles[tile, 1])
            partial[at] = o
            level[at] = jnp.broadcast_to(new, shape)
        return carry

    lax.fori_loop(0, lax.div(total + width - 1, width), several, 0)

    def join(i, lse, out, skip):
        head = order[early + skip + i]
        start, end = begin[head], begin[head + 1]
        base = jnp.sum(jnp.where(lane == head, lse_ref[...], 0.0), axis=1, keepdims=True)
        base = jnp.broadcast_to(base, shape)
        spots = [jnp.minimum(start + e, most - 1) for e in range(4)]
        levels = [jnp.where(start + e < end, level[p], -1e30) for e, p in enumerate(spots)]
        m = functools.reduce(jnp.maximum, levels, base)
        l = jnp.exp(base - m)
        o = l * o_ref[head if by_head else skip + i]
        for e, p in enumerate(spots):
            w = jnp.exp(levels[e] - m)
            l = l + w
            o = o + jnp.where(start + e < end, w * partial[p], 0.0)
        out[head if by_head else i] = (o / l).astype(out.dtype)
        return jnp.where(lane == head, m + jnp.log(l), lse)

    lse, skip = lse_ref[...], 0
    for out in outs:
        count = heads - early if by_head else out.shape[0]
        unroll = count if wide else 2
        lse = lax.fori_loop(0, count, functools.partial(join, out=out, skip=skip), lse, unroll=unroll)
        skip += out.shape[0]
    lse_out[...] = lse if by_head else lse.T[:heads]


def merge_kernel(far, mine, lse_here, lse_got, *rest):
    *got, result, out, sems = rest
    a, b = lse_here[...], lse_got[...]
    heads = b.shape[0]
    b = jnp.concatenate([b, jnp.zeros((a.shape[1] - heads, a.shape[0]), b.dtype)], axis=0).T
    m = jnp.maximum(a, b)
    wa, wb = jnp.exp(a - m), jnp.exp(b - m)
    share = wb / (wa + wb)
    lane = lax.broadcasted_iota(jnp.int32, a.shape, 1)
    leaving = []
    for part in got:
        for i in range(part.shape[0]):
            slot = len(leaving)
            head = far[slot]
            at = columns(head)
            weight = jnp.sum(jnp.where(lane == head, share, 0.0), axis=1, keepdims=True)
            own = mine[head]
            out[:, at] = (own + weight * (part[i].astype(jnp.float32) - own)).astype(out.dtype)
            leaving.append(pltpu.make_async_copy(out.at[:, at], result.at[:, at], sems.at[slot]))
            leaving[-1].start()
    for copy in leaving:
        copy.wait()


def exchange(room, late, planes, queries, keys, values, mate_k, sends, takes, where):
    rows, features = queries.shape
    heads = features // HEAD_DIM
    early = heads - late
    f32, bf16, i32 = jnp.float32, jnp.bfloat16, jnp.int32
    shape = jax.ShapeDtypeStruct
    tile = (rows, HEAD_DIM)
    count = planes * OWN
    across = [(d, d ^ 2) for d in range(count)]
    beside = [(d, d ^ 1) for d in range(count)]
    barrier = lax.optimization_barrier

    mate_v = lax.ppermute(values, "seq", beside)
    far_q = lax.ppermute(queries, "seq", across)
    packed = pl.pallas_call(
        functools.partial(pack_kernel, heads, planes, room),
        out_shape=[shape((room, 2) + tile, bf16)] * (planes - 1),
        in_specs=[SMEM] * 2 + [VMEM] * 4,
        out_specs=[VMEM] * (planes - 1),
        compiler_params=params(8 + room // 4),
        cost_estimate=cost(4 << 30),
        name="pack",
    )(where, sends, keys, values, mate_k, mate_v)
    landed = [
        lax.ppermute(packed[step - 1], "seq", [(d, (d + OWN * step) % count) for d in range(count)])
        for step in range(1, planes)
    ]

    where, takes, *packed = barrier((where, takes, *packed))
    most_pairs = min(4 * (planes - 1) * room, HEAD_DIM)
    pair, begin, order, far = pl.pallas_call(
        functools.partial(plan_kernel, heads, planes, room),
        out_shape=[shape((n,), i32) for n in (most_pairs, heads + 1, heads, heads)],
        in_specs=[SMEM] * 2,
        out_specs=[SMEM] * 4,
        compiler_params=params(4),
        cost_estimate=cost(4 << 30),
        name="plan",
    )(where, takes)
    here, lse_here, turned = pl.pallas_call(
        functools.partial(here_kernel, heads),
        out_shape=[shape((heads,) + tile, f32), shape(tile, f32), shape((heads, HEAD_DIM, 2 * rows), bf16)],
        in_specs=[VMEM] * 5,
        out_specs=[VMEM] * 3,
        compiler_params=params(14),
        cost_estimate=cost(1 << 30),
        name="here",
    )(queries, keys, values, mate_k, mate_v)

    def attend_far(order, lse, start, parts):
        return pl.pallas_call(
            functools.partial(far_kernel, start),
            out_shape=[shape((n,) + tile, kind) for n, kind in parts] + [shape(tile, f32)],
            in_specs=[SMEM] + [VMEM] * 5,
            out_specs=[VMEM] * (len(parts) + 1),
            compiler_params=params(12),
            cost_estimate=cost(1 << 30),
            name="far",
        )(order, lse, far_q, turned, values, mate_v)

    second = min(early, max(thirds(late)[-1] + 2, early - 8))
    parts = [n for n in (early - second, second) if n]
    lse_far, arrived = lse_here, []
    if early:
        sent, lse_far = attend_far(order, lse_far, 0, [(parts[0], bf16)])
        arrived = [lax.ppermute(sent, "seq", across)]
    kinds = [(n, bf16) for n in parts[1:]] + [(late, f32)]
    *sent, rest, lse_far = attend_far(order, lse_far, early - sum(parts[1:]), kinds)
    arrived += [lax.ppermute(x, "seq", across) for x in sent]
    *landed, rest, lse_far, first = barrier((*landed, rest, lse_far, arrived[:-1]))
    arrived = first + arrived[len(first) :]
    boxes = []
    for got in landed:
        boxes += [got, lax.ppermute(got, "seq", beside)]

    def add_extras(q, o, lse, by_head, parts):
        return pl.pallas_call(
            functools.partial(late_kernel, len(boxes), early, by_head, room),
            out_shape=[shape((n,) + tile, kind) for n, kind in parts] + [shape(tile if by_head else (heads, rows), f32)],
            in_specs=[SMEM] * 3 + [VMEM] * 3 + [HBM] * len(boxes),
            out_specs=[VMEM] * (len(parts) + 1),
            scratch_shapes=[
                pltpu.VMEM((len(boxes) * room, 2) + tile, bf16),
                pltpu.VMEM((most_pairs,) + tile, f32),
                pltpu.VMEM((most_pairs,) + tile, f32),
                pltpu.SemaphoreType.DMA((len(boxes),)),
            ],
            compiler_params=params(min(8 + 2 * room, 48)),
            cost_estimate=cost(1 << 20),
            name="late",
        )(order, pair, begin, q, o, lse, *boxes)

    *far_late, lse_far = add_extras(far_q, rest, lse_far, False, [(n, bf16) for n in thirds(late)])
    arrived = [lax.ppermute(lse_far, "seq", across), *arrived] + [lax.ppermute(x, "seq", across) for x in far_late]
    here, lse_here = add_extras(queries, here, lse_here, True, [(heads, f32)])

    return pl.pallas_call(
        merge_kernel,
        out_shape=pltpu.HBM((rows, features), bf16),
        in_specs=[SMEM] + [VMEM] * (2 + len(arrived)),
        out_specs=pl.BlockSpec(memory_space=pltpu.HBM),
        scratch_shapes=[
            pltpu.VMEM((rows, features), bf16),
            pltpu.SemaphoreType.DMA((heads,)),
        ],
        compiler_params=params(12),
        cost_estimate=cost(1 << 20),
        name="merge",
    )(far, here, lse_here, *arrived)


def per_plane(queries, keys, values, kept, counts):
    heads, planes, slots = kept.shape
    device = lax.axis_index("seq").astype(jnp.int32)
    where = jnp.stack([device >> 2, device, (device >> 1) & 1, device & 1])
    beside = [(d, d ^ 1) for d in range(planes * OWN)]
    mate_k = lax.ppermute(keys, "seq", beside)
    shape = jax.ShapeDtypeStruct
    sends, takes, choice = pl.pallas_call(
        functools.partial(lists_kernel, planes, slots),
        out_shape=[
            shape((heads + 8, HEAD_DIM), jnp.int32),
            shape((planes * OWN, HEAD_DIM), jnp.int32),
            shape((1,), jnp.int32),
        ],
        in_specs=[SMEM] + [VMEM] * 2,
        out_specs=[VMEM] * 2 + [SMEM],
        compiler_params=params(60),
        name="lists",
    )(where, kept.transpose(1, 2, 0).reshape(planes * slots, heads), counts.T)
    sizes = SIZES + ((heads, heads),)
    return lax.switch(
        choice[0],
        [functools.partial(exchange, room, late, planes) for room, late in sizes],
        queries,
        keys,
        values,
        mate_k,
        sends,
        takes,
        where,
    )


def attend_tile(query_tile, key_tiles, value_tiles, slot_list, live_count):
    row_count = query_tile.shape[0]
    factor = 1.0 / query_tile.shape[1] ** 0.5
    start_state = (
        jnp.full((row_count,), -1e30, jnp.float32),
        jnp.zeros((row_count,), jnp.float32),
        jnp.zeros((row_count, query_tile.shape[1]), jnp.float32),
    )

    def advance(block_num, state_now):
        running, totals, numerator = state_now
        first = (block_num * GROUP).astype(jnp.int32)
        chosen = lax.dynamic_slice_in_dim(slot_list, first, GROUP)
        key_block = key_tiles[chosen].reshape(GROUP * KTILE, query_tile.shape[1])
        value_block = value_tiles[chosen].reshape(GROUP * KTILE, query_tile.shape[1])
        scores = jnp.dot(query_tile, key_block.T, preferred_element_type=jnp.float32) * factor
        live_mask = jnp.repeat(first + jnp.arange(GROUP, dtype=jnp.int32) < live_count, KTILE)
        scores = jnp.where(live_mask[None, :], scores, -1e30)
        new_max = jnp.maximum(running, jnp.max(scores, axis=1))
        rescale = jnp.exp(running - new_max)
        weights = jnp.exp(scores - new_max[:, None])
        totals = totals * rescale + jnp.sum(weights, axis=1)
        numerator = numerator * rescale[:, None] + jnp.dot(
            weights.astype(jnp.bfloat16), value_block, preferred_element_type=jnp.float32
        )
        return (new_max, totals, numerator)

    block_total = (live_count + GROUP - 1) // GROUP
    running, totals, numerator = lax.fori_loop(jnp.int32(0), block_total, advance, start_state)
    return (numerator / totals[:, None]).astype(jnp.bfloat16)


def per_device(queries, keys, values, kept, counts):
    local_rows, feature_count = queries.shape
    shards = lax.axis_size("seq")
    device = lax.axis_index("seq")
    head_count = feature_count // HEAD_DIM
    replicas = max(1, shards // head_count)
    slots_here = max(1, head_count // shards)
    total_rows = local_rows * shards
    tile_count = counts.shape[1]
    stacked = jnp.stack([queries, keys, values])
    copied = jnp.broadcast_to(
        stacked.reshape(3, local_rows, head_count, 1, HEAD_DIM),
        (3, local_rows, head_count, replicas, HEAD_DIM),
    )
    copied = copied.reshape(3, local_rows, head_count * replicas, HEAD_DIM)
    arrived = lax.all_to_all(copied, "seq", split_axis=2, concat_axis=1, tiled=True)
    head_data = arrived.transpose(2, 0, 1, 3)
    tiles_each = tile_count // replicas
    results = []
    for j in range(slots_here):
        global_slot = device * slots_here + j
        head_id = global_slot // replicas
        replica_id = global_slot % replicas
        slot_rows = lax.dynamic_index_in_dim(kept, head_id, 0, keepdims=False)
        count_row = lax.dynamic_index_in_dim(counts, head_id, 0, keepdims=False)
        all_queries = head_data[j, 0]
        key_tiles = head_data[j, 1].reshape(total_rows // KTILE, KTILE, HEAD_DIM)
        value_tiles = head_data[j, 2].reshape(total_rows // KTILE, KTILE, HEAD_DIM)
        rounds = jnp.arange(tiles_each, dtype=jnp.int32)
        tile_ids = replica_id * tiles_each + rounds

        def process(i, output):
            tile_id = tile_ids[i]
            query_tile = lax.dynamic_slice_in_dim(all_queries, tile_id * QTILE, QTILE, 0)
            finished = attend_tile(
                query_tile, key_tiles, value_tiles, slot_rows[tile_id], count_row[tile_id]
            )
            return lax.dynamic_update_slice_in_dim(output, finished, tile_id * QTILE, 0)

        results.append(
            lax.fori_loop(0, tiles_each, process, jnp.zeros((total_rows, HEAD_DIM), jnp.bfloat16))
        )
    gathered = jnp.stack(results, axis=1)
    returned = lax.all_to_all(gathered, "seq", split_axis=0, concat_axis=1, tiled=True)
    combined = (
        returned.reshape(local_rows, head_count, replicas, HEAD_DIM).astype(jnp.float32).sum(axis=2)
    )
    return combined.astype(jnp.bfloat16).reshape(local_rows, feature_count)


def solution(mesh):
    by_rows = P(("groups", "seq"), None)
    placed = (by_rows, by_rows, by_rows, P("groups", None, None), P("groups", None))

    def step(queries, keys, values, kept, counts):
        heads, planes, slots = kept.shape
        one_tile_each = queries.shape[0] == KTILE and mesh.shape["seq"] == planes * OWN
        fits = heads % 8 == 0 and heads <= 32 and heads * (slots - OWN) <= HEAD_DIM and planes == 4
        run = per_plane if one_tile_each and fits else per_device
        return run(queries, keys, values, kept, counts)

    return jax.shard_map(step, mesh=mesh, in_specs=placed, out_specs=by_rows, check_vma=False)
```

```python
import functools

import jax
import jax.numpy as jnp
from jax import lax
from jax.experimental import pallas as pl
from jax.experimental.pallas import tpu as pltpu
from jax.sharding import PartitionSpec as P

HEAD_DIM = 128
QTILE = 512
KTILE = 128
GROUP = 4
OWN = QTILE // KTILE
SIZES = ((5, 14), (5, 16), (6, 18), (7, 20))
MIB = 1 << 20
SMEM = pl.BlockSpec(memory_space=pltpu.SMEM)
VMEM = pl.BlockSpec(memory_space=pltpu.VMEM)
HBM = pl.BlockSpec(memory_space=pl.ANY)


def params(mib):
    return pltpu.CompilerParams(vmem_limit_bytes=mib * MIB)


def cost(flops):
    return pl.CostEstimate(flops=flops, bytes_accessed=8 << 20, transcendentals=0)


def thirds(late):
    return late // 3, late // 3, late - 2 * (late // 3)


def columns(head):
    if isinstance(head, int):
        return pl.ds(head * HEAD_DIM, HEAD_DIM)
    return pl.ds(pl.multiple_of(head * HEAD_DIM, HEAD_DIM), HEAD_DIM)


def dot(a, b):
    return jnp.dot(a, b, preferred_element_type=jnp.float32)


def lists_kernel(planes, slots, where, kept, counts, sends, takes, choice):
    plane, pair = where[0], where[1] >> 1
    heads = kept.shape[1]
    shape = (planes * OWN, heads)
    half = (planes * OWN // 2, heads)
    ids = lax.broadcasted_iota(jnp.int32, shape, 0)
    chips = lax.broadcasted_iota(jnp.int32, half, 0)
    bit = jnp.left_shift(jnp.int32(1), lax.broadcasted_iota(jnp.int32, shape, 1))
    lane = lax.broadcasted_iota(jnp.int32, (1, HEAD_DIM), 1)
    most = jnp.zeros((planes * OWN // 2, 1), jnp.int32)
    touched = jnp.zeros((1, 1), jnp.int32)
    taken = jnp.zeros(shape, jnp.int32)
    wanted = []
    for t in range(planes):
        hits = jnp.zeros(shape, jnp.int32)
        per_chip = jnp.zeros(half, jnp.int32)
        for j in range(OWN, slots):
            tile = kept[t * slots + j : t * slots + j + 1, :]
            live = counts[t : t + 1, :] > j
            hits = jnp.where((ids == tile) & live, 1, hits)
            per_chip = per_chip + jnp.where((chips == (tile >> 1)) & live, 1, 0)
        most = jnp.maximum(most, jnp.sum(per_chip, axis=1, keepdims=True))
        for side in range(2):
            some = jnp.max(jnp.where(((ids >> 1) & 1) == side, hits, 0), axis=0, keepdims=True)
            touched = jnp.maximum(touched, jnp.sum(some, axis=1, keepdims=True))
        bits = hits * bit
        for turn in range(2):
            wanted.append(jnp.sum(jnp.where(ids == 2 * pair + turn, hits, 0), axis=0, keepdims=True))
        taken = jnp.where(plane == t, bits, taken)
    square = (heads, heads)
    at, head = lax.broadcasted_iota(jnp.int32, square, 0), lax.broadcasted_iota(jnp.int32, square, 1)
    before = jnp.where(at < head, 1.0, 0.0)
    named = jnp.concatenate(wanted, axis=0)
    rank = dot(named.astype(jnp.float32), before).astype(jnp.int32)
    rows = jnp.zeros((heads, HEAD_DIM), jnp.int32)
    count = jnp.zeros((1, HEAD_DIM), jnp.int32)
    for i in range(2 * planes):
        here = (at == rank[i : i + 1, :]) & (named[i : i + 1, :] == 1)
        rows = jnp.where(lane == i, jnp.sum(jnp.where(here, head, 0), axis=1, keepdims=True), rows)
        count = jnp.where(lane == i, jnp.sum(named[i : i + 1, :], axis=1, keepdims=True), count)
    sends[0:heads, :] = rows
    sends[heads : heads + 8, :] = jnp.broadcast_to(count, (8, HEAD_DIM))
    takes[...] = jnp.where(
        lane == 0,
        jnp.sum(taken, axis=1, keepdims=True),
        jnp.sum(jnp.where(taken != 0, 1, 0), axis=1, keepdims=True),
    )
    top, wide = jnp.max(most), jnp.max(touched)
    index = jnp.int32(len(SIZES))
    for i, (room, late) in reversed(list(enumerate(SIZES))):
        index = jnp.where((top <= 2 * room) & (wide <= late), i, index)
    choice[0] = index


def pack_kernel(heads, planes, room, where, sends, k_ref, v_ref, mate_k, mate_v, *outs):
    plane, core = where[0], where[3]
    for step, out in enumerate(outs, 1):
        lane = 2 * lax.rem(plane + step, planes)
        first, both = sends[heads, lane], sends[heads, lane] + sends[heads, lane + 1]

        def take(slot, carry, out=out, lane=lane, first=first):
            at = core * room + slot
            turn = jnp.where(at >= first, 1, 0)
            head = sends[at - turn * first, lane + turn]

            @pl.when(core == turn)
            def _():
                out[slot, 0] = k_ref[:, columns(head)].T
                out[slot, 1] = v_ref[:, columns(head)]

            @pl.when(core != turn)
            def _():
                out[slot, 0] = mate_k[:, columns(head)].T
                out[slot, 1] = mate_v[:, columns(head)]

            return carry

        lax.fori_loop(0, jnp.clip(both - core * room, 0, room), take, 0)


def plan_kernel(heads, planes, room, where, takes, pair, begin, order, far):
    plane, side, core = where[0], where[2], where[3]
    near, other, starts = [], [], []
    for step in range(1, planes):
        source = lax.rem(plane - step + planes, planes) * OWN
        for turn in range(2):
            near.append(takes[source + 2 * side + turn, 0])
            starts.append(takes[source + 2 * side, 1] if turn else jnp.int32(0))
            other.append(takes[source + 2 * (1 - side) + turn, 0])
    any_near = functools.reduce(jnp.bitwise_or, near)
    any_other = functools.reduce(jnp.bitwise_or, other)

    def held(bits):
        return lax.fori_loop(0, heads, lambda h, n: n + ((bits >> h) & 1), jnp.int32(0))

    def put(head, state):
        a, b, c, d, pairs, *used = state
        none, far_none = 1 - ((any_near >> head) & 1), 1 - ((any_other >> head) & 1)
        at = jnp.where(none == 1, a, b)
        order[at] = head
        far[jnp.where(far_none == 1, c, d)] = head
        begin[head] = pairs
        for i, bits in enumerate(near):
            hit = (bits >> head) & 1
            sender = jnp.where(used[i] >= room, 1, 0)
            box = i // 2 * 2 + jnp.where(sender == core, 0, 1)

            @pl.when(hit == 1)
            def _(i=i, pairs=pairs, used=used, sender=sender, box=box):
                pair[pairs] = head * 4096 + box * room + used[i] - sender * room

            pairs = pairs + hit
            used = used[:i] + [used[i] + hit] + used[i + 1 :]
        return (a + none, b + 1 - none, c + far_none, d + 1 - far_none, pairs, *used)

    zero = jnp.int32(0)
    first = (zero, heads - held(any_near), zero, heads - held(any_other), zero, *starts)
    begin[heads] = lax.fori_loop(0, heads, put, first)[4]


def soften(q, k_t, v):
    s = dot(q, k_t) * (1.0 / HEAD_DIM**0.5)
    m = jnp.max(s, axis=1, keepdims=True)
    w = jnp.exp(s - m)
    l = jnp.sum(w, axis=1, keepdims=True)
    return dot(w.astype(jnp.bfloat16), v) / l, m + jnp.log(l)


def here_kernel(heads, q_ref, k_ref, v_ref, mate_k, mate_v, out, lse_out, turned):
    lane = lax.broadcasted_iota(jnp.int32, lse_out.shape, 1)

    def attend(head, lse):
        at = columns(head)
        k_t = jnp.concatenate([k_ref[:, at].T, mate_k[:, at].T], axis=1)
        turned[head] = k_t
        v = jnp.concatenate([v_ref[:, at], mate_v[:, at]], axis=0)
        o, new = soften(q_ref[:, at], k_t, v)
        out[head] = o
        return jnp.where(lane == head, new, lse)

    lse_out[...] = lax.fori_loop(0, heads, attend, jnp.zeros(lse_out.shape, jnp.float32), unroll=4)


def far_kernel(start, order, lse_ref, q_ref, turned, v_ref, mate_v, *outs):
    *parts, lse_out = outs
    lane = lax.broadcasted_iota(jnp.int32, lse_out.shape, 1)
    lse = lse_ref[...]
    for part in parts:

        def attend(i, lse, part=part, start=start):
            head = order[start + i]
            at = columns(head)
            v = jnp.concatenate([v_ref[:, at], mate_v[:, at]], axis=0)
            o, new = soften(q_ref[:, at], turned[head], v)
            part[i] = o.astype(part.dtype)
            return jnp.where(lane == head, new, lse)

        lse = lax.fori_loop(0, part.shape[0], attend, lse, unroll=4)
        start += part.shape[0]
    lse_out[...] = lse


def late_kernel(sends, early, by_head, room, order, pair, begin, q_ref, o_ref, lse_ref, *rest):
    boxes, rest = rest[: sends], rest[sends:]
    *outs, lse_out, tiles, partial, level, sems = rest
    copies = [
        pltpu.make_async_copy(box, tiles.at[pl.ds(b * room, room)], sems.at[b]) for b, box in enumerate(boxes)
    ]
    for copy in copies:
        copy.start()
    heads = order.shape[0]
    shape = lse_ref.shape
    most = partial.shape[0]
    lane = lax.broadcasted_iota(jnp.int32, shape, 1)
    total = begin[heads]
    for copy in copies:
        copy.wait()

    if by_head:
        outs[0][...] = o_ref[...]
    wide = not by_head and heads - early <= 20
    width = 8 if wide else 4

    def several(i, carry):
        for j in range(width):
            at = jnp.minimum(width * i + j, total - 1)
            code = pair[at]
            head, tile = code >> 12, code & 4095
            o, new = soften(q_ref[:, columns(head)], tiles[tile, 0], tiles[tile, 1])
            partial[at] = o
            level[at] = jnp.broadcast_to(new, shape)
        return carry

    lax.fori_loop(0, lax.div(total + width - 1, width), several, 0)

    def join(i, lse, out, skip):
        head = order[early + skip + i]
        start, end = begin[head], begin[head + 1]
        base = jnp.sum(jnp.where(lane == head, lse_ref[...], 0.0), axis=1, keepdims=True)
        base = jnp.broadcast_to(base, shape)
        spots = [jnp.minimum(start + e, most - 1) for e in range(4)]
        levels = [jnp.where(start + e < end, level[p], -1e30) for e, p in enumerate(spots)]
        m = functools.reduce(jnp.maximum, levels, base)
        l = jnp.exp(base - m)
        o = l * o_ref[head if by_head else skip + i]
        for e, p in enumerate(spots):
            w = jnp.exp(levels[e] - m)
            l = l + w
            o = o + jnp.where(start + e < end, w * partial[p], 0.0)
        out[head if by_head else i] = (o / l).astype(out.dtype)
        return jnp.where(lane == head, m + jnp.log(l), lse)

    lse, skip = lse_ref[...], 0
    for out in outs:
        count = heads - early if by_head else out.shape[0]
        unroll = count if wide else 2
        lse = lax.fori_loop(0, count, functools.partial(join, out=out, skip=skip), lse, unroll=unroll)
        skip += out.shape[0]
    lse_out[...] = lse if by_head else lse.T[:heads]


def merge_kernel(far, mine, lse_here, lse_got, *rest):
    *got, result, out, sems = rest
    a, b = lse_here[...], lse_got[...]
    heads = b.shape[0]
    b = jnp.concatenate([b, jnp.zeros((a.shape[1] - heads, a.shape[0]), b.dtype)], axis=0).T
    m = jnp.maximum(a, b)
    wa, wb = jnp.exp(a - m), jnp.exp(b - m)
    share = wb / (wa + wb)
    lane = lax.broadcasted_iota(jnp.int32, a.shape, 1)
    leaving = []
    for part in got:
        for i in range(part.shape[0]):
            slot = len(leaving)
            head = far[slot]
            at = columns(head)
            weight = jnp.sum(jnp.where(lane == head, share, 0.0), axis=1, keepdims=True)
            own = mine[head]
            out[:, at] = (own + weight * (part[i].astype(jnp.float32) - own)).astype(out.dtype)
            leaving.append(pltpu.make_async_copy(out.at[:, at], result.at[:, at], sems.at[slot]))
            leaving[-1].start()
    for copy in leaving:
        copy.wait()


def exchange(room, late, planes, queries, keys, values, mate_k, sends, takes, where):
    rows, features = queries.shape
    heads = features // HEAD_DIM
    early = heads - late
    f32, bf16, i32 = jnp.float32, jnp.bfloat16, jnp.int32
    shape = jax.ShapeDtypeStruct
    tile = (rows, HEAD_DIM)
    count = planes * OWN
    across = [(d, d ^ 2) for d in range(count)]
    beside = [(d, d ^ 1) for d in range(count)]
    barrier = lax.optimization_barrier

    mate_v = lax.ppermute(values, "seq", beside)
    far_q = lax.ppermute(queries, "seq", across)
    packed = pl.pallas_call(
        functools.partial(pack_kernel, heads, planes, room),
        out_shape=[shape((room, 2) + tile, bf16)] * (planes - 1),
        in_specs=[SMEM] * 2 + [VMEM] * 4,
        out_specs=[VMEM] * (planes - 1),
        compiler_params=params(8 + room // 4),
        cost_estimate=cost(4 << 30),
        name="pack",
    )(where, sends, keys, values, mate_k, mate_v)
    landed = [
        lax.ppermute(packed[step - 1], "seq", [(d, (d + OWN * step) % count) for d in range(count)])
        for step in range(1, planes)
    ]

    where, takes, *packed = barrier((where, takes, *packed))
    most_pairs = min(4 * (planes - 1) * room, HEAD_DIM)
    pair, begin, order, far = pl.pallas_call(
        functools.partial(plan_kernel, heads, planes, room),
        out_shape=[shape((n,), i32) for n in (most_pairs, heads + 1, heads, heads)],
        in_specs=[SMEM] * 2,
        out_specs=[SMEM] * 4,
        compiler_params=params(4),
        cost_estimate=cost(4 << 30),
        name="plan",
    )(where, takes)
    here, lse_here, turned = pl.pallas_call(
        functools.partial(here_kernel, heads),
        out_shape=[shape((heads,) + tile, f32), shape(tile, f32), shape((heads, HEAD_DIM, 2 * rows), bf16)],
        in_specs=[VMEM] * 5,
        out_specs=[VMEM] * 3,
        compiler_params=params(14),
        cost_estimate=cost(1 << 30),
        name="here",
    )(queries, keys, values, mate_k, mate_v)

    def attend_far(order, lse, start, parts):
        return pl.pallas_call(
            functools.partial(far_kernel, start),
            out_shape=[shape((n,) + tile, kind) for n, kind in parts] + [shape(tile, f32)],
            in_specs=[SMEM] + [VMEM] * 5,
            out_specs=[VMEM] * (len(parts) + 1),
            compiler_params=params(12),
            cost_estimate=cost(1 << 30),
            name="far",
        )(order, lse, far_q, turned, values, mate_v)

    second = min(early, max(thirds(late)[-1] + 2, early - 8))
    parts = [n for n in (early - second, second) if n]
    lse_far, arrived = lse_here, []
    if early:
        sent, lse_far = attend_far(order, lse_far, 0, [(parts[0], bf16)])
        arrived = [lax.ppermute(sent, "seq", across)]
    kinds = [(n, bf16) for n in parts[1:]] + [(late, f32)]
    *sent, rest, lse_far = attend_far(order, lse_far, early - sum(parts[1:]), kinds)
    arrived += [lax.ppermute(x, "seq", across) for x in sent]
    *landed, rest, lse_far, first = barrier((*landed, rest, lse_far, arrived[:-1]))
    arrived = first + arrived[len(first) :]
    boxes = []
    for got in landed:
        boxes += [got, lax.ppermute(got, "seq", beside)]

    def add_extras(q, o, lse, by_head, parts):
        return pl.pallas_call(
            functools.partial(late_kernel, len(boxes), early, by_head, room),
            out_shape=[shape((n,) + tile, kind) for n, kind in parts] + [shape(tile if by_head else (heads, rows), f32)],
            in_specs=[SMEM] * 3 + [VMEM] * 3 + [HBM] * len(boxes),
            out_specs=[VMEM] * (len(parts) + 1),
            scratch_shapes=[
                pltpu.VMEM((len(boxes) * room, 2) + tile, bf16),
                pltpu.VMEM((most_pairs,) + tile, f32),
                pltpu.VMEM((most_pairs,) + tile, f32),
                pltpu.SemaphoreType.DMA((len(boxes),)),
            ],
            compiler_params=params(min(8 + 2 * room, 48)),
            cost_estimate=cost(1 << 20),
            name="late",
        )(order, pair, begin, q, o, lse, *boxes)

    *far_late, lse_far = add_extras(far_q, rest, lse_far, False, [(n, bf16) for n in thirds(late)])
    arrived = [lax.ppermute(lse_far, "seq", across), *arrived] + [lax.ppermute(x, "seq", across) for x in far_late]
    here, lse_here = add_extras(queries, here, lse_here, True, [(heads, f32)])

    return pl.pallas_call(
        merge_kernel,
        out_shape=pltpu.HBM((rows, features), bf16),
        in_specs=[SMEM] + [VMEM] * (2 + len(arrived)),
        out_specs=pl.BlockSpec(memory_space=pltpu.HBM),
        scratch_shapes=[
            pltpu.VMEM((rows, features), bf16),
            pltpu.SemaphoreType.DMA((heads,)),
        ],
        compiler_params=params(12),
        cost_estimate=cost(1 << 20),
        name="merge",
    )(far, here, lse_here, *arrived)


def per_plane(queries, keys, values, kept, counts):
    heads, planes, slots = kept.shape
    device = lax.axis_index("seq").astype(jnp.int32)
    where = jnp.stack([device >> 2, device, (device >> 1) & 1, device & 1])
    beside = [(d, d ^ 1) for d in range(planes * OWN)]
    mate_k = lax.ppermute(keys, "seq", beside)
    shape = jax.ShapeDtypeStruct
    sends, takes, choice = pl.pallas_call(
        functools.partial(lists_kernel, planes, slots),
        out_shape=[
            shape((heads + 8, HEAD_DIM), jnp.int32),
            shape((planes * OWN, HEAD_DIM), jnp.int32),
            shape((1,), jnp.int32),
        ],
        in_specs=[SMEM] + [VMEM] * 2,
        out_specs=[VMEM] * 2 + [SMEM],
        compiler_params=params(60),
        name="lists",
    )(where, kept.transpose(1, 2, 0).reshape(planes * slots, heads), counts.T)
    sizes = SIZES + ((heads, heads),)
    return lax.switch(
        choice[0],
        [functools.partial(exchange, room, late, planes) for room, late in sizes],
        queries,
        keys,
        values,
        mate_k,
        sends,
        takes,
        where,
    )


def attend_tile(query_tile, key_tiles, value_tiles, slot_list, live_count):
    row_count = query_tile.shape[0]
    factor = 1.0 / query_tile.shape[1] ** 0.5
    start_state = (
        jnp.full((row_count,), -1e30, jnp.float32),
        jnp.zeros((row_count,), jnp.float32),
        jnp.zeros((row_count, query_tile.shape[1]), jnp.float32),
    )

    def advance(block_num, state_now):
        running, totals, numerator = state_now
        first = (block_num * GROUP).astype(jnp.int32)
        chosen = lax.dynamic_slice_in_dim(slot_list, first, GROUP)
        key_block = key_tiles[chosen].reshape(GROUP * KTILE, query_tile.shape[1])
        value_block = value_tiles[chosen].reshape(GROUP * KTILE, query_tile.shape[1])
        scores = jnp.dot(query_tile, key_block.T, preferred_element_type=jnp.float32) * factor
        live_mask = jnp.repeat(first + jnp.arange(GROUP, dtype=jnp.int32) < live_count, KTILE)
        scores = jnp.where(live_mask[None, :], scores, -1e30)
        new_max = jnp.maximum(running, jnp.max(scores, axis=1))
        rescale = jnp.exp(running - new_max)
        weights = jnp.exp(scores - new_max[:, None])
        totals = totals * rescale + jnp.sum(weights, axis=1)
        numerator = numerator * rescale[:, None] + jnp.dot(
            weights.astype(jnp.bfloat16), value_block, preferred_element_type=jnp.float32
        )
        return (new_max, totals, numerator)

    block_total = (live_count + GROUP - 1) // GROUP
    running, totals, numerator = lax.fori_loop(jnp.int32(0), block_total, advance, start_state)
    return (numerator / totals[:, None]).astype(jnp.bfloat16)


def per_device(queries, keys, values, kept, counts):
    local_rows, feature_count = queries.shape
    shards = lax.axis_size("seq")
    device = lax.axis_index("seq")
    head_count = feature_count // HEAD_DIM
    replicas = max(1, shards // head_count)
    slots_here = max(1, head_count // shards)
    total_rows = local_rows * shards
    tile_count = counts.shape[1]
    stacked = jnp.stack([queries, keys, values])
    copied = jnp.broadcast_to(
        stacked.reshape(3, local_rows, head_count, 1, HEAD_DIM),
        (3, local_rows, head_count, replicas, HEAD_DIM),
    )
    copied = copied.reshape(3, local_rows, head_count * replicas, HEAD_DIM)
    arrived = lax.all_to_all(copied, "seq", split_axis=2, concat_axis=1, tiled=True)
    head_data = arrived.transpose(2, 0, 1, 3)
    tiles_each = tile_count // replicas
    results = []
    for j in range(slots_here):
        global_slot = device * slots_here + j
        head_id = global_slot // replicas
        replica_id = global_slot % replicas
        slot_rows = lax.dynamic_index_in_dim(kept, head_id, 0, keepdims=False)
        count_row = lax.dynamic_index_in_dim(counts, head_id, 0, keepdims=False)
        all_queries = head_data[j, 0]
        key_tiles = head_data[j, 1].reshape(total_rows // KTILE, KTILE, HEAD_DIM)
        value_tiles = head_data[j, 2].reshape(total_rows // KTILE, KTILE, HEAD_DIM)
        rounds = jnp.arange(tiles_each, dtype=jnp.int32)
        tile_ids = replica_id * tiles_each + rounds

        def process(i, output):
            tile_id = tile_ids[i]
            query_tile = lax.dynamic_slice_in_dim(all_queries, tile_id * QTILE, QTILE, 0)
            finished = attend_tile(
                query_tile, key_tiles, value_tiles, slot_rows[tile_id], count_row[tile_id]
            )
            return lax.dynamic_update_slice_in_dim(output, finished, tile_id * QTILE, 0)

        results.append(
            lax.fori_loop(0, tiles_each, process, jnp.zeros((total_rows, HEAD_DIM), jnp.bfloat16))
        )
    gathered = jnp.stack(results, axis=1)
    returned = lax.all_to_all(gathered, "seq", split_axis=0, concat_axis=1, tiled=True)
    combined = (
        returned.reshape(local_rows, head_count, replicas, HEAD_DIM).astype(jnp.float32).sum(axis=2)
    )
    return combined.astype(jnp.bfloat16).reshape(local_rows, feature_count)


def solution(mesh):
    by_rows = P(("groups", "seq"), None)
    placed = (by_rows, by_rows, by_rows, P("groups", None, None), P("groups", None))

    def step(queries, keys, values, kept, counts):
        heads, planes, slots = kept.shape
        one_tile_each = queries.shape[0] == KTILE and mesh.shape["seq"] == planes * OWN
        fits = heads % 8 == 0 and heads <= 32 and heads * (slots - OWN) <= HEAD_DIM and planes == 4
        run = per_plane if one_tile_each and fits else per_device
        return run(queries, keys, values, kept, counts)

    return jax.shard_map(step, mesh=mesh, in_specs=placed, out_specs=by_rows, check_vma=False)
```
